128 devices in a mesh: az: 32 (over x, y_hi, z), rad: 4 (over y_lo, core).
Axes of the slice: x: 4, y: 4 (y_hi: 2, y_lo: 2; y = y_hi * 2 + y_lo), z: 4, core: 2. Of those that a mesh axis runs over, the one named last changes fastest.
Arguments:
- state: float32 [8, 128, 32768], P(None, 'rad', 'az'), as said below
- row_shift: int32 [128], replicated, may hold values from 0 to 1023
- row_frac: float32 [128], replicated, may hold values from 0 to 1
- edge_shift: int32 [1], replicated, may hold values from 0 to 1023
- edge_frac: float32 [1], replicated, may hold values from 0 to 1
Outputs:
- new_state: float32 [8, 128, 32768], P(None, 'rad', 'az')
The draws below stay inside these ranges and needn't reach their ends.
Inputs may be any that keep to these rules, and one draw needn't show every extreme that they name: `state`: field 0 (density) lies between 0.5 and 2 and field 7 (tracer) is positive.
All inputs are finite; a program needn't handle non-finite values.
Results may differ from the reference program's by a relative error of at most 0.00002.
Values sent between devices are 32-bit elements; how exact they have to be, the bound alone decides.
A program may use at most 128 MiB of HBM per device.

```python
import jax
import jax.numpy as jnp

NZ = 32
NR = 128
NA = 1024


def draw_state(key, part):
    key = jax.random.fold_in(key, 7)
    keys = jax.random.split(key, 4)
    shape = (NR, NA * NZ)
    density = jnp.exp(jax.random.uniform(keys[0], shape, jnp.float32, -0.6, 0.6))
    momenta = jnp.clip(0.5 * jax.random.normal(keys[1], (3,) + shape, jnp.float32), -2.0, 2.0)
    magnetic = jnp.clip(0.5 * jax.random.normal(keys[2], (3,) + shape, jnp.float32), -2.0, 2.0)
    tracer = density * jax.random.uniform(keys[3], shape, jnp.float32, 0.2, 1.0)
    return jnp.concatenate([density[None], momenta, magnetic, tracer[None]], axis=0)


def plant(values, rng, least, top_value):
    place = [jax.random.randint(jax.random.fold_in(rng, axis), (), 0, length) for axis, length in enumerate(values.shape)]
    main_axis = values.shape.index(max(values.shape))
    neighbour = place[:main_axis] + [(place[main_axis] + 1) % values.shape[main_axis]] + place[main_axis + 1:]
    return values.at[tuple(place)].set(least).at[tuple(neighbour)].set(top_value)


def setup_inputs(seed: int = 0) -> dict:
    key_of = jax.random.split(jax.random.key(seed), 6)
    state = draw_state(jax.random.fold_in(key_of[5], 71), 0)
    row_shift = plant(jax.random.randint(key_of[1], (NR,), 0, NA), jax.random.fold_in(key_of[1], 1), 0, NA - 1).astype(jnp.int32)
    row_frac = jnp.clip(jax.random.uniform(key_of[2], (NR,), jnp.float32, 0.0, 1.0), 0.0, 1.0)
    edge_shift = jax.random.randint(key_of[3], (1,), 0, NA).astype(jnp.int32)
    edge_frac = jnp.clip(jax.random.uniform(key_of[4], (1,), jnp.float32, 0.0, 1.0), 0.0, 1.0)
    return dict(state=state, row_shift=row_shift, row_frac=row_frac, edge_shift=edge_shift, edge_frac=edge_frac)


time_step = 0.2
sound_sq = 1.0
rotation = 1.0
shear_rate = 1.5

def plus_x(field):
    return jnp.roll(field, -1, axis=0)

def minus_x(field):
    return jnp.roll(field, 1, axis=0)

def plus_y(field):
    return jnp.roll(field, -NZ, axis=1)

def minus_y(field):
    return jnp.roll(field, NZ, axis=1)

def plus_z(field):
    level = jnp.arange(field.shape[1]) % NZ
    return jnp.where(level[None, :] == NZ - 1, jnp.roll(field, NZ - 1, axis=1), jnp.roll(field, -1, axis=1))

def minus_z(field):
    level = jnp.arange(field.shape[1]) % NZ
    return jnp.where(level[None, :] == 0, jnp.roll(field, 1 - NZ, axis=1), jnp.roll(field, 1, axis=1))

def side_flux(cells, normal, face_field):
    density, momenta, magnetic, tracer = cells
    velocity = [m / density for m in momenta]
    field_b = list(magnetic)
    field_b[normal] = face_field
    b_square = field_b[0] * field_b[0] + field_b[1] * field_b[1] + field_b[2] * field_b[2]
    pressure = sound_sq * density + 0.5 * b_square
    normal_speed = velocity[normal]
    fluxes = [density * normal_speed]
    for axis_index in range(3):
        flux_term = momenta[axis_index] * normal_speed - face_field * field_b[axis_index]
        if axis_index == normal:
            flux_term = flux_term + pressure
        fluxes.append(flux_term)
    fluxes.append(tracer * normal_speed)
    conserved = [density] + list(momenta) + [tracer]
    signal = jnp.abs(normal_speed) + jnp.sqrt(sound_sq + b_square / density)
    return (fluxes, conserved, signal)

def face_flux(cells, step_back, normal, face_field):
    density, momenta, magnetic, tracer = cells
    behind = (step_back(density), tuple((step_back(m) for m in momenta)), tuple((step_back(b) for b in magnetic)), step_back(tracer))
    left_flux, left_cons, left_signal = side_flux(behind, normal, face_field)
    right_flux, right_cons, right_signal = side_flux(cells, normal, face_field)
    bound = jnp.maximum(left_signal, right_signal)
    result = []
    for position in range(5):
        result.append(0.5 * (left_flux[position] + right_flux[position]) - 0.5 * bound * (right_cons[position] - left_cons[position]))
    return result

def advance(block):
    density = block[0]
    momenta = (block[1], block[2], block[3])
    faces = (block[4], block[5], block[6])
    tracer = block[7]
    centred = (0.5 * (faces[0] + plus_x(faces[0])), 0.5 * (faces[1] + plus_y(faces[1])), 0.5 * (faces[2] + plus_z(faces[2])))
    cells = (density, momenta, centred, tracer)
    flux_x = face_flux(cells, minus_x, 0, faces[0])
    flux_y = face_flux(cells, minus_y, 1, faces[1])
    flux_z = face_flux(cells, minus_z, 2, faces[2])
    conserved = [density] + list(momenta) + [tracer]
    updated = []
    for position in range(5):
        change = plus_x(flux_x[position]) - flux_x[position]
        change = change + plus_y(flux_y[position]) - flux_y[position]
        change = change + plus_z(flux_z[position]) - flux_z[position]
        updated.append(conserved[position] - time_step * change)
    updated[1] = updated[1] + time_step * 2.0 * rotation * momenta[1]
    updated[2] = updated[2] - time_step * (2.0 - shear_rate) * rotation * momenta[0]
    velocity = [m / density for m in momenta]
    emf_x = -(velocity[1] * centred[2] - velocity[2] * centred[1])
    emf_y = -(velocity[2] * centred[0] - velocity[0] * centred[2])
    emf_z = -(velocity[0] * centred[1] - velocity[1] * centred[0])
    edge_x = 0.25 * (emf_x + minus_y(emf_x) + minus_z(emf_x) + minus_y(minus_z(emf_x)))
    edge_y = 0.25 * (emf_y + minus_x(emf_y) + minus_z(emf_y) + minus_x(minus_z(emf_y)))
    edge_z = 0.25 * (emf_z + minus_x(emf_z) + minus_y(emf_z) + minus_x(minus_y(emf_z)))
    next_face_x = faces[0] - time_step * (plus_y(edge_z) - edge_z - (plus_z(edge_y) - edge_y))
    next_face_y = faces[1] - time_step * (plus_z(edge_x) - edge_x - (plus_x(edge_z) - edge_z))
    next_face_z = faces[2] - time_step * (plus_x(edge_y) - edge_y - (plus_y(edge_x) - edge_x))
    return jnp.stack([updated[0], updated[1], updated[2], updated[3], next_face_x, next_face_y, next_face_z, updated[4]])

def roll_row(row_data, amount):
    return jnp.roll(row_data, amount * NZ, axis=-1)

def shift_rows(fields, shifts, fractions):
    first = jax.vmap(roll_row, in_axes=(1, 0), out_axes=1)(fields, shifts)
    second = jax.vmap(roll_row, in_axes=(1, 0), out_axes=1)(fields, shifts + 1)
    weight = fractions[None, :, None]
    return (1.0 - weight) * first + weight * second

def reference(state, row_shift, row_frac, edge_shift, edge_frac):
    moved = shift_rows(state, row_shift, row_frac)
    inner_shift = jnp.broadcast_to(edge_shift, (2,)).astype(jnp.int32)
    inner_frac = jnp.broadcast_to(edge_frac, (2,))
    outer_shift = jnp.broadcast_to(NA - 1 - edge_shift, (2,)).astype(jnp.int32)
    outer_frac = jnp.broadcast_to(1.0 - edge_frac, (2,))
    lower = shift_rows(moved[:, NR - 2:], inner_shift, inner_frac)
    upper = shift_rows(moved[:, :2], outer_shift, outer_frac)
    extended = jnp.concatenate([lower, moved, upper], axis=1)
    return advance(extended)[:, 2:-2]
```

```python
import jax
import jax.numpy as jnp
from jax import lax
from jax.experimental import pallas as pl
from jax.experimental.pallas import tpu as pltpu
from jax.sharding import PartitionSpec as P

MESH = pl.DeviceIdType.MESH
NZ = 32
FIELDS = 8
ROWS = 32
COLUMNS = 1024
RING = 32
TILE = 128
TILES = RING * COLUMNS // TILE
SLOTS = ROWS + 3
FLIGHT = 16
TIME_STEP = 0.2


def place():
    az, rad = lax.axis_index("az"), lax.axis_index("rad")
    return az // 8, (az // 4) % 2, az % 4, rad // 2, rad % 2


def holder_of(group, row):
    i = row % 16
    low = (group % 2 + i // 4 + (i // 2) % 2) % 2
    return {"az": 2 * i + low, "rad": (1 - group // 2) * 2 + row // 16}


def exchange_kernel(
    state_ref, shift_ref, frac_ref, edge_shift_ref, edge_frac_ref,
    cells_ref,
    rows_ref, held_ref, moved_ref, ghost_ref,
    out_sem, back_sem, ghost_sem, held_sem, row_sem, halo_sem, face_sem,
):
    x, y_hi, z, y_lo, core = place()
    az, rad = lax.axis_index("az"), lax.axis_index("rad")
    parity = (x + y_hi + z) % 2
    group = (1 - y_lo) * 2 + parity
    row = core * 16 + az // 2
    is_last = row == ROWS - 1
    is_low = row < 2
    is_ghost = jnp.logical_or(is_last, is_low)
    at_edge = jnp.logical_or(
        jnp.logical_and(is_last, group == 3), jnp.logical_and(is_low, group == 0)
    )

    barrier = pltpu.get_barrier_semaphore()

    def greet(d, carry):
        pl.semaphore_signal(barrier, inc=1, device_id={"az": d, "rad": group}, device_id_type=MESH)
        return carry

    lax.fori_loop(0, RING, greet, 0)
    for ghost_group, ghost_row in (((rad + 3) % 4, ROWS - 1), ((rad + 1) % 4, 0), ((rad + 1) % 4, 1)):
        pl.semaphore_signal(
            barrier, inc=1, device_id=holder_of(ghost_group, ghost_row), device_id_type=MESH
        )

    def gather(r, carry):
        for t in range(8):
            first_field = (r // 8) * 64 + t * 8 + r % 8
            rows_ref[r, t] = state_ref[pl.ds(first_field, FIELDS, stride=ROWS * 8), :]
        return carry

    lax.fori_loop(0, ROWS, gather, 0)
    pl.semaphore_wait(barrier, jnp.where(is_ghost, 2 * RING, RING))

    offset_parity = (core + parity) % 2

    def send_out(k, carry):
        half, i = k // 16, k % 16
        dx, dz = i % 4, (i // 4 + i) % 4
        dy = (offset_parity + dx + dz) % 2
        target = ((x + dx) % 4) * 8 + ((y_hi + dy) % 2) * 4 + (z + dz) % 4
        copy = pltpu.make_async_remote_copy(
            src_ref=rows_ref.at[half * 16 + target // 2],
            dst_ref=held_ref.at[pl.ds(az * 8, 8)],
            send_sem=out_sem.at[k % FLIGHT],
            recv_sem=held_sem,
            device_id={"az": target, "rad": (1 - y_lo) * 2 + half},
            device_id_type=MESH,
        )

        @pl.when(k >= FLIGHT)
        def _():
            copy.wait_send()

        copy.start()
        return carry

    lax.fori_loop(0, RING, send_out, 0)
    pltpu.make_async_remote_copy(
        src_ref=held_ref, dst_ref=held_ref, send_sem=out_sem.at[0], recv_sem=held_sem,
        device_id={"az": az, "rad": (rad + 2) % 4}, device_id_type=MESH,
    ).wait_recv()

    lane = lax.broadcasted_iota(jnp.int32, (FIELDS, TILE), 1)

    def held_tile(t):
        return held_ref[t]

    def moved_tile(t):
        return moved_ref[t // 8, t % 8]

    def remap(load, shift, fraction):
        def shifted(t, cells):
            whole, part = cells // 4, (cells % 4) * NZ
            here = (t + 2 * TILES - whole) % TILES
            both = jnp.where(lane < TILE - part, load(here), load((here + TILES - 1) % TILES))
            return pltpu.roll(both, part, 1)

        def tile(t):
            return (1.0 - fraction) * shifted(t, shift) + fraction * shifted(t, shift + 1)

        return tile

    def fill(target_ref, tile, d):
        for j in range(8):
            target_ref[d, j] = tile(8 * d + j)
        after, before = tile((8 * d + 8) % TILES), tile((8 * d + TILES - 1) % TILES)
        target_ref[d, 8] = jnp.where(lane < TILE - NZ, after, before)

    first = remap(held_tile, shift_ref[group * ROWS + row], frac_ref[group * ROWS + row])
    edge_shift, edge_frac = edge_shift_ref[0], edge_frac_ref[0]
    second = remap(
        moved_tile,
        jnp.where(is_last, edge_shift, RING * COLUMNS // NZ - 1 - edge_shift),
        jnp.where(is_last, edge_frac, 1.0 - edge_frac),
    )

    @pl.when(at_edge)
    def _():
        def prepare(d, carry):
            fill(moved_ref, first, d)
            return carry

        lax.fori_loop(0, RING, prepare, 0)

    ghost_group = jnp.where(is_last, (group + 1) % 4, (group + 3) % 4)

    def send_back(k, carry):
        dx, dz, dy = k % 4, (k // 4 + k) % 4, (k // 16 + k) % 2
        d = ((x + dx) % 4) * 8 + ((y_hi + dy) % 2) * 4 + (z + dz) % 4
        slot = k % FLIGHT

        @pl.when(jnp.logical_not(at_edge))
        def _():
            fill(moved_ref, first, d)

        copy = pltpu.make_async_remote_copy(
            src_ref=moved_ref.at[d],
            dst_ref=cells_ref.at[row + 1],
            send_sem=back_sem.at[slot],
            recv_sem=row_sem,
            device_id={"az": d, "rad": group},
            device_id_type=MESH,
        )

        @pl.when(k >= FLIGHT)
        def _():
            copy.wait_send()

        copy.start()

        def ghost_row(source_ref):
            return pltpu.make_async_remote_copy(
                src_ref=source_ref.at[d],
                dst_ref=cells_ref.at[jnp.where(is_last, 0, ROWS + 1)],
                send_sem=ghost_sem.at[slot],
                recv_sem=halo_sem.at[jnp.where(is_last, 0, 1)],
                device_id={"az": d, "rad": ghost_group},
                device_id_type=MESH,
            )

        def ghost_face(source_ref):
            return pltpu.make_async_remote_copy(
                src_ref=source_ref.at[d, :, 4:5],
                dst_ref=cells_ref.at[ROWS + 2, :, 4:5],
                send_sem=ghost_sem.at[slot],
                recv_sem=face_sem,
                device_id={"az": d, "rad": ghost_group},
                device_id_type=MESH,
            )

        @pl.when(jnp.logical_and(is_ghost, at_edge))
        def _():
            fill(ghost_ref, second, d)

        for make, wanted in ((ghost_row, jnp.logical_or(is_last, row == 0)), (ghost_face, row == 1)):
            for source_ref, here in ((ghost_ref, at_edge), (moved_ref, jnp.logical_not(at_edge))):
                @pl.when(jnp.logical_and(wanted, here))
                def _(make=make, source_ref=source_ref):
                    ghost_copy = make(source_ref)

                    @pl.when(k >= FLIGHT)
                    def _():
                        ghost_copy.wait_send()

                    ghost_copy.start()

        return carry

    lax.fori_loop(0, RING, send_back, 0)

    def drain(slot, carry):
        def left(source_ref, sem):
            pltpu.make_async_remote_copy(
                src_ref=source_ref, dst_ref=source_ref, send_sem=sem.at[slot], recv_sem=held_sem,
                device_id={"az": az, "rad": (rad + 2) % 4}, device_id_type=MESH,
            ).wait_send()

        left(rows_ref.at[0], out_sem)
        left(moved_ref.at[0], back_sem)

        @pl.when(jnp.logical_or(is_last, row == 0))
        def _():
            left(moved_ref.at[0], ghost_sem)

        @pl.when(row == 1)
        def _():
            left(moved_ref.at[0, :, 4:5], ghost_sem)

        return carry

    lax.fori_loop(0, FLIGHT, drain, 0)

    def arrived(target_ref, sem):
        pltpu.make_async_remote_copy(
            src_ref=target_ref, dst_ref=target_ref, send_sem=out_sem.at[0], recv_sem=sem,
            device_id={"az": az, "rad": (rad + 2) % 4}, device_id_type=MESH,
        ).wait_recv()

    arrived(cells_ref.at[1 : ROWS + 1], row_sem)
    arrived(cells_ref.at[0], halo_sem.at[0])
    arrived(cells_ref.at[ROWS + 1], halo_sem.at[1])
    arrived(cells_ref.at[ROWS + 2, :, 4:5], face_sem)


def exchange(state, row_shift, row_frac, edge_shift, edge_frac):
    vmem, smem = pl.BlockSpec(memory_space=pltpu.VMEM), pl.BlockSpec(memory_space=pltpu.SMEM)
    dma = pltpu.SemaphoreType.DMA
    return pl.pallas_call(
        exchange_kernel,
        out_shape=jax.ShapeDtypeStruct((SLOTS, 9, FIELDS, TILE), jnp.float32),
        in_specs=[vmem, smem, smem, smem, smem],
        out_specs=vmem,
        scratch_shapes=[
            pltpu.VMEM((ROWS, 8, FIELDS, TILE), jnp.float32),
            pltpu.VMEM((TILES, FIELDS, TILE), jnp.float32),
            pltpu.VMEM((RING, 9, FIELDS, TILE), jnp.float32),
            pltpu.VMEM((RING, 9, FIELDS, TILE), jnp.float32),
            dma((FLIGHT,)), dma((FLIGHT,)), dma((FLIGHT,)),
            dma, dma, dma((2,)), dma,
        ],
        compiler_params=pltpu.CompilerParams(
            collective_id=0, has_side_effects=True, vmem_limit_bytes=24 * 2**20
        ),
        name="exchange",
    )(state, row_shift, row_frac, edge_shift, edge_frac)


def side(cell, normal, face):
    density, momenta, magnetic, tracer, inverse = cell
    field = list(magnetic)
    field[normal] = face
    square = field[0] * field[0] + field[1] * field[1] + field[2] * field[2]
    speed = momenta[normal] * inverse
    flux = [momenta[normal]]
    for n in range(3):
        term = momenta[n] * speed - face * field[n]
        if n == normal:
            term = term + (density + 0.5 * square)
        flux.append(term)
    flux.append(tracer * speed)
    reach = 1.0 + square * inverse
    return flux, jnp.abs(speed) + reach * lax.rsqrt(reach)


def face_flux(before, cell, normal, face):
    left, left_signal = side(before, normal, face)
    right, right_signal = side(cell, normal, face)
    bound = jnp.maximum(left_signal, right_signal)
    left_state = [before[0], *before[1], before[3]]
    right_state = [cell[0], *cell[1], cell[3]]
    return [
        0.5 * ((left[n] + right[n]) - bound * (right_state[n] - left_state[n])) for n in range(5)
    ]


def step_kernel(cells_ref, out_ref, flux_ref, part_ref, emf_ref):
    lane = lax.broadcasted_iota(jnp.int32, (8, TILE), 1)
    level = lane % NZ

    def load(field, row, tile):
        return cells_ref[
            pl.ds(((row + 1) * 9 + tile) * FIELDS + field, 8, stride=9 * FIELDS), :
        ]

    def plus_z(v):
        return jnp.where(level == NZ - 1, pltpu.roll(v, NZ - 1, 1), pltpu.roll(v, TILE - 1, 1))

    def minus_z(v):
        return jnp.where(level == 0, pltpu.roll(v, TILE - NZ + 1, 1), pltpu.roll(v, 1, 1))

    def minus_y(before, v):
        return pltpu.roll(jnp.where(lane >= TILE - NZ, before, v), NZ, 1)

    def plus_y(v, after):
        return pltpu.roll(jnp.where(lane < NZ, after, v), TILE - NZ, 1)

    def read(row, tile, after):
        density = load(0, row, tile)
        momenta = [load(n, row, tile) for n in (1, 2, 3)]
        faces = [load(n, row, tile) for n in (4, 5, 6)]
        tracer = load(7, row, tile)
        centred = [
            0.5 * (faces[0] + load(4, row + 1, tile)),
            0.5 * (faces[1] + plus_y(faces[1], load(5, row, after))),
            0.5 * (faces[2] + plus_z(faces[2])),
        ]
        return (density, momenta, centred, tracer, 1.0 / density), faces

    def block(b, carry):
        row = b * 8

        def first(tile, carry):
            before, after = (tile + 8) % 9, (tile + 1) % 9
            lower, _ = read(row - 1, tile, after)
            cell, faces = read(row, tile, after)
            upper, upper_faces = read(row + 1, tile, after)
            density, momenta, centred, tracer, inverse = cell

            def shifted(field):
                return minus_y(load(field, row, before), load(field, row, tile))

            before_bz = shifted(6)
            behind_density = shifted(0)
            behind = (
                behind_density,
                [shifted(n) for n in (1, 2, 3)],
                [
                    minus_y(0.5 * (load(4, row, before) + load(4, row + 1, before)), centred[0]),
                    None,
                    0.5 * (before_bz + plus_z(before_bz)),
                ],
                shifted(7),
                1.0 / behind_density,
            )
            flux_y = face_flux(behind, cell, 1, faces[1])
            for n in range(5):
                flux_ref[tile, n] = flux_y[n]
            flux_low = face_flux(lower, cell, 0, faces[0])
            flux_high = face_flux(cell, upper, 0, upper_faces[0])
            below = (
                minus_z(density),
                [minus_z(m) for m in momenta],
                [minus_z(centred[0]), minus_z(centred[1]), None],
                minus_z(tracer),
                minus_z(inverse),
            )
            flux_z = face_flux(below, cell, 2, faces[2])
            state = [density, *momenta, tracer]
            for n in range(5):
                change = (flux_high[n] - flux_low[n]) + (plus_z(flux_z[n]) - flux_z[n])
                value = state[n] - TIME_STEP * change
                if n == 1:
                    value = value + TIME_STEP * 2.0 * momenta[1]
                if n == 2:
                    value = value - TIME_STEP * 0.5 * momenta[0]
                part_ref[tile, n] = value

            def velocity(c):
                return [m * c[4] for m in c[1]]

            def emf_y(c, v):
                return v[0] * c[2][2] - v[2] * c[2][0]

            def emf_z(c, v):
                return v[1] * c[2][0] - v[0] * c[2][1]

            v_lower, v, v_upper = velocity(lower), velocity(cell), velocity(upper)
            emf_x = v[2] * centred[1] - v[1] * centred[2]
            y_lower, y_here, y_upper = emf_y(lower, v_lower), emf_y(cell, v), emf_y(upper, v_upper)
            z_lower, z_here, z_upper = emf_z(lower, v_lower), emf_z(cell, v), emf_z(upper, v_upper)
            x_below = minus_z(emf_x)
            y_pair = y_here + y_lower
            y_across = y_upper - y_lower
            part_ref[tile, 5] = faces[0] + 0.25 * TIME_STEP * (plus_z(y_pair) - minus_z(y_pair))
            part_ref[tile, 6] = faces[1]
            part_ref[tile, 7] = faces[2] - 0.25 * TIME_STEP * (y_across + minus_z(y_across))
            emf_ref[tile, 0] = z_here + z_lower
            emf_ref[tile, 1] = (plus_z(emf_x) - x_below) - (z_upper - z_lower)
            emf_ref[tile, 2] = emf_x + x_below
            return carry

        lax.fori_loop(0, 9, first, 0)

        def last(tile, carry):
            before, after = (tile + 8) % 9, tile + 1
            rows, columns = pl.ds(row, 8), pl.ds(pl.multiple_of(tile * TILE, TILE), TILE)
            for n, field in enumerate((0, 1, 2, 3, 7)):
                flux = flux_ref[tile, n]
                out_ref[field, rows, columns] = part_ref[tile, n] - TIME_STEP * (
                    plus_y(flux, flux_ref[after, n]) - flux
                )
            around = [
                (emf_ref[before, n], emf_ref[tile, n], emf_ref[after, n]) for n in range(3)
            ]
            across_z = plus_y(around[0][1], around[0][2]) - minus_y(around[0][0], around[0][1])
            pair = around[1][1] + minus_y(around[1][0], around[1][1])
            across_x = plus_y(around[2][1], around[2][2]) - minus_y(around[2][0], around[2][1])
            out_ref[4, rows, columns] = part_ref[tile, 5] - 0.25 * TIME_STEP * across_z
            out_ref[5, rows, columns] = part_ref[tile, 6] - 0.25 * TIME_STEP * pair
            out_ref[6, rows, columns] = part_ref[tile, 7] + 0.25 * TIME_STEP * across_x
            return carry

        lax.fori_loop(0, 8, last, 0)
        return carry

    lax.fori_loop(0, ROWS // 8, block, 0)


def advance(cells):
    return pl.pallas_call(
        step_kernel,
        out_shape=jax.ShapeDtypeStruct((FIELDS, ROWS, COLUMNS), jnp.float32),
        in_specs=[pl.BlockSpec(memory_space=pltpu.VMEM)],
        out_specs=pl.BlockSpec(memory_space=pltpu.VMEM),
        scratch_shapes=[
            pltpu.VMEM((9, 5, 8, TILE), jnp.float32),
            pltpu.VMEM((9, 8, 8, TILE), jnp.float32),
            pltpu.VMEM((9, 3, 8, TILE), jnp.float32),
        ],
        compiler_params=pltpu.CompilerParams(vmem_limit_bytes=16 * 2**20),
        name="advance",
    )(cells.reshape(SLOTS * 9 * FIELDS, TILE))


def per_device(state, row_shift, row_frac, edge_shift, edge_frac):
    tiles = state.reshape(FIELDS, ROWS // 8, 8, COLUMNS // TILE, TILE).transpose(0, 1, 3, 2, 4)
    tiles = tiles.reshape(FIELDS * ROWS * 8, TILE)
    return advance(exchange(tiles, row_shift, row_frac, edge_shift, edge_frac))


def solution(mesh):
    return jax.shard_map(
        per_device,
        mesh=mesh,
        in_specs=(P(None, "rad", "az"), P(), P(), P(), P()),
        out_specs=P(None, "rad", "az"),
        check_vma=False,
    )
```

```python
import jax
import jax.numpy as jnp
from jax import lax
from jax.experimental import pallas as pl
from jax.experimental.pallas import tpu as pltpu
from jax.sharding import PartitionSpec as P

MESH = pl.DeviceIdType.MESH
NZ = 32
FIELDS = 8
ROWS = 32
COLUMNS = 1024
RING = 32
TILE = 128
TILES = RING * COLUMNS // TILE
SLOTS = ROWS + 3
FLIGHT = 16
PAD = 16
GHOSTS = 17
GHOST_PAD = 24
TIME_STEP = 0.2


def place():
    az, rad = lax.axis_index("az"), lax.axis_index("rad")
    return az // 8, (az // 4) % 2, az % 4, rad // 2, rad % 2


def holder_of(group, row):
    i = row % 16
    low = (group % 2 + i // 4 + (i // 2) % 2) % 2
    return {"az": 2 * i + low, "rad": (1 - group // 2) * 2 + row // 16}


def ghost_source(n):
    if n < 8:
        return ROWS - 1, n, 2 * n
    if n < 16:
        return 0, n - 8, 2 * n
    return 1, 4, 17


def exchange_kernel(
    state_hbm, shift_hbm, frac_hbm, edge_shift_hbm, edge_frac_hbm,
    cells_ref,
    state_ref, shift_ref, frac_ref, edge_shift_ref, edge_frac_ref,
    rows_ref, strips_ref, held_ref, strip_held_ref, moved_ref, moved_strip_ref, ghosts_ref,
    in_sem, out_sem, strip_sem, back_sem, ghost_sem, held_sem, strip_held_sem, row_sem, ghosts_sem,
):
    x, y_hi, z, y_lo, core = place()
    az, rad = lax.axis_index("az"), lax.axis_index("rad")
    parity = (x + y_hi + z) % 2
    group = (1 - y_lo) * 2 + parity
    row = core * 16 + az // 2
    ghost = jnp.where(row == 17, 16, row // 2)
    has_ghost = jnp.logical_or(row % 2 == 0, row == 17)
    from_below = ghost < 8
    ghost_group = jnp.where(from_below, (group + 3) % 4, (group + 1) % 4)

    loads = [
        pltpu.make_async_copy(source, target, in_sem.at[n])
        for n, (source, target) in enumerate(
            (
                (state_hbm, state_ref), (shift_hbm, shift_ref), (frac_hbm, frac_ref),
                (edge_shift_hbm, edge_shift_ref), (edge_frac_hbm, edge_frac_ref),
            )
        )
    ]
    for load in loads:
        load.start()

    barrier = pltpu.get_barrier_semaphore()

    def greet(target_group):
        def one(d, carry):
            pl.semaphore_signal(
                barrier, inc=1, device_id={"az": d, "rad": target_group}, device_id_type=MESH
            )
            return carry

        lax.fori_loop(0, RING, one, 0)

    greet(group)

    @pl.when(has_ghost)
    def _():
        greet(ghost_group)

    for load in loads:
        load.wait()
    for n in range(GHOSTS):
        r, field, _ = ghost_source(n)
        strips_ref[n] = state_ref[pl.ds(field * 256 + r // 8 * 64 + r % 8, 8, stride=8), :]
    pl.semaphore_wait(barrier, RING + GHOSTS)

    def send_strip(n):
        _, _, taker = ghost_source(n)
        return pltpu.make_async_remote_copy(
            src_ref=strips_ref.at[n],
            dst_ref=strip_held_ref.at[pl.ds(pl.multiple_of(az * 8, 8), 8)],
            send_sem=strip_sem.at[n],
            recv_sem=strip_held_sem,
            device_id=holder_of((rad + (1 if n < 8 else 3)) % 4, taker),
            device_id_type=MESH,
        )

    for n in range(GHOSTS):
        send_strip(n).start()

    offset_parity = (core + parity) % 2

    def send_out(k, carry):
        half, i = k // 16, k % 16
        dx, dz = i % 4, (i // 4 + i) % 4
        dy = (offset_parity + dx + dz) % 2
        target = ((x + dx) % 4) * 8 + ((y_hi + dy) % 2) * 4 + (z + dz) % 4
        r = half * 16 + target // 2
        for t in range(8):
            rows_ref[r, t] = state_ref[
                pl.ds((r // 8) * 64 + t * 8 + r % 8, FIELDS, stride=ROWS * 8), :
            ]
        copy = pltpu.make_async_remote_copy(
            src_ref=rows_ref.at[r],
            dst_ref=held_ref.at[pl.ds(az * 8, 8)],
            send_sem=out_sem.at[k % FLIGHT],
            recv_sem=held_sem,
            device_id={"az": target, "rad": (1 - y_lo) * 2 + half},
            device_id_type=MESH,
        )

        @pl.when(k >= FLIGHT)
        def _():
            copy.wait_send()

        copy.start()
        return carry

    lax.fori_loop(0, RING, send_out, 0)

    def arrived(target_ref, sem):
        pltpu.make_async_remote_copy(
            src_ref=target_ref, dst_ref=target_ref, send_sem=out_sem.at[0], recv_sem=sem,
            device_id={"az": az, "rad": (rad + 2) % 4}, device_id_type=MESH,
        ).wait_recv()

    arrived(held_ref.at[:TILES], held_sem)
    for t in range(PAD):
        held_ref[TILES + t] = held_ref[t]

    @pl.when(has_ghost)
    def _():
        arrived(strip_held_ref.at[:TILES], strip_held_sem)
        strip_held_ref[TILES:, :] = strip_held_ref[:GHOST_PAD, :]

    lane = lax.broadcasted_iota(jnp.int32, (FIELDS, TILE), 1)

    def taps_of(cells, weights):
        taps = []
        for n, weight in enumerate(weights):
            part = ((cells + n) % 4) * NZ
            halo = (lane + part) % TILE < TILE - NZ
            taps.append((1 - (cells % 4 + n) // 4, part, lane < TILE - part, halo, weight))
        return cells // 4, taps

    def first_tile(d, whole):
        return lax.rem(8 * d + 2 * TILES - 3 - whole, TILES)

    shift, fraction = shift_ref[group * ROWS + row], frac_ref[group * ROWS + row]
    row_whole, row_taps = taps_of(shift, (1.0 - fraction, fraction))

    def fill(d):
        base = first_tile(d, row_whole)
        total = [None] * 9
        for start, part, here, halo, weight in row_taps:
            block = held_ref[pl.ds(base + start, 11)]
            both = [jnp.where(here, block[j + 1], block[j]) for j in range(10)]
            both = both[1:9] + [jnp.where(halo, both[9], both[0])]
            for j in range(9):
                term = weight * pltpu.roll(both[j], part, 1)
                total[j] = term if total[j] is None else total[j] + term
        for j in range(9):
            moved_ref[d, j] = total[j]

    source_row = ghost_group * ROWS + jnp.where(from_below, ROWS - 1, ghost // 16)
    shift, fraction = shift_ref[source_row], frac_ref[source_row]
    edge_shift, edge_frac = edge_shift_ref[0], edge_frac_ref[0]
    at_low, at_high = group == 0, group == 3
    more = jnp.where(
        from_below,
        jnp.where(at_low, edge_shift, 0),
        jnp.where(at_high, RING * COLUMNS // NZ - 1 - edge_shift, 0),
    )
    edge = jnp.where(
        from_below, jnp.where(at_low, edge_frac, 0.0), jnp.where(at_high, 1.0 - edge_frac, 0.0)
    )
    strip_whole, strip_taps = taps_of(
        lax.rem(shift + more, RING * COLUMNS // NZ),
        (
            (1.0 - edge) * (1.0 - fraction),
            (1.0 - edge) * fraction + edge * (1.0 - fraction),
            edge * fraction,
        ),
    )

    def fill_strip(d):
        base = first_tile(d, strip_whole)
        inner = outer = None
        for start, part, here, halo, weight in strip_taps:
            at = lambda n: strip_held_ref[pl.ds(base + start + n, 8), :]
            inside = jnp.where(here, at(2), at(1))
            outside = jnp.where(halo, jnp.where(here, at(10), at(9)), jnp.where(here, at(1), at(0)))
            inside = weight * pltpu.roll(inside, part, 1)
            outside = weight * pltpu.roll(outside, part, 1)
            inner = inside if inner is None else inner + inside
            outer = outside if outer is None else outer + outside
        moved_strip_ref[d, 0:8] = inner
        moved_strip_ref[d, 8:16] = outer

    def send_back(k, carry):
        dx, dz, dy = k % 4, (k // 4 + k) % 4, (k // 16 + k) % 2
        d = ((x + dx) % 4) * 8 + ((y_hi + dy) % 2) * 4 + (z + dz) % 4
        slot = k % FLIGHT
        fill(d)
        copy = pltpu.make_async_remote_copy(
            src_ref=moved_ref.at[d],
            dst_ref=cells_ref.at[row + 1],
            send_sem=back_sem.at[slot],
            recv_sem=row_sem,
            device_id={"az": d, "rad": group},
            device_id_type=MESH,
        )

        @pl.when(k >= FLIGHT)
        def _():
            copy.wait_send()

        copy.start()

        @pl.when(has_ghost)
        def _():
            fill_strip(d)
            strip_copy = pltpu.make_async_remote_copy(
                src_ref=moved_strip_ref.at[d, :9],
                dst_ref=ghosts_ref.at[pl.ds(pl.multiple_of(ghost * 16, 16), 9)],
                send_sem=ghost_sem.at[slot],
                recv_sem=ghosts_sem,
                device_id={"az": d, "rad": group},
                device_id_type=MESH,
            )

            @pl.when(k >= FLIGHT)
            def _():
                strip_copy.wait_send()

            strip_copy.start()

        return carry

    lax.fori_loop(0, RING, send_back, 0)

    def left(source_ref, sem):
        pltpu.make_async_remote_copy(
            src_ref=source_ref, dst_ref=source_ref, send_sem=sem, recv_sem=held_sem,
            device_id={"az": az, "rad": (rad + 2) % 4}, device_id_type=MESH,
        ).wait_send()

    def drain(slot, carry):
        left(rows_ref.at[0], out_sem.at[slot])
        left(moved_ref.at[0], back_sem.at[slot])

        @pl.when(has_ghost)
        def _():
            left(moved_strip_ref.at[0, :9], ghost_sem.at[slot])

        return carry

    lax.fori_loop(0, FLIGHT, drain, 0)
    for n in range(GHOSTS):
        send_strip(n).wait_send()

    arrived(cells_ref.at[1 : ROWS + 1], row_sem)
    arrived(moved_strip_ref.at[:GHOSTS, :9], ghosts_sem)
    for t in range(9):
        cells_ref[0, t] = ghosts_ref[pl.ds(t, FIELDS, stride=16), :]
        cells_ref[ROWS + 1, t] = ghosts_ref[pl.ds(FIELDS * 16 + t, FIELDS, stride=16), :]
        cells_ref[ROWS + 2, t] = jnp.broadcast_to(ghosts_ref[pl.ds(256 + t, 1), :], (8, TILE))


def exchange(state, row_shift, row_frac, edge_shift, edge_frac):
    dma, smem = pltpu.SemaphoreType.DMA, pltpu.SMEM
    return pl.pallas_call(
        exchange_kernel,
        out_shape=jax.ShapeDtypeStruct((SLOTS, 9, FIELDS, TILE), jnp.float32),
        in_specs=[pl.BlockSpec(memory_space=pltpu.HBM)] * 5,
        out_specs=pl.BlockSpec(memory_space=pltpu.VMEM),
        scratch_shapes=[
            pltpu.VMEM(state.shape, jnp.float32),
            smem(row_shift.shape, jnp.int32), smem(row_frac.shape, jnp.float32),
            smem((1,), jnp.int32), smem((1,), jnp.float32),
            pltpu.VMEM((ROWS, 8, FIELDS, TILE), jnp.float32),
            pltpu.VMEM((GHOSTS, 8, TILE), jnp.float32),
            pltpu.VMEM((TILES + PAD, FIELDS, TILE), jnp.float32),
            pltpu.VMEM((TILES + GHOST_PAD, TILE), jnp.float32),
            pltpu.VMEM((RING, 9, FIELDS, TILE), jnp.float32),
            pltpu.VMEM((RING, 16, TILE), jnp.float32),
            pltpu.VMEM((GHOSTS * 16, TILE), jnp.float32),
            dma((5,)), dma((FLIGHT,)), dma((GHOSTS,)), dma((FLIGHT,)), dma((FLIGHT,)),
            dma, dma, dma, dma,
        ],
        compiler_params=pltpu.CompilerParams(
            collective_id=0, has_side_effects=True, vmem_limit_bytes=24 * 2**20
        ),
        name="exchange",
    )(state, row_shift, row_frac, edge_shift, edge_frac)


def side(cell, normal, face):
    density, momenta, magnetic, tracer, inverse = cell
    field = list(magnetic)
    field[normal] = face
    square = field[0] * field[0] + field[1] * field[1] + field[2] * field[2]
    speed = momenta[normal] * inverse
    flux = [momenta[normal]]
    for n in range(3):
        term = momenta[n] * speed - face * field[n]
        if n == normal:
            term = term + (density + 0.5 * square)
        flux.append(term)
    flux.append(tracer * speed)
    reach = 1.0 + square * inverse
    return flux, jnp.abs(speed) + reach * lax.rsqrt(reach)


def face_flux(before, cell, normal, face):
    left, left_signal = side(before, normal, face)
    right, right_signal = side(cell, normal, face)
    bound = jnp.maximum(left_signal, right_signal)
    left_state = [before[0], *before[1], before[3]]
    right_state = [cell[0], *cell[1], cell[3]]
    return [
        0.5 * ((left[n] + right[n]) - bound * (right_state[n] - left_state[n])) for n in range(5)
    ]


def step_kernel(cells_ref, out_ref, flux_ref, part_ref, emf_ref):
    lane = lax.broadcasted_iota(jnp.int32, (8, TILE), 1)
    level = lane % NZ
    up = jnp.where(level == NZ - 1, lane - (NZ - 1), lane + 1)
    down = jnp.where(level == 0, lane + (NZ - 1), lane - 1)

    def load(field, row, tile):
        return cells_ref[
            pl.ds(((row + 1) * 9 + tile) * FIELDS + field, 8, stride=9 * FIELDS), :
        ]

    def plus_z(v):
        return jnp.take_along_axis(v, up, axis=1, mode="promise_in_bounds")

    def minus_z(v):
        return jnp.take_along_axis(v, down, axis=1, mode="promise_in_bounds")

    def minus_y(before, v):
        return pltpu.roll(jnp.where(lane >= TILE - NZ, before, v), NZ, 1)

    def plus_y(v, after):
        return pltpu.roll(jnp.where(lane < NZ, after, v), TILE - NZ, 1)

    def read(row, tile, after):
        density = load(0, row, tile)
        momenta = [load(n, row, tile) for n in (1, 2, 3)]
        faces = [load(n, row, tile) for n in (4, 5, 6)]
        tracer = load(7, row, tile)
        centred = [
            0.5 * (faces[0] + load(4, row + 1, tile)),
            0.5 * (faces[1] + plus_y(faces[1], load(5, row, after))),
            0.5 * (faces[2] + plus_z(faces[2])),
        ]
        return (density, momenta, centred, tracer, 1.0 / density), faces

    def block(b, carry):
        row = b * 8

        def first(tile, carry):
            before, after = (tile + 8) % 9, (tile + 1) % 9
            lower, _ = read(row - 1, tile, after)
            cell, faces = read(row, tile, after)
            upper, upper_faces = read(row + 1, tile, after)
            density, momenta, centred, tracer, inverse = cell

            def shifted(field):
                return minus_y(load(field, row, before), load(field, row, tile))

            before_bz = shifted(6)
            behind_density = shifted(0)
            behind = (
                behind_density,
                [shifted(n) for n in (1, 2, 3)],
                [
                    minus_y(0.5 * (load(4, row, before) + load(4, row + 1, before)), centred[0]),
                    None,
                    0.5 * (before_bz + plus_z(before_bz)),
                ],
                shifted(7),
                1.0 / behind_density,
            )
            flux_y = face_flux(behind, cell, 1, faces[1])
            for n in range(5):
                flux_ref[tile, n] = flux_y[n]
            flux_low = face_flux(lower, cell, 0, faces[0])
            flux_high = face_flux(cell, upper, 0, upper_faces[0])
            below = (
                minus_z(density),
                [minus_z(m) for m in momenta],
                [minus_z(centred[0]), minus_z(centred[1]), None],
                minus_z(tracer),
                minus_z(inverse),
            )
            flux_z = face_flux(below, cell, 2, faces[2])
            state = [density, *momenta, tracer]
            for n in range(5):
                change = (flux_high[n] - flux_low[n]) + (plus_z(flux_z[n]) - flux_z[n])
                value = state[n] - TIME_STEP * change
                if n == 1:
                    value = value + TIME_STEP * 2.0 * momenta[1]
                if n == 2:
                    value = value - TIME_STEP * 0.5 * momenta[0]
                part_ref[tile, n] = value

            def velocity(c):
                return [m * c[4] for m in c[1]]

            def emf_y(c, v):
                return v[0] * c[2][2] - v[2] * c[2][0]

            def emf_z(c, v):
                return v[1] * c[2][0] - v[0] * c[2][1]

            v_lower, v, v_upper = velocity(lower), velocity(cell), velocity(upper)
            emf_x = v[2] * centred[1] - v[1] * centred[2]
            y_lower, y_here, y_upper = emf_y(lower, v_lower), emf_y(cell, v), emf_y(upper, v_upper)
            z_lower, z_here, z_upper = emf_z(lower, v_lower), emf_z(cell, v), emf_z(upper, v_upper)
            x_below = minus_z(emf_x)
            y_pair = y_here + y_lower
            y_across = y_upper - y_lower
            part_ref[tile, 5] = faces[0] + 0.25 * TIME_STEP * (plus_z(y_pair) - minus_z(y_pair))
            part_ref[tile, 6] = faces[1]
            part_ref[tile, 7] = faces[2] - 0.25 * TIME_STEP * (y_across + minus_z(y_across))
            emf_ref[tile, 0] = z_here + z_lower
            emf_ref[tile, 1] = (plus_z(emf_x) - x_below) - (z_upper - z_lower)
            emf_ref[tile, 2] = emf_x + x_below
            return carry

        lax.fori_loop(0, 9, first, 0, unroll=9)

        def last(tile, carry):
            before, after = (tile + 8) % 9, tile + 1
            rows, columns = pl.ds(row, 8), pl.ds(pl.multiple_of(tile * TILE, TILE), TILE)
            for n, field in enumerate((0, 1, 2, 3, 7)):
                flux = flux_ref[tile, n]
                out_ref[field, rows, columns] = part_ref[tile, n] - TIME_STEP * (
                    plus_y(flux, flux_ref[after, n]) - flux
                )
            around = [
                (emf_ref[before, n], emf_ref[tile, n], emf_ref[after, n]) for n in range(3)
            ]
            across_z = plus_y(around[0][1], around[0][2]) - minus_y(around[0][0], around[0][1])
            pair = around[1][1] + minus_y(around[1][0], around[1][1])
            across_x = plus_y(around[2][1], around[2][2]) - minus_y(around[2][0], around[2][1])
            out_ref[4, rows, columns] = part_ref[tile, 5] - 0.25 * TIME_STEP * across_z
            out_ref[5, rows, columns] = part_ref[tile, 6] - 0.25 * TIME_STEP * pair
            out_ref[6, rows, columns] = part_ref[tile, 7] + 0.25 * TIME_STEP * across_x
            return carry

        lax.fori_loop(0, 8, last, 0, unroll=8)
        return carry

    lax.fori_loop(0, ROWS // 8, block, 0)


def advance(cells):
    return pl.pallas_call(
        step_kernel,
        out_shape=jax.ShapeDtypeStruct((FIELDS, ROWS, COLUMNS), jnp.float32),
        in_specs=[pl.BlockSpec(memory_space=pltpu.VMEM)],
        out_specs=pl.BlockSpec(memory_space=pltpu.VMEM),
        scratch_shapes=[
            pltpu.VMEM((9, 5, 8, TILE), jnp.float32),
            pltpu.VMEM((9, 8, 8, TILE), jnp.float32),
            pltpu.VMEM((9, 3, 8, TILE), jnp.float32),
        ],
        compiler_params=pltpu.CompilerParams(vmem_limit_bytes=16 * 2**20),
        name="advance",
    )(cells.reshape(SLOTS * 9 * FIELDS, TILE))


def per_device(state, row_shift, row_frac, edge_shift, edge_frac):
    tiles = state.reshape(FIELDS, ROWS // 8, 8, COLUMNS // TILE, TILE).transpose(0, 1, 3, 2, 4)
    tiles = tiles.reshape(FIELDS * ROWS * 8, TILE)
    return advance(exchange(tiles, row_shift, row_frac, edge_shift, edge_frac))


def solution(mesh):
    return jax.shard_map(
        per_device,
        mesh=mesh,
        in_specs=(P(None, "rad", "az"), P(), P(), P(), P()),
        out_specs=P(None, "rad", "az"),
        check_vma=False,
    )
```

```python
import jax
import jax.numpy as jnp
from jax import lax
from jax.experimental import pallas as pl
from jax.experimental.pallas import tpu as pltpu
from jax.sharding import PartitionSpec as P

MESH = pl.DeviceIdType.MESH
NZ = 32
FIELDS = 8
HELD = 4
ROWS = 32
HALF = 16
COLUMNS = 1024
RING = 32
TILE = 128
TILES = RING * COLUMNS // TILE
PAD = 24
WINDOW = 36
LINES = 40
SLOTS = ROWS + 3
GHOSTS = 17
VMEM_LIMIT = 60 * 2**20
TIME_STEP = 0.2


def place():
    az, rad = lax.axis_index("az"), lax.axis_index("rad")
    return az // 8, (az // 4) % 2, az % 4, rad // 2, rad % 2


def holder_of(group, index):
    i = index % 16
    low = (group % 2 + i // 4 + (i // 2) % 2) % 2
    return {"az": 2 * i + low, "rad": (1 - group // 2) * 2 + index // 16}


def ghost_source(n):
    if n < 8:
        return ROWS - 1, n, 2 * n
    if n < 16:
        return 0, n - 8, 2 * n
    return 1, 4, 17


def kernel(
    state_hbm, shift_hbm, frac_hbm, edge_shift_hbm, edge_frac_hbm,
    out_hbm,
    state_ref, shift_ref, frac_ref, edge_shift_ref, edge_frac_ref,
    rows_ref, strips_ref, held_low_ref, held_high_ref, strip_held_ref, moved_ref, moved_strip_ref, cells_ref, ghosts_ref,
    out_ref, flux_ref, part_ref, emf_ref,
    in_sem, rows_sem, strips_sem, back_sem, ghosts_back_sem, held_sem, strip_held_sem, row_sem, ghosts_sem, done_sem,
):
    x, y_hi, z, y_lo, core = place()
    az, rad = lax.axis_index("az"), lax.axis_index("rad")
    parity = (x + y_hi + z) % 2
    group = (1 - y_lo) * 2 + parity
    index = core * 16 + az // 2
    ghost = jnp.where(index == 17, 16, index // 2)
    has_ghost = jnp.logical_or(index % 2 == 0, index == 17)
    from_below = ghost < 8
    ghost_group = jnp.where(from_below, (group + 3) % 4, (group + 1) % 4)

    loads = [
        pltpu.make_async_copy(source, target, in_sem.at[n])
        for n, (source, target) in enumerate(
            (
                (state_hbm, state_ref), (shift_hbm, shift_ref), (frac_hbm, frac_ref),
                (edge_shift_hbm, edge_shift_ref), (edge_frac_hbm, edge_frac_ref),
            )
        )
    ]
    for load in loads:
        load.start()

    barrier = pltpu.get_barrier_semaphore()

    def greet(target_group):
        def one(d, carry):
            pl.semaphore_signal(
                barrier, inc=1, device_id={"az": d, "rad": target_group}, device_id_type=MESH
            )
            return carry

        lax.fori_loop(0, RING, one, 0)

    greet(group)

    @pl.when(has_ghost)
    def _():
        greet(ghost_group)

    for load in loads:
        load.wait()

    def field_lines(field, r):
        return state_ref[pl.ds(field * 256 + r // 8 * 64 + r % 8, 8, stride=8), :]

    for n in range(GHOSTS):
        r, field, _ = ghost_source(n)
        strips_ref[n] = field_lines(field, r)
    pl.semaphore_wait(barrier, RING + GHOSTS)

    for n in range(GHOSTS):
        pltpu.make_async_remote_copy(
            src_ref=strips_ref.at[n],
            dst_ref=strip_held_ref.at[pl.ds(pl.multiple_of(az * 8, 8), 8)],
            send_sem=strips_sem,
            recv_sem=strip_held_sem,
            device_id=holder_of((rad + (1 if n < 8 else 3)) % 4, ghost_source(n)[2]),
            device_id_type=MESH,
        ).start()

    offset_parity = (core + parity) % 2
    held_refs = (held_low_ref, held_high_ref)

    def send_out(half):
        def one(k, carry):
            part, i = k // 16, k % 16
            dx, dz = i % 4, (i // 4 + i) % 4
            dy = (offset_parity + dx + dz) % 2
            target = ((x + dx) % 4) * 8 + ((y_hi + dy) % 2) * 4 + (z + dz) % 4
            r = half * HALF + target // 2
            for f in range(HELD):
                rows_ref[r, part, f] = field_lines(part * HELD + f, r)
            pltpu.make_async_remote_copy(
                src_ref=rows_ref.at[r, part],
                dst_ref=held_refs[half].at[:, pl.ds(pl.multiple_of(az * 8, 8), 8)],
                send_sem=rows_sem,
                recv_sem=held_sem.at[half],
                device_id={"az": target, "rad": (1 - y_lo) * 2 + part},
                device_id_type=MESH,
            ).start()
            return carry

        lax.fori_loop(0, RING, one, 0)

    send_out(0)
    send_out(1)

    def same_size(ref, send_sem, recv_sem):
        return pltpu.make_async_remote_copy(
            src_ref=ref, dst_ref=ref, send_sem=send_sem, recv_sem=recv_sem,
            device_id={"az": az, "rad": (rad + 2) % 4}, device_id_type=MESH,
        )

    lane = lax.broadcasted_iota(jnp.int32, (8, TILE), 1)

    def taps_of(cells, weights):
        taps = []
        for n, weight in enumerate(weights):
            part = ((cells + n) % 4) * NZ
            halo = (lane + part) % TILE < TILE - NZ
            taps.append((1 - (cells % 4 + n) // 4, part, lane < TILE - part, halo, weight))
        return cells // 4, taps

    def blend(taps, tile_lines, halo_lines, fields):
        inner, outer = [None] * fields, None
        for start, part, here, halo, weight in taps:
            for f in range(fields):
                both = jnp.where(here, tile_lines(f, start + 2), tile_lines(f, start + 1))
                term = weight * pltpu.roll(both, part, 1)
                inner[f] = term if inner[f] is None else inner[f] + term
            after = jnp.where(here, halo_lines(start + 10), halo_lines(start + 9))
            before = jnp.where(here, halo_lines(start + 1), halo_lines(start))
            term = weight * pltpu.roll(jnp.where(halo, after, before), part, 1)
            outer = term if outer is None else outer + term
        return inner, outer

    def send_back(half):
        held_ref = held_refs[half]
        same_size(held_ref.at[:, :TILES], rows_sem, held_sem.at[half]).wait_recv()
        for f in range(HELD):
            held_ref[f, TILES:] = held_ref[f, :PAD]
        r = half * HALF + az // 2
        shift, fraction = shift_ref[group * ROWS + r], frac_ref[group * ROWS + r]
        whole, taps = taps_of(shift, (1.0 - fraction, fraction))

        def fill(d):
            base = lax.rem(8 * d + 2 * TILES - 3 - whole, TILES)
            inner, outer = blend(
                taps,
                lambda f, n: held_ref[f, pl.ds(base + n, 8), :],
                lambda n: jnp.concatenate(
                    [held_ref[f, pl.ds(base + n, 1), :] for f in range(HELD)] * 2, axis=0
                ),
                HELD,
            )
            for f in range(HELD):
                moved_ref[half, d, f * 8 : f * 8 + 8] = inner[f]
            moved_ref[half, d, 32:LINES] = outer

        if half == 0:
            strip_whole, strip_taps = ghost_taps()

        def fill_strip(d):
            base = lax.rem(8 * d + 2 * TILES - 3 - strip_whole, TILES)
            lines = lambda n: strip_held_ref[pl.ds(base + n, 8), :]
            inner, outer = blend(strip_taps, lambda f, n: lines(n), lines, 1)
            moved_strip_ref[d, 0:8] = inner[0]
            moved_strip_ref[d, 8:16] = outer

        def one(k, carry):
            dx, dz, dy = k % 4, (k // 4 + k) % 4, (k // 16 + k) % 2
            d = ((x + dx) % 4) * 8 + ((y_hi + dy) % 2) * 4 + (z + dz) % 4
            fill(d)
            pltpu.make_async_remote_copy(
                src_ref=moved_ref.at[half, d, :WINDOW],
                dst_ref=cells_ref.at[pl.ds(pl.multiple_of(((r + 1) * 2 + core) * LINES, 8), WINDOW)],
                send_sem=back_sem,
                recv_sem=row_sem.at[half],
                device_id={"az": d, "rad": group},
                device_id_type=MESH,
            ).start()

            if half == 0:
                @pl.when(has_ghost)
                def _():
                    fill_strip(d)
                    pltpu.make_async_remote_copy(
                        src_ref=moved_strip_ref.at[d, :9],
                        dst_ref=ghosts_ref.at[pl.ds(pl.multiple_of(ghost * 16, 16), 9)],
                        send_sem=ghosts_back_sem,
                        recv_sem=ghosts_sem,
                        device_id={"az": d, "rad": group},
                        device_id_type=MESH,
                    ).start()

            return carry

        lax.fori_loop(0, RING, one, 0)

    def ghost_taps():
        @pl.when(has_ghost)
        def _():
            same_size(strip_held_ref.at[:TILES], strips_sem, strip_held_sem).wait_recv()
            strip_held_ref[TILES:, :] = strip_held_ref[:PAD, :]

        source_row = ghost_group * ROWS + jnp.where(from_below, ROWS - 1, ghost // 16)
        shift, fraction = shift_ref[source_row], frac_ref[source_row]
        edge_shift, edge_frac = edge_shift_ref[0], edge_frac_ref[0]
        at_low, at_high = group == 0, group == 3
        more = jnp.where(
            from_below,
            jnp.where(at_low, edge_shift, 0),
            jnp.where(at_high, RING * COLUMNS // NZ - 1 - edge_shift, 0),
        )
        edge = jnp.where(
            from_below, jnp.where(at_low, edge_frac, 0.0), jnp.where(at_high, 1.0 - edge_frac, 0.0)
        )
        return taps_of(
            lax.rem(shift + more, RING * COLUMNS // NZ),
            (
                (1.0 - edge) * (1.0 - fraction),
                (1.0 - edge) * fraction + edge * (1.0 - fraction),
                edge * fraction,
            ),
        )

    send_back(0)
    send_back(1)

    def finish(block):
        return pltpu.make_async_copy(
            out_ref.at[:, pl.ds(pl.multiple_of(block * 8, 8), 8)],
            out_hbm.at[:, pl.ds(pl.multiple_of(block * 8, 8), 8)],
            done_sem,
        )

    def arrived(half):
        same_size(cells_ref.at[: HALF * 2 * WINDOW], back_sem, row_sem.at[half]).wait_recv()

    arrived(0)
    same_size(ghosts_ref.at[: GHOSTS * 9], ghosts_back_sem, ghosts_sem).wait_recv()
    for n in range(GHOSTS):
        slot, field = ((0, n) if n < 8 else (ROWS + 1, n - 8) if n < 16 else (ROWS + 2, 4))
        first = (slot * 2 + field // HELD) * LINES
        at = first + field % HELD * 8
        cells_ref[at : at + 8] = ghosts_ref[n * 16 : n * 16 + 8]
        cells_ref[first + 32 + field % HELD : first + 33 + field % HELD] = ghosts_ref[n * 16 + 8 : n * 16 + 9]
    step_block(cells_ref, out_ref, flux_ref, part_ref, emf_ref, 0)
    finish(0).start()
    arrived(1)

    def later(block, carry):
        step_block(cells_ref, out_ref, flux_ref, part_ref, emf_ref, block)
        finish(block).start()
        return carry

    lax.fori_loop(1, ROWS // 8, later, 0)

    same_size(rows_ref, rows_sem, held_sem.at[0]).wait_send()
    same_size(strips_ref, strips_sem, held_sem.at[0]).wait_send()
    same_size(moved_ref.at[:, :, :WINDOW], back_sem, held_sem.at[0]).wait_send()

    @pl.when(has_ghost)
    def _():
        same_size(moved_strip_ref.at[:, :9], ghosts_back_sem, held_sem.at[0]).wait_send()

    pltpu.make_async_copy(out_ref, out_hbm, done_sem).wait()


def side(cell, normal, face):
    density, momenta, magnetic, tracer, inverse = cell
    field = list(magnetic)
    field[normal] = face
    square = field[0] * field[0] + field[1] * field[1] + field[2] * field[2]
    speed = momenta[normal] * inverse
    flux = [momenta[normal]]
    for n in range(3):
        term = momenta[n] * speed - face * field[n]
        if n == normal:
            term = term + (density + 0.5 * square)
        flux.append(term)
    flux.append(tracer * speed)
    reach = 1.0 + square * inverse
    return flux, jnp.abs(speed) + reach * lax.rsqrt(reach)


def face_flux(before, cell, normal, face):
    left, left_signal = side(before, normal, face)
    right, right_signal = side(cell, normal, face)
    bound = jnp.maximum(left_signal, right_signal)
    left_state = [before[0], *before[1], before[3]]
    right_state = [cell[0], *cell[1], cell[3]]
    return [
        0.5 * ((left[n] + right[n]) - bound * (right_state[n] - left_state[n])) for n in range(5)
    ]


def step_block(cells_ref, out_ref, flux_ref, part_ref, emf_ref, block):
    lane = lax.broadcasted_iota(jnp.int32, (8, TILE), 1)
    level = lane % NZ
    up = jnp.where(level == NZ - 1, lane - (NZ - 1), lane + 1)
    down = jnp.where(level == 0, lane + (NZ - 1), lane - 1)

    def load(field, row, tile):
        line = field % HELD * 8 + tile if tile < 8 else 32 + field % HELD
        first = ((row + 1) * 2 + field // HELD) * LINES + line
        return cells_ref[pl.ds(first, 8, stride=2 * LINES), :]

    def plus_z(v):
        return jnp.take_along_axis(v, up, axis=1, mode="promise_in_bounds")

    def minus_z(v):
        return jnp.take_along_axis(v, down, axis=1, mode="promise_in_bounds")

    def minus_y(before, v):
        return pltpu.roll(jnp.where(lane >= TILE - NZ, before, v), NZ, 1)

    def plus_y(v, after):
        return pltpu.roll(jnp.where(lane < NZ, after, v), TILE - NZ, 1)

    def read(row, tile, after):
        density = load(0, row, tile)
        momenta = [load(n, row, tile) for n in (1, 2, 3)]
        faces = [load(n, row, tile) for n in (4, 5, 6)]
        tracer = load(7, row, tile)
        centred = [
            0.5 * (faces[0] + load(4, row + 1, tile)),
            0.5 * (faces[1] + plus_y(faces[1], load(5, row, after))),
            0.5 * (faces[2] + plus_z(faces[2])),
        ]
        return (density, momenta, centred, tracer, 1.0 / density), faces

    row = pl.multiple_of(block * 8, 8)

    def first(tile):
        before, after = (tile + 8) % 9, (tile + 1) % 9
        lower, _ = read(row - 1, tile, after)
        cell, faces = read(row, tile, after)
        upper, upper_faces = read(row + 1, tile, after)
        density, momenta, centred, tracer, inverse = cell

        def shifted(field):
            return minus_y(load(field, row, before), load(field, row, tile))

        before_bz = shifted(6)
        behind_density = shifted(0)
        behind = (
            behind_density,
            [shifted(n) for n in (1, 2, 3)],
            [
                minus_y(0.5 * (load(4, row, before) + load(4, row + 1, before)), centred[0]),
                None,
                0.5 * (before_bz + plus_z(before_bz)),
            ],
            shifted(7),
            1.0 / behind_density,
        )
        flux_y = face_flux(behind, cell, 1, faces[1])
        for n in range(5):
            flux_ref[tile, n] = flux_y[n]
        flux_low = face_flux(lower, cell, 0, faces[0])
        flux_high = face_flux(cell, upper, 0, upper_faces[0])
        below = (
            minus_z(density),
            [minus_z(m) for m in momenta],
            [minus_z(centred[0]), minus_z(centred[1]), None],
            minus_z(tracer),
            minus_z(inverse),
        )
        flux_z = face_flux(below, cell, 2, faces[2])
        state = [density, *momenta, tracer]
        for n in range(5):
            change = (flux_high[n] - flux_low[n]) + (plus_z(flux_z[n]) - flux_z[n])
            value = state[n] - TIME_STEP * change
            if n == 1:
                value = value + TIME_STEP * 2.0 * momenta[1]
            if n == 2:
                value = value - TIME_STEP * 0.5 * momenta[0]
            part_ref[tile, n] = value

        def velocity(c):
            return [m * c[4] for m in c[1]]

        def emf_y(c, v):
            return v[0] * c[2][2] - v[2] * c[2][0]

        def emf_z(c, v):
            return v[1] * c[2][0] - v[0] * c[2][1]

        v_lower, v, v_upper = velocity(lower), velocity(cell), velocity(upper)
        emf_x = v[2] * centred[1] - v[1] * centred[2]
        y_lower, y_here, y_upper = emf_y(lower, v_lower), emf_y(cell, v), emf_y(upper, v_upper)
        z_lower, z_here, z_upper = emf_z(lower, v_lower), emf_z(cell, v), emf_z(upper, v_upper)
        x_below = minus_z(emf_x)
        y_pair = y_here + y_lower
        y_across = y_upper - y_lower
        part_ref[tile, 5] = faces[0] + 0.25 * TIME_STEP * (plus_z(y_pair) - minus_z(y_pair))
        part_ref[tile, 6] = faces[1]
        part_ref[tile, 7] = faces[2] - 0.25 * TIME_STEP * (y_across + minus_z(y_across))
        emf_ref[tile, 0] = z_here + z_lower
        emf_ref[tile, 1] = (plus_z(emf_x) - x_below) - (z_upper - z_lower)
        emf_ref[tile, 2] = emf_x + x_below

    for tile in range(9):
        first(tile)

    def last(tile):
        before, after = (tile + 8) % 9, tile + 1
        rows, columns = pl.ds(row, 8), pl.ds(tile * TILE, TILE)
        for n, field in enumerate((0, 1, 2, 3, 7)):
            flux = flux_ref[tile, n]
            out_ref[field, rows, columns] = part_ref[tile, n] - TIME_STEP * (
                plus_y(flux, flux_ref[after, n]) - flux
            )
        around = [
            (emf_ref[before, n], emf_ref[tile, n], emf_ref[after, n]) for n in range(3)
        ]
        across_z = plus_y(around[0][1], around[0][2]) - minus_y(around[0][0], around[0][1])
        pair = around[1][1] + minus_y(around[1][0], around[1][1])
        across_x = plus_y(around[2][1], around[2][2]) - minus_y(around[2][0], around[2][1])
        out_ref[4, rows, columns] = part_ref[tile, 5] - 0.25 * TIME_STEP * across_z
        out_ref[5, rows, columns] = part_ref[tile, 6] - 0.25 * TIME_STEP * pair
        out_ref[6, rows, columns] = part_ref[tile, 7] + 0.25 * TIME_STEP * across_x

    for tile in range(8):
        last(tile)


def per_device(state, row_shift, row_frac, edge_shift, edge_frac):
    tiles = state.reshape(FIELDS, ROWS // 8, 8, COLUMNS // TILE, TILE).transpose(0, 1, 3, 2, 4)
    tiles = tiles.reshape(FIELDS * ROWS * 8, TILE)
    dma, smem = pltpu.SemaphoreType.DMA, pltpu.SMEM

    def vmem(*shape):
        return pltpu.VMEM(shape, jnp.float32)

    return pl.pallas_call(
        kernel,
        out_shape=jax.ShapeDtypeStruct((FIELDS, ROWS, COLUMNS), jnp.float32),
        in_specs=[pl.BlockSpec(memory_space=pltpu.HBM)] * 5,
        out_specs=pl.BlockSpec(memory_space=pltpu.HBM),
        scratch_shapes=[
            vmem(*tiles.shape),
            smem(row_shift.shape, jnp.int32), smem(row_frac.shape, jnp.float32),
            smem((1,), jnp.int32), smem((1,), jnp.float32),
            vmem(ROWS, 2, HELD, 8, TILE),
            vmem(GHOSTS, 8, TILE),
            vmem(HELD, TILES + PAD, TILE),
            vmem(HELD, TILES + PAD, TILE),
            vmem(TILES + PAD, TILE),
            vmem(2, RING, LINES, TILE),
            vmem(RING, 16, TILE),
            vmem(SLOTS * 2 * LINES, TILE),
            vmem(GHOSTS * 16, TILE),
            vmem(FIELDS, ROWS, COLUMNS),
            vmem(9, 5, 8, TILE), vmem(9, 8, 8, TILE), vmem(9, 3, 8, TILE),
            dma((5,)), dma, dma, dma, dma, dma((2,)), dma, dma((2,)), dma, dma,
        ],
        compiler_params=pltpu.CompilerParams(
            collective_id=0, has_side_effects=True, vmem_limit_bytes=VMEM_LIMIT
        ),
        name="step",
    )(tiles, row_shift, row_frac, edge_shift, edge_frac)


def solution(mesh):
    return jax.shard_map(
        per_device,
        mesh=mesh,
        in_specs=(P(None, "rad", "az"), P(), P(), P(), P()),
        out_specs=P(None, "rad", "az"),
        check_vma=False,
    )
```

```python
import jax
import jax.numpy as jnp
from jax import lax
from jax.experimental import pallas as pl
from jax.experimental.pallas import tpu as pltpu
from jax.sharding import PartitionSpec as P

MESH = pl.DeviceIdType.MESH
NZ = 32
FIELDS = 8
HELD = 2
PIECES = 4
PARTS = 4
GROUPED = 4
ROWS = 32
COLUMNS = 1024
RING = 32
TILE = 128
TILES = RING * COLUMNS // TILE
PAD = 24
WINDOW = 18
LINES = 24
SLOTS = (6, 8)
BX_PIECE = 2
GHOSTS = 17
VMEM_LIMIT = 60 * 2**20
TIME_STEP = 0.2


def place():
    az, rad = lax.axis_index("az"), lax.axis_index("rad")
    return az // 8, (az // 4) % 2, az % 4, rad // 2, rad % 2


def row_of(part, first):
    last = first == 7
    if part == 0:
        return jnp.where(last, 3, 0), first
    return part - jnp.where(last, 1, 0), first


def ghost_holder(n):
    i = 2 if n == 16 else n % 8 // 2 * 4 + n % 2
    group = 0 if n < 8 else 3
    low = (group % 2 + i // 4 + (i // 2) % 2) % 2
    return {"az": 2 * i + low, "rad": 2 if n < 8 else 1}


def ghost_source(n):
    if n < 8:
        return ROWS - 1, n
    if n < 16:
        return 0, n - 8
    return 1, 4


def kernel(
    state_hbm, shift_hbm, frac_hbm, edge_shift_hbm, edge_frac_hbm,
    out_hbm,
    state_ref, shift_ref, frac_ref, edge_shift_ref, edge_frac_ref,
    rows_ref, strips_ref, held_0_ref, held_1_ref, held_2_ref, held_3_ref, strip_held_ref,
    moved_ref, moved_strip_ref, cells_ref, ghosts_ref,
    out_ref, flux_ref, part_ref, emf_ref,
    in_sem, rows_sem, strips_sem, back_sem, ghosts_back_sem, held_sem, strip_held_sem, row_sem, ghosts_sem,
    hand_sem, handed_sem, done_sem,
):
    x, y_hi, z, y_lo, core = place()
    az, rad = lax.axis_index("az"), lax.axis_index("rad")
    parity = (x + y_hi + z) % 2
    group = (1 - y_lo) * 2 + parity
    index = core * 16 + az // 2
    piece, first_row = index // 8, index % 8
    held_refs = (held_0_ref, held_1_ref, held_2_ref, held_3_ref)
    among = index % 16
    for_inner = jnp.logical_and(jnp.logical_and(group == 0, core == 0), among % 4 < 2)
    for_outer = jnp.logical_and(
        jnp.logical_and(group == 3, core == 1), jnp.logical_or(among % 4 < 2, among == 2)
    )
    has_ghost = jnp.logical_or(for_inner, for_outer)
    ghost = jnp.where(among == 2, 16, among // 4 * 2 + among % 4 + jnp.where(for_outer, 8, 0))

    loads = [
        pltpu.make_async_copy(source, target, in_sem.at[n])
        for n, (source, target) in enumerate(
            (
                (state_hbm, state_ref), (shift_hbm, shift_ref), (frac_hbm, frac_ref),
                (edge_shift_hbm, edge_shift_ref), (edge_frac_hbm, edge_frac_ref),
            )
        )
    ]
    for load in loads:
        load.start()

    barrier = pltpu.get_barrier_semaphore()

    def greet(target_az, target_rad):
        pl.semaphore_signal(
            barrier, inc=1, device_id={"az": target_az, "rad": target_rad}, device_id_type=MESH
        )

    for d in range(RING):
        greet(d, group)

    @pl.when(rad > 0)
    def _():
        greet(az, rad - 1)

    @pl.when(rad < 3)
    def _():
        greet(az, rad + 1)

    @pl.when(has_ghost)
    def _():
        for d in range(RING):
            greet(d, 3 - group)

    for load in loads:
        load.wait()

    def field_lines(field, row):
        eighth, rest = row if isinstance(row, tuple) else (row // 8, row % 8)
        return state_ref[pl.ds(field * 256 + eighth * 64 + rest, 8, stride=8), :]

    pl.semaphore_wait(barrier, RING + jnp.where(rad == 0, 10, jnp.where(rad == 3, 9, 2)))

    my_lines = pl.ds(pl.multiple_of(az * 8, 8), 8)

    def send_strips(ghosts):
        for n in ghosts:
            r, field = ghost_source(n)
            strips_ref[n] = field_lines(field, r)
            pltpu.make_async_remote_copy(
                src_ref=strips_ref.at[n],
                dst_ref=strip_held_ref.at[my_lines],
                send_sem=strips_sem,
                recv_sem=strip_held_sem,
                device_id=ghost_holder(n),
                device_id_type=MESH,
            ).start()

    pl.when(rad == 3)(lambda: send_strips(range(8)))
    pl.when(rad == 0)(lambda: send_strips(range(8, GHOSTS)))
    offset_parity = (core + parity) % 2

    def send_out(part):
        def some(j, carry):
            sends = []
            for m in range(GROUPED):
                k = j * GROUPED + m
                side, i = k // 16, k % 16
                dx, dz = i % 4, (i // 4 + i) % 4
                dy = (offset_parity + dx + dz) % 2
                target = ((x + dx) % 4) * 8 + ((y_hi + dy) % 2) * 4 + (z + dz) % 4
                to_piece, first = side * 2 + target // 16, target // 2 % 8
                row = row_of(part, first)
                for f in range(HELD):
                    rows_ref[to_piece, first, part, f] = field_lines(to_piece * HELD + f, row)
                sends.append(
                    pltpu.make_async_remote_copy(
                        src_ref=rows_ref.at[to_piece, first, part],
                        dst_ref=held_refs[part].at[:, my_lines],
                        send_sem=rows_sem,
                        recv_sem=held_sem.at[part],
                        device_id={"az": target, "rad": (1 - y_lo) * 2 + side},
                        device_id_type=MESH,
                    )
                )
            for send in sends:
                send.start()
            return carry

        lax.fori_loop(0, RING // GROUPED, some, 0)

    for part in range(PARTS):
        send_out(part)

    def same_size(ref, send_sem, recv_sem):
        return pltpu.make_async_remote_copy(
            src_ref=ref, dst_ref=ref, send_sem=send_sem, recv_sem=recv_sem,
            device_id={"az": az, "rad": (rad + 2) % 4}, device_id_type=MESH,
        )

    lane = lax.broadcasted_iota(jnp.int32, (8, TILE), 1)

    def taps_of(cells, weights):
        taps = []
        for n, weight in enumerate(weights):
            part = ((cells + n) % 4) * NZ
            halo = (lane + part) % TILE < TILE - NZ
            taps.append((1 - (cells % 4 + n) // 4, part, lane < TILE - part, halo, weight))
        return cells // 4, taps

    def blend(taps, tile_lines, halo_lines, fields):
        inner, outer = [None] * fields, None
        for start, part, here, halo, weight in taps:
            for f in range(fields):
                both = jnp.where(here, tile_lines(f, start + 2), tile_lines(f, start + 1))
                term = weight * pltpu.roll(both, part, 1)
                inner[f] = term if inner[f] is None else inner[f] + term
            after = jnp.where(here, halo_lines(start + 10), halo_lines(start + 9))
            before = jnp.where(here, halo_lines(start + 1), halo_lines(start))
            term = weight * pltpu.roll(jnp.where(halo, after, before), part, 1)
            outer = term if outer is None else outer + term
        return inner, outer

    odd = lax.broadcasted_iota(jnp.int32, (8, TILE), 0) % 2 == 1

    def ghost_taps():
        source_row = jnp.where(for_inner, ROWS * 4 - 1, ghost // 16)
        shift, fraction = shift_ref[source_row], frac_ref[source_row]
        edge_shift, edge_frac = edge_shift_ref[0], edge_frac_ref[0]
        more = jnp.where(for_inner, edge_shift, RING * COLUMNS // NZ - 1 - edge_shift)
        edge = jnp.where(for_inner, edge_frac, 1.0 - edge_frac)
        return taps_of(
            lax.rem(shift + more, RING * COLUMNS // NZ),
            (
                (1.0 - edge) * (1.0 - fraction),
                (1.0 - edge) * fraction + edge * (1.0 - fraction),
                edge * fraction,
            ),
        )

    def target(k):
        dx, dz, dy = k % 4, (k // 4 + k) % 4, (k // 16 + k) % 2
        return ((x + dx) % 4) * 8 + ((y_hi + dy) % 2) * 4 + (z + dz) % 4

    def first_tile(d, whole):
        return lax.rem(8 * d + 2 * TILES - 3 - whole, TILES)

    def send_back(part):
        held_ref = held_refs[part]
        same_size(held_ref.at[:, :TILES], rows_sem, held_sem.at[part]).wait_recv()
        for f in range(HELD):
            held_ref[f, TILES:] = held_ref[f, :PAD]
        eighth, rest = row_of(part, first_row)
        r = group * ROWS + eighth * 8 + rest
        shift, fraction = shift_ref[r], frac_ref[r]
        whole, taps = taps_of(shift, (1.0 - fraction, fraction))

        def fill(d):
            base = first_tile(d, whole)

            def halo_lines(n):
                pair = [
                    jnp.broadcast_to(held_ref[f, pl.ds(base + n, 1), :], (8, TILE))
                    for f in range(HELD)
                ]
                return jnp.where(odd, pair[1], pair[0])

            inner, outer = blend(
                taps, lambda f, n: held_ref[f, pl.ds(base + n, 8), :], halo_lines, HELD
            )
            for f in range(HELD):
                moved_ref[part, d, f * 8 : f * 8 + 8] = inner[f]
            moved_ref[part, d, HELD * 8 :] = outer

        def some(j, carry):
            ds = [target(j * GROUPED + m) for m in range(GROUPED)]
            for d in ds:
                fill(d)
            for d in ds:
                pltpu.make_async_remote_copy(
                    src_ref=moved_ref.at[part, d, :WINDOW],
                    dst_ref=cells_ref.at[eighth + 1, rest, piece, :WINDOW],
                    send_sem=back_sem,
                    recv_sem=row_sem.at[part],
                    device_id={"az": d, "rad": group},
                    device_id_type=MESH,
                ).start()
            return carry

        lax.fori_loop(0, RING // GROUPED, some, 0)

    def send_ghosts():
        same_size(strip_held_ref.at[:TILES], strips_sem, strip_held_sem).wait_recv()
        strip_held_ref[TILES:, :] = strip_held_ref[:PAD, :]
        whole, taps = ghost_taps()

        def fill(d):
            base = first_tile(d, whole)
            lines = lambda n: strip_held_ref[pl.ds(base + n, 8), :]
            inner, outer = blend(taps, lambda f, n: lines(n), lines, 1)
            moved_strip_ref[d, 0:8] = inner[0]
            moved_strip_ref[d, 8:16] = outer

        def some(j, carry):
            ds = [target(j * GROUPED + m) for m in range(GROUPED)]
            for d in ds:
                fill(d)
            for d in ds:
                pltpu.make_async_remote_copy(
                    src_ref=moved_strip_ref.at[d, :9],
                    dst_ref=ghosts_ref.at[pl.ds(pl.multiple_of(ghost * 16, 16), 9)],
                    send_sem=ghosts_back_sem,
                    recv_sem=ghosts_sem,
                    device_id={"az": d, "rad": group},
                    device_id_type=MESH,
                ).start()
            return carry

        lax.fori_loop(0, RING // GROUPED, some, 0)

    for part in range(PARTS):
        send_back(part)
        if part == 0:
            pl.when(has_ghost)(send_ghosts)

    def arrived(part):
        same_size(cells_ref.at[1, :, :, :WINDOW], back_sem, row_sem.at[part]).wait_recv()

    def hand(source, slot, n, neighbour):
        return pltpu.make_async_remote_copy(
            src_ref=source,
            dst_ref=slot,
            send_sem=hand_sem.at[n],
            recv_sem=handed_sem.at[n],
            device_id={"az": az, "rad": neighbour},
            device_id_type=MESH,
        )

    to_outer = [hand(cells_ref.at[4, 7, :, :WINDOW], cells_ref.at[0, 7, :, :WINDOW], 0, (rad + 1) % 4)]
    to_inner = [
        hand(cells_ref.at[1, 0, :, :WINDOW], cells_ref.at[5, 0, :, :WINDOW], 1, (rad + 3) % 4),
        hand(cells_ref.at[1, 1, BX_PIECE, :WINDOW], cells_ref.at[5, 1, BX_PIECE, :WINDOW], 2, (rad + 3) % 4),
    ]
    arrived(0)

    @pl.when(rad < 3)
    def _():
        for copy in to_outer:
            copy.start()

    @pl.when(rad > 0)
    def _():
        for copy in to_inner:
            copy.start()

    lines_ref = cells_ref.reshape(SLOTS[0] * SLOTS[1] * PIECES * LINES, TILE)

    def take_ghosts(ghosts):
        same_size(ghosts_ref.at[: len(ghosts) * 9], ghosts_back_sem, ghosts_sem).wait_recv()
        for n in ghosts:
            row, field = (-1, n) if n < 8 else (ROWS, n - 8) if n < 16 else (ROWS + 1, 4)
            first = ((row + 8) * PIECES + field // HELD) * LINES
            at, ninth = first + field % HELD * 8, first + HELD * 8 + field % HELD
            lines_ref[at : at + 8, :] = ghosts_ref[n * 16 : n * 16 + 8]
            lines_ref[ninth : ninth + 1, :] = ghosts_ref[n * 16 + 8 : n * 16 + 9]

    def received(copies):
        for copy in copies:
            copy.wait_recv()

    def finish(block):
        return pltpu.make_async_copy(
            out_ref.at[:, pl.ds(pl.multiple_of(block * 8, 8), 8)],
            out_hbm.at[:, pl.ds(pl.multiple_of(block * 8, 8), 8)],
            done_sem,
        )

    def one(block, carry):
        @pl.when(block == 0)
        def _():
            arrived(1)
            pl.when(rad > 0)(lambda: received(to_outer))
            pl.when(rad == 0)(lambda: take_ghosts(range(8)))

        pl.when(block == 1)(lambda: arrived(2))

        @pl.when(block == 2)
        def _():
            arrived(3)
            pl.when(rad < 3)(lambda: received(to_inner))
            pl.when(rad == 3)(lambda: take_ghosts(range(8, GHOSTS)))

        step_block(lines_ref, out_ref, flux_ref, part_ref, emf_ref, block)
        finish(block).start()
        return carry

    lax.fori_loop(0, ROWS // 8, one, 0)

    same_size(rows_ref, rows_sem, held_sem.at[0]).wait_send()
    same_size(moved_ref.at[:, :, :WINDOW], back_sem, held_sem.at[0]).wait_send()

    @pl.when(rad == 3)
    def _():
        same_size(strips_ref.at[:8], strips_sem, held_sem.at[0]).wait_send()

    @pl.when(rad == 0)
    def _():
        same_size(strips_ref.at[8:GHOSTS], strips_sem, held_sem.at[0]).wait_send()

    @pl.when(has_ghost)
    def _():
        same_size(moved_strip_ref.at[:, :9], ghosts_back_sem, held_sem.at[0]).wait_send()

    @pl.when(rad < 3)
    def _():
        for copy in to_outer:
            copy.wait_send()

    @pl.when(rad > 0)
    def _():
        for copy in to_inner:
            copy.wait_send()

    pltpu.make_async_copy(out_ref, out_hbm, done_sem).wait()


def side(cell, normal, face):
    density, momenta, magnetic, tracer, inverse = cell
    field = list(magnetic)
    field[normal] = face
    square = field[0] * field[0] + field[1] * field[1] + field[2] * field[2]
    speed = momenta[normal] * inverse
    flux = [momenta[normal]]
    for n in range(3):
        term = momenta[n] * speed - face * field[n]
        if n == normal:
            term = term + (density + 0.5 * square)
        flux.append(term)
    flux.append(tracer * speed)
    reach = 1.0 + square * inverse
    return flux, jnp.abs(speed) + reach * lax.rsqrt(reach)


def face_flux(before, cell, normal, face):
    left, left_signal = side(before, normal, face)
    right, right_signal = side(cell, normal, face)
    bound = jnp.maximum(left_signal, right_signal)
    left_state = [before[0], *before[1], before[3]]
    right_state = [cell[0], *cell[1], cell[3]]
    return [
        0.5 * ((left[n] + right[n]) - bound * (right_state[n] - left_state[n])) for n in range(5)
    ]


def step_block(cells_ref, out_ref, flux_ref, part_ref, emf_ref, block):
    lane = lax.broadcasted_iota(jnp.int32, (8, TILE), 1)
    level = lane % NZ
    up = jnp.where(level == NZ - 1, lane - (NZ - 1), lane + 1)
    down = jnp.where(level == 0, lane + (NZ - 1), lane - 1)

    def load(field, row, tile):
        line = field % HELD * 8 + tile if tile < 8 else HELD * 8 + field % HELD
        first = ((row + 8) * PIECES + field // HELD) * LINES + line
        return cells_ref[pl.ds(first, 8, stride=PIECES * LINES), :]

    def plus_z(v):
        return jnp.take_along_axis(v, up, axis=1, mode="promise_in_bounds")

    def minus_z(v):
        return jnp.take_along_axis(v, down, axis=1, mode="promise_in_bounds")

    def minus_y(before, v):
        return pltpu.roll(jnp.where(lane >= TILE - NZ, before, v), NZ, 1)

    def plus_y(v, after):
        return pltpu.roll(jnp.where(lane < NZ, after, v), TILE - NZ, 1)

    def read(row, tile, after):
        density = load(0, row, tile)
        momenta = [load(n, row, tile) for n in (1, 2, 3)]
        faces = [load(n, row, tile) for n in (4, 5, 6)]
        tracer = load(7, row, tile)
        centred = [
            0.5 * (faces[0] + load(4, row + 1, tile)),
            0.5 * (faces[1] + plus_y(faces[1], load(5, row, after))),
            0.5 * (faces[2] + plus_z(faces[2])),
        ]
        return (density, momenta, centred, tracer, 1.0 / density), faces

    row = pl.multiple_of(block * 8, 8)

    def first(tile):
        before, after = (tile + 8) % 9, (tile + 1) % 9
        lower, _ = read(row - 1, tile, after)
        cell, faces = read(row, tile, after)
        upper, upper_faces = read(row + 1, tile, after)
        density, momenta, centred, tracer, inverse = cell

        def shifted(field):
            return minus_y(load(field, row, before), load(field, row, tile))

        before_bz = shifted(6)
        behind_density = shifted(0)
        behind = (
            behind_density,
            [shifted(n) for n in (1, 2, 3)],
            [
                minus_y(0.5 * (load(4, row, before) + load(4, row + 1, before)), centred[0]),
                None,
                0.5 * (before_bz + plus_z(before_bz)),
            ],
            shifted(7),
            1.0 / behind_density,
        )
        flux_y = face_flux(behind, cell, 1, faces[1])
        for n in range(5):
            flux_ref[tile, n] = flux_y[n]
        flux_low = face_flux(lower, cell, 0, faces[0])
        flux_high = face_flux(cell, upper, 0, upper_faces[0])
        below = (
            minus_z(density),
            [minus_z(m) for m in momenta],
            [minus_z(centred[0]), minus_z(centred[1]), None],
            minus_z(tracer),
            minus_z(inverse),
        )
        flux_z = face_flux(below, cell, 2, faces[2])
        state = [density, *momenta, tracer]
        for n in range(5):
            change = (flux_high[n] - flux_low[n]) + (plus_z(flux_z[n]) - flux_z[n])
            value = state[n] - TIME_STEP * change
            if n == 1:
                value = value + TIME_STEP * 2.0 * momenta[1]
            if n == 2:
                value = value - TIME_STEP * 0.5 * momenta[0]
            part_ref[tile, n] = value

        def velocity(c):
            return [m * c[4] for m in c[1]]

        def emf_y(c, v):
            return v[0] * c[2][2] - v[2] * c[2][0]

        def emf_z(c, v):
            return v[1] * c[2][0] - v[0] * c[2][1]

        v_lower, v, v_upper = velocity(lower), velocity(cell), velocity(upper)
        emf_x = v[2] * centred[1] - v[1] * centred[2]
        y_lower, y_here, y_upper = emf_y(lower, v_lower), emf_y(cell, v), emf_y(upper, v_upper)
        z_lower, z_here, z_upper = emf_z(lower, v_lower), emf_z(cell, v), emf_z(upper, v_upper)
        x_below = minus_z(emf_x)
        y_pair = y_here + y_lower
        y_across = y_upper - y_lower
        part_ref[tile, 5] = faces[0] + 0.25 * TIME_STEP * (plus_z(y_pair) - minus_z(y_pair))
        part_ref[tile, 6] = faces[1]
        part_ref[tile, 7] = faces[2] - 0.25 * TIME_STEP * (y_across + minus_z(y_across))
        emf_ref[tile, 0] = z_here + z_lower
        emf_ref[tile, 1] = (plus_z(emf_x) - x_below) - (z_upper - z_lower)
        emf_ref[tile, 2] = emf_x + x_below

    for tile in range(9):
        first(tile)

    def last(tile):
        before, after = (tile + 8) % 9, tile + 1
        rows, columns = pl.ds(row, 8), pl.ds(tile * TILE, TILE)
        for n, field in enumerate((0, 1, 2, 3, 7)):
            flux = flux_ref[tile, n]
            out_ref[field, rows, columns] = part_ref[tile, n] - TIME_STEP * (
                plus_y(flux, flux_ref[after, n]) - flux
            )
        around = [
            (emf_ref[before, n], emf_ref[tile, n], emf_ref[after, n]) for n in range(3)
        ]
        across_z = plus_y(around[0][1], around[0][2]) - minus_y(around[0][0], around[0][1])
        pair = around[1][1] + minus_y(around[1][0], around[1][1])
        across_x = plus_y(around[2][1], around[2][2]) - minus_y(around[2][0], around[2][1])
        out_ref[4, rows, columns] = part_ref[tile, 5] - 0.25 * TIME_STEP * across_z
        out_ref[5, rows, columns] = part_ref[tile, 6] - 0.25 * TIME_STEP * pair
        out_ref[6, rows, columns] = part_ref[tile, 7] + 0.25 * TIME_STEP * across_x

    for tile in range(8):
        last(tile)


def per_device(state, row_shift, row_frac, edge_shift, edge_frac):
    tiles = state.reshape(FIELDS, ROWS // 8, 8, COLUMNS // TILE, TILE).transpose(0, 1, 3, 2, 4)
    tiles = tiles.reshape(FIELDS * ROWS * 8, TILE)
    dma, smem = pltpu.SemaphoreType.DMA, pltpu.SMEM

    def vmem(*shape):
        return pltpu.VMEM(shape, jnp.float32)

    return pl.pallas_call(
        kernel,
        out_shape=jax.ShapeDtypeStruct((FIELDS, ROWS, COLUMNS), jnp.float32),
        in_specs=[pl.BlockSpec(memory_space=pltpu.HBM)] * 5,
        out_specs=pl.BlockSpec(memory_space=pltpu.HBM),
        scratch_shapes=[
            vmem(*tiles.shape),
            smem(row_shift.shape, jnp.int32), smem(row_frac.shape, jnp.float32),
            smem((1,), jnp.int32), smem((1,), jnp.float32),
            vmem(PIECES, 8, PARTS, HELD, 8, TILE),
            vmem(GHOSTS, 8, TILE),
            *[vmem(HELD, TILES + PAD, TILE)] * PARTS,
            vmem(TILES + PAD, TILE),
            vmem(PARTS, RING, LINES, TILE),
            vmem(RING, 16, TILE),
            vmem(*SLOTS, PIECES, LINES, TILE),
            vmem(GHOSTS * 16, TILE),
            vmem(FIELDS, ROWS, COLUMNS),
            vmem(9, 5, 8, TILE), vmem(9, 8, 8, TILE), vmem(9, 3, 8, TILE),
            dma((5,)), dma, dma, dma, dma, dma((PARTS,)), dma, dma((PARTS,)), dma, dma((3,)), dma((3,)), dma,
        ],
        compiler_params=pltpu.CompilerParams(
            collective_id=0, has_side_effects=True, vmem_limit_bytes=VMEM_LIMIT
        ),
        name="step",
    )(tiles, row_shift, row_frac, edge_shift, edge_frac)


def solution(mesh):
    return jax.shard_map(
        per_device,
        mesh=mesh,
        in_specs=(P(None, "rad", "az"), P(), P(), P(), P()),
        out_specs=P(None, "rad", "az"),
        check_vma=False,
    )
```

```python
import jax
import jax.numpy as jnp
from jax import lax
from jax.experimental import pallas as pl
from jax.experimental.pallas import tpu as pltpu
from jax.sharding import PartitionSpec as P

MESH = pl.DeviceIdType.MESH
NZ = 32
FIELDS = 8
HELD = 2
PIECES = 4
PARTS = 4
GROUPED = 4
ROWS = 32
COLUMNS = 1024
RING = 32
TILE = 128
TILES = RING * COLUMNS // TILE
PAD = 24
WINDOW = 18
LINES = 24
SLOTS = (6, 8)
BX_PIECE = 2
GHOSTS = 17
VMEM_LIMIT = 28 * 2**20
TIME_STEP = 0.2


def place():
    az, rad = lax.axis_index("az"), lax.axis_index("rad")
    return az // 8, (az // 4) % 2, az % 4, rad // 2, rad % 2


def row_of(part, first):
    last = first == 7
    if part == 0:
        return jnp.where(last, 3, 0), first
    return part - jnp.where(last, 1, 0), first


def ghost_holder(n):
    i = 2 if n == 16 else n % 8 // 2 * 4 + n % 2
    group = 0 if n < 8 else 3
    low = (group % 2 + i // 4 + (i // 2) % 2) % 2
    return {"az": 2 * i + low, "rad": 2 if n < 8 else 1}


def ghost_source(n):
    if n < 8:
        return ROWS - 1, n
    if n < 16:
        return 0, n - 8
    return 1, 4


def kernel(
    state_hbm, shift_hbm, frac_hbm, edge_shift_ref, edge_frac_ref,
    out_ref,
    state_ref, shift_ref, frac_ref,
    rows_ref, strips_ref, held_0_ref, held_1_ref, held_2_ref, held_3_ref, strip_held_ref,
    moved_ref, moved_strip_ref, cells_ref, ghosts_ref,
    flux_ref, part_ref, emf_ref,
    in_sem, rows_sem, strips_sem, back_sem, ghosts_back_sem, held_sem, strip_held_sem, row_sem, ghosts_sem,
    hand_sem, handed_sem,
):
    x, y_hi, z, y_lo, core = place()
    az, rad = lax.axis_index("az"), lax.axis_index("rad")
    parity = (x + y_hi + z) % 2
    group = (1 - y_lo) * 2 + parity
    index = core * 16 + az // 2
    piece, first_row = index // 8, index % 8
    held_refs = (held_0_ref, held_1_ref, held_2_ref, held_3_ref)
    among = index % 16
    for_inner = jnp.logical_and(jnp.logical_and(group == 0, core == 0), among % 4 < 2)
    for_outer = jnp.logical_and(
        jnp.logical_and(group == 3, core == 1), jnp.logical_or(among % 4 < 2, among == 2)
    )
    has_ghost = jnp.logical_or(for_inner, for_outer)
    ghost = jnp.where(among == 2, 16, among // 4 * 2 + among % 4 + jnp.where(for_outer, 8, 0))

    loads = [
        pltpu.make_async_copy(source, target, in_sem.at[n])
        for n, (source, target) in enumerate(
            ((state_hbm, state_ref), (shift_hbm, shift_ref), (frac_hbm, frac_ref))
        )
    ]
    for load in loads:
        load.start()

    barrier = pltpu.get_barrier_semaphore()

    def greet(target_az, target_rad):
        pl.semaphore_signal(
            barrier, inc=1, device_id={"az": target_az, "rad": target_rad}, device_id_type=MESH
        )

    for d in range(RING):
        greet(d, group)

    @pl.when(rad > 0)
    def _():
        greet(az, rad - 1)

    @pl.when(rad < 3)
    def _():
        greet(az, rad + 1)

    @pl.when(has_ghost)
    def _():
        for d in range(RING):
            greet(d, 3 - group)

    for load in loads:
        load.wait()

    def field_lines(field, row):
        eighth, rest = row if isinstance(row, tuple) else (row // 8, row % 8)
        return state_ref[pl.ds(field * 256 + eighth * 64 + rest, 8, stride=8), :]

    pl.semaphore_wait(barrier, RING + jnp.where(rad == 0, 10, jnp.where(rad == 3, 9, 2)))

    my_lines = pl.ds(pl.multiple_of(az * 8, 8), 8)

    def send_strips(ghosts):
        for n in ghosts:
            r, field = ghost_source(n)
            strips_ref[n] = field_lines(field, r)
            pltpu.make_async_remote_copy(
                src_ref=strips_ref.at[n],
                dst_ref=strip_held_ref.at[my_lines],
                send_sem=strips_sem,
                recv_sem=strip_held_sem,
                device_id=ghost_holder(n),
                device_id_type=MESH,
            ).start()

    pl.when(rad == 3)(lambda: send_strips(range(8)))
    pl.when(rad == 0)(lambda: send_strips(range(8, GHOSTS)))
    offset_parity = (core + parity) % 2

    def send_out(part):
        def some(j, carry):
            sends = []
            for m in range(GROUPED):
                k = j * GROUPED + m
                side, i = k // 16, k % 16
                dx, dz = i % 4, (i // 4 + i) % 4
                dy = (offset_parity + dx + dz) % 2
                target = ((x + dx) % 4) * 8 + ((y_hi + dy) % 2) * 4 + (z + dz) % 4
                to_piece, first = side * 2 + target // 16, target // 2 % 8
                row = row_of(part, first)
                for f in range(HELD):
                    rows_ref[to_piece, first, part, f] = field_lines(to_piece * HELD + f, row)
                sends.append(
                    pltpu.make_async_remote_copy(
                        src_ref=rows_ref.at[to_piece, first, part],
                        dst_ref=held_refs[part].at[:, my_lines],
                        send_sem=rows_sem,
                        recv_sem=held_sem.at[part],
                        device_id={"az": target, "rad": (1 - y_lo) * 2 + side},
                        device_id_type=MESH,
                    )
                )
            for send in sends:
                send.start()
            return carry

        lax.fori_loop(0, RING // GROUPED, some, 0)

    for part in range(PARTS):
        send_out(part)

    def same_size(ref, send_sem, recv_sem):
        return pltpu.make_async_remote_copy(
            src_ref=ref, dst_ref=ref, send_sem=send_sem, recv_sem=recv_sem,
            device_id={"az": az, "rad": (rad + 2) % 4}, device_id_type=MESH,
        )

    lane = lax.broadcasted_iota(jnp.int32, (8, TILE), 1)

    def taps_of(cells, weights):
        taps = []
        for n, weight in enumerate(weights):
            part = ((cells + n) % 4) * NZ
            halo = (lane + part) % TILE < TILE - NZ
            taps.append((1 - (cells % 4 + n) // 4, part, lane < TILE - part, halo, weight))
        return cells // 4, taps

    def blend(taps, tile_lines, halo_lines, fields):
        inner, outer = [None] * fields, None
        for start, part, here, halo, weight in taps:
            for f in range(fields):
                both = jnp.where(here, tile_lines(f, start + 2), tile_lines(f, start + 1))
                term = weight * pltpu.roll(both, part, 1)
                inner[f] = term if inner[f] is None else inner[f] + term
            after = jnp.where(here, halo_lines(start + 10), halo_lines(start + 9))
            before = jnp.where(here, halo_lines(start + 1), halo_lines(start))
            term = weight * pltpu.roll(jnp.where(halo, after, before), part, 1)
            outer = term if outer is None else outer + term
        return inner, outer

    odd = lax.broadcasted_iota(jnp.int32, (8, TILE), 0) % 2 == 1

    def ghost_taps():
        source_row = jnp.where(for_inner, ROWS * 4 - 1, ghost // 16)
        shift, fraction = shift_ref[source_row], frac_ref[source_row]
        edge_shift, edge_frac = edge_shift_ref[0], edge_frac_ref[0]
        more = jnp.where(for_inner, edge_shift, RING * COLUMNS // NZ - 1 - edge_shift)
        edge = jnp.where(for_inner, edge_frac, 1.0 - edge_frac)
        return taps_of(
            lax.rem(shift + more, RING * COLUMNS // NZ),
            (
                (1.0 - edge) * (1.0 - fraction),
                (1.0 - edge) * fraction + edge * (1.0 - fraction),
                edge * fraction,
            ),
        )

    def target(k):
        dx, dz, dy = k % 4, (k // 4 + k) % 4, (k // 16 + k) % 2
        return ((x + dx) % 4) * 8 + ((y_hi + dy) % 2) * 4 + (z + dz) % 4

    def first_tile(d, whole):
        return lax.rem(8 * d + 2 * TILES - 3 - whole, TILES)

    def send_back(part):
        held_ref = held_refs[part]
        same_size(held_ref.at[:, :TILES], rows_sem, held_sem.at[part]).wait_recv()
        for f in range(HELD):
            held_ref[f, TILES:] = held_ref[f, :PAD]
        eighth, rest = row_of(part, first_row)
        r = group * ROWS + eighth * 8 + rest
        shift, fraction = shift_ref[r], frac_ref[r]
        whole, taps = taps_of(shift, (1.0 - fraction, fraction))

        def fill(d):
            base = first_tile(d, whole)

            def halo_lines(n):
                pair = [
                    jnp.broadcast_to(held_ref[f, pl.ds(base + n, 1), :], (8, TILE))
                    for f in range(HELD)
                ]
                return jnp.where(odd, pair[1], pair[0])

            inner, outer = blend(
                taps, lambda f, n: held_ref[f, pl.ds(base + n, 8), :], halo_lines, HELD
            )
            for f in range(HELD):
                moved_ref[part, d, f * 8 : f * 8 + 8] = inner[f]
            moved_ref[part, d, HELD * 8 :] = outer

        def some(j, carry):
            ds = [target(j * GROUPED + m) for m in range(GROUPED)]
            for d in ds:
                fill(d)
            for d in ds:
                pltpu.make_async_remote_copy(
                    src_ref=moved_ref.at[part, d, :WINDOW],
                    dst_ref=cells_ref.at[eighth + 1, rest, piece, :WINDOW],
                    send_sem=back_sem,
                    recv_sem=row_sem.at[part],
                    device_id={"az": d, "rad": group},
                    device_id_type=MESH,
                ).start()
            return carry

        lax.fori_loop(0, RING // GROUPED, some, 0)

    def send_ghosts():
        same_size(strip_held_ref.at[:TILES], strips_sem, strip_held_sem).wait_recv()
        strip_held_ref[TILES:, :] = strip_held_ref[:PAD, :]
        whole, taps = ghost_taps()

        def fill(d):
            base = first_tile(d, whole)
            lines = lambda n: strip_held_ref[pl.ds(base + n, 8), :]
            inner, outer = blend(taps, lambda f, n: lines(n), lines, 1)
            moved_strip_ref[d, 0:8] = inner[0]
            moved_strip_ref[d, 8:16] = outer

        def some(j, carry):
            ds = [target(j * GROUPED + m) for m in range(GROUPED)]
            for d in ds:
                fill(d)
            for d in ds:
                pltpu.make_async_remote_copy(
                    src_ref=moved_strip_ref.at[d, :9],
                    dst_ref=ghosts_ref.at[pl.ds(pl.multiple_of(ghost * 16, 16), 9)],
                    send_sem=ghosts_back_sem,
                    recv_sem=ghosts_sem,
                    device_id={"az": d, "rad": group},
                    device_id_type=MESH,
                ).start()
            return carry

        lax.fori_loop(0, RING // GROUPED, some, 0)

    for part in range(PARTS):
        send_back(part)
        if part == 0:
            pl.when(has_ghost)(send_ghosts)

    def arrived(part):
        same_size(cells_ref.at[1, :, :, :WINDOW], back_sem, row_sem.at[part]).wait_recv()

    def hand(source, slot, n, neighbour):
        return pltpu.make_async_remote_copy(
            src_ref=source,
            dst_ref=slot,
            send_sem=hand_sem.at[n],
            recv_sem=handed_sem.at[n],
            device_id={"az": az, "rad": neighbour},
            device_id_type=MESH,
        )

    to_outer = [hand(cells_ref.at[4, 7, :, :WINDOW], cells_ref.at[0, 7, :, :WINDOW], 0, (rad + 1) % 4)]
    to_inner = [
        hand(cells_ref.at[1, 0, :, :WINDOW], cells_ref.at[5, 0, :, :WINDOW], 1, (rad + 3) % 4),
        hand(cells_ref.at[1, 1, BX_PIECE, :WINDOW], cells_ref.at[5, 1, BX_PIECE, :WINDOW], 2, (rad + 3) % 4),
    ]
    arrived(0)

    @pl.when(rad < 3)
    def _():
        for copy in to_outer:
            copy.start()

    @pl.when(rad > 0)
    def _():
        for copy in to_inner:
            copy.start()

    lines_ref = cells_ref.reshape(SLOTS[0] * SLOTS[1] * PIECES * LINES, TILE)

    def take_ghosts(ghosts):
        same_size(ghosts_ref.at[: len(ghosts) * 9], ghosts_back_sem, ghosts_sem).wait_recv()
        for n in ghosts:
            row, field = (-1, n) if n < 8 else (ROWS, n - 8) if n < 16 else (ROWS + 1, 4)
            first = ((row + 8) * PIECES + field // HELD) * LINES
            at, ninth = first + field % HELD * 8, first + HELD * 8 + field % HELD
            lines_ref[at : at + 8, :] = ghosts_ref[n * 16 : n * 16 + 8]
            lines_ref[ninth : ninth + 1, :] = ghosts_ref[n * 16 + 8 : n * 16 + 9]

    def received(copies):
        for copy in copies:
            copy.wait_recv()

    def one(block, carry):
        @pl.when(block == 0)
        def _():
            arrived(1)
            pl.when(rad > 0)(lambda: received(to_outer))
            pl.when(rad == 0)(lambda: take_ghosts(range(8)))

        pl.when(block == 1)(lambda: arrived(2))

        @pl.when(block == 2)
        def _():
            arrived(3)
            pl.when(rad < 3)(lambda: received(to_inner))
            pl.when(rad == 3)(lambda: take_ghosts(range(8, GHOSTS)))

        step_block(lines_ref, out_ref, flux_ref, part_ref, emf_ref, block)
        return carry

    lax.fori_loop(0, ROWS // 8, one, 0)

    same_size(rows_ref, rows_sem, held_sem.at[0]).wait_send()
    same_size(moved_ref.at[:, :, :WINDOW], back_sem, held_sem.at[0]).wait_send()

    @pl.when(rad == 3)
    def _():
        same_size(strips_ref.at[:8], strips_sem, held_sem.at[0]).wait_send()

    @pl.when(rad == 0)
    def _():
        same_size(strips_ref.at[8:GHOSTS], strips_sem, held_sem.at[0]).wait_send()

    @pl.when(has_ghost)
    def _():
        same_size(moved_strip_ref.at[:, :9], ghosts_back_sem, held_sem.at[0]).wait_send()

    @pl.when(rad < 3)
    def _():
        for copy in to_outer:
            copy.wait_send()

    @pl.when(rad > 0)
    def _():
        for copy in to_inner:
            copy.wait_send()


def side(cell, normal, face):
    density, momenta, magnetic, tracer, inverse = cell
    field = list(magnetic)
    field[normal] = face
    square = field[0] * field[0] + field[1] * field[1] + field[2] * field[2]
    speed = momenta[normal] * inverse
    flux = [momenta[normal]]
    for n in range(3):
        term = momenta[n] * speed - face * field[n]
        if n == normal:
            term = term + (density + 0.5 * square)
        flux.append(term)
    flux.append(tracer * speed)
    reach = 1.0 + square * inverse
    return flux, jnp.abs(speed) + reach * lax.rsqrt(reach)


def face_flux(before, cell, normal, face):
    left, left_signal = side(before, normal, face)
    right, right_signal = side(cell, normal, face)
    bound = jnp.maximum(left_signal, right_signal)
    left_state = [before[0], *before[1], before[3]]
    right_state = [cell[0], *cell[1], cell[3]]
    return [
        0.5 * ((left[n] + right[n]) - bound * (right_state[n] - left_state[n])) for n in range(5)
    ]


def step_block(cells_ref, out_ref, flux_ref, part_ref, emf_ref, block):
    lane = lax.broadcasted_iota(jnp.int32, (8, TILE), 1)
    level = lane % NZ
    up = jnp.where(level == NZ - 1, lane - (NZ - 1), lane + 1)
    down = jnp.where(level == 0, lane + (NZ - 1), lane - 1)

    def load(field, row, tile):
        line = field % HELD * 8 + tile if tile < 8 else HELD * 8 + field % HELD
        first = ((row + 8) * PIECES + field // HELD) * LINES + line
        return cells_ref[pl.ds(first, 8, stride=PIECES * LINES), :]

    def plus_z(v):
        return jnp.take_along_axis(v, up, axis=1, mode="promise_in_bounds")

    def minus_z(v):
        return jnp.take_along_axis(v, down, axis=1, mode="promise_in_bounds")

    def minus_y(before, v):
        return pltpu.roll(jnp.where(lane >= TILE - NZ, before, v), NZ, 1)

    def plus_y(v, after):
        return pltpu.roll(jnp.where(lane < NZ, after, v), TILE - NZ, 1)

    def read(row, tile, after):
        density = load(0, row, tile)
        momenta = [load(n, row, tile) for n in (1, 2, 3)]
        faces = [load(n, row, tile) for n in (4, 5, 6)]
        tracer = load(7, row, tile)
        centred = [
            0.5 * (faces[0] + load(4, row + 1, tile)),
            0.5 * (faces[1] + plus_y(faces[1], load(5, row, after))),
            0.5 * (faces[2] + plus_z(faces[2])),
        ]
        return (density, momenta, centred, tracer, 1.0 / density), faces

    row = pl.multiple_of(block * 8, 8)

    def first(tile):
        before, after = (tile + 8) % 9, (tile + 1) % 9
        lower, _ = read(row - 1, tile, after)
        cell, faces = read(row, tile, after)
        upper, upper_faces = read(row + 1, tile, after)
        density, momenta, centred, tracer, inverse = cell

        def shifted(field):
            return minus_y(load(field, row, before), load(field, row, tile))

        before_bz = shifted(6)
        behind_density = shifted(0)
        behind = (
            behind_density,
            [shifted(n) for n in (1, 2, 3)],
            [
                minus_y(0.5 * (load(4, row, before) + load(4, row + 1, before)), centred[0]),
                None,
                0.5 * (before_bz + plus_z(before_bz)),
            ],
            shifted(7),
            1.0 / behind_density,
        )
        flux_y = face_flux(behind, cell, 1, faces[1])
        for n in range(5):
            flux_ref[tile, n] = flux_y[n]
        flux_low = face_flux(lower, cell, 0, faces[0])
        flux_high = face_flux(cell, upper, 0, upper_faces[0])
        below = (
            minus_z(density),
            [minus_z(m) for m in momenta],
            [minus_z(centred[0]), minus_z(centred[1]), None],
            minus_z(tracer),
            minus_z(inverse),
        )
        flux_z = face_flux(below, cell, 2, faces[2])
        state = [density, *momenta, tracer]
        for n in range(5):
            change = (flux_high[n] - flux_low[n]) + (plus_z(flux_z[n]) - flux_z[n])
            value = state[n] - TIME_STEP * change
            if n == 1:
                value = value + TIME_STEP * 2.0 * momenta[1]
            if n == 2:
                value = value - TIME_STEP * 0.5 * momenta[0]
            part_ref[tile, n] = value

        def velocity(c):
            return [m * c[4] for m in c[1]]

        def emf_y(c, v):
            return v[0] * c[2][2] - v[2] * c[2][0]

        def emf_z(c, v):
            return v[1] * c[2][0] - v[0] * c[2][1]

        v_lower, v, v_upper = velocity(lower), velocity(cell), velocity(upper)
        emf_x = v[2] * centred[1] - v[1] * centred[2]
        y_lower, y_here, y_upper = emf_y(lower, v_lower), emf_y(cell, v), emf_y(upper, v_upper)
        z_lower, z_here, z_upper = emf_z(lower, v_lower), emf_z(cell, v), emf_z(upper, v_upper)
        x_below = minus_z(emf_x)
        y_pair = y_here + y_lower
        y_across = y_upper - y_lower
        part_ref[tile, 5] = faces[0] + 0.25 * TIME_STEP * (plus_z(y_pair) - minus_z(y_pair))
        part_ref[tile, 6] = faces[1]
        part_ref[tile, 7] = faces[2] - 0.25 * TIME_STEP * (y_across + minus_z(y_across))
        emf_ref[tile, 0] = z_here + z_lower
        emf_ref[tile, 1] = (plus_z(emf_x) - x_below) - (z_upper - z_lower)
        emf_ref[tile, 2] = emf_x + x_below

    for tile in range(9):
        first(tile)

    def last(tile):
        before, after = (tile + 8) % 9, tile + 1
        rows, columns = pl.ds(row, 8), pl.ds(tile * TILE, TILE)
        for n, field in enumerate((0, 1, 2, 3, 7)):
            flux = flux_ref[tile, n]
            out_ref[field, rows, columns] = part_ref[tile, n] - TIME_STEP * (
                plus_y(flux, flux_ref[after, n]) - flux
            )
        around = [
            (emf_ref[before, n], emf_ref[tile, n], emf_ref[after, n]) for n in range(3)
        ]
        across_z = plus_y(around[0][1], around[0][2]) - minus_y(around[0][0], around[0][1])
        pair = around[1][1] + minus_y(around[1][0], around[1][1])
        across_x = plus_y(around[2][1], around[2][2]) - minus_y(around[2][0], around[2][1])
        out_ref[4, rows, columns] = part_ref[tile, 5] - 0.25 * TIME_STEP * across_z
        out_ref[5, rows, columns] = part_ref[tile, 6] - 0.25 * TIME_STEP * pair
        out_ref[6, rows, columns] = part_ref[tile, 7] + 0.25 * TIME_STEP * across_x

    for tile in range(8):
        last(tile)


def per_device(state, row_shift, row_frac, edge_shift, edge_frac):
    tiles = state.reshape(FIELDS, ROWS // 8, 8, COLUMNS // TILE, TILE).transpose(0, 1, 3, 2, 4)
    tiles = tiles.reshape(FIELDS * ROWS * 8, TILE)
    dma, smem = pltpu.SemaphoreType.DMA, pltpu.SMEM

    def vmem(*shape):
        return pltpu.VMEM(shape, jnp.float32)

    return pl.pallas_call(
        kernel,
        out_shape=jax.ShapeDtypeStruct((FIELDS, ROWS, COLUMNS), jnp.float32),
        in_specs=[pl.BlockSpec(memory_space=pltpu.HBM)] * 3 + [pl.BlockSpec(memory_space=pltpu.SMEM)] * 2,
        out_specs=pl.BlockSpec(memory_space=pltpu.VMEM),
        scratch_shapes=[
            vmem(*tiles.shape),
            smem(row_shift.shape, jnp.int32), smem(row_frac.shape, jnp.float32),
            vmem(PIECES, 8, PARTS, HELD, 8, TILE),
            vmem(GHOSTS, 8, TILE),
            *[vmem(HELD, TILES + PAD, TILE)] * PARTS,
            vmem(TILES + PAD, TILE),
            vmem(PARTS, RING, LINES, TILE),
            vmem(RING, 16, TILE),
            vmem(*SLOTS, PIECES, LINES, TILE),
            vmem(GHOSTS * 16, TILE),
            vmem(9, 5, 8, TILE), vmem(9, 8, 8, TILE), vmem(9, 3, 8, TILE),
            dma((3,)), dma, dma, dma, dma, dma((PARTS,)), dma, dma((PARTS,)), dma, dma((3,)), dma((3,)),
        ],
        compiler_params=pltpu.CompilerParams(
            collective_id=0, has_side_effects=True, vmem_limit_bytes=VMEM_LIMIT
        ),
        name="step",
    )(
        *[pltpu.with_memory_space_constraint(a, pltpu.HBM) for a in (tiles, row_shift, row_frac)],
        edge_shift,
        edge_frac,
    )


def solution(mesh):
    return jax.shard_map(
        per_device,
        mesh=mesh,
        in_specs=(P(None, "rad", "az"), P(), P(), P(), P()),
        out_specs=P(None, "rad", "az"),
        check_vma=False,
    )
```

```python
import jax
import jax.numpy as jnp
from jax import lax
from jax.experimental import pallas as pl
from jax.experimental.pallas import tpu as pltpu
from jax.sharding import PartitionSpec as P

MESH = pl.DeviceIdType.MESH
NZ = 32
FIELDS = 8
HELD = 2
PIECES = 4
PARTS = 4
GROUPED = 4
ROWS = 32
COLUMNS = 1024
RING = 32
TILE = 128
TILES = RING * COLUMNS // TILE
PAD = 24
WINDOW = 18
LINES = 24
SLOTS = (6, 8)
BX_PIECE = 2
GHOSTS = 17
VMEM_LIMIT = 28 * 2**20
TIME_STEP = 0.2


def place():
    az, rad = lax.axis_index("az"), lax.axis_index("rad")
    return az // 8, (az // 4) % 2, az % 4, rad // 2, rad % 2


def row_of(part, first):
    last = first == 7
    if part == 0:
        return jnp.where(last, 3, 0), first
    return part - jnp.where(last, 1, 0), first


def ghost_holder(n):
    i = 2 if n == 16 else n % 8 // 2 * 4 + n % 2
    group = 0 if n < 8 else 3
    low = (group % 2 + i // 4 + (i // 2) % 2) % 2
    return {"az": 2 * i + low, "rad": 2 if n < 8 else 1}


def ghost_source(n):
    if n < 8:
        return ROWS - 1, n
    if n < 16:
        return 0, n - 8
    return 1, 4


def kernel(
    state_hbm, shift_hbm, frac_hbm, edge_shift_ref, edge_frac_ref,
    out_ref,
    state_ref, shift_ref, frac_ref,
    rows_ref, strips_ref, held_0_ref, held_1_ref, held_2_ref, held_3_ref, strip_held_ref,
    moved_ref, moved_strip_ref, cells_ref, ghosts_ref,
    flux_ref, part_ref, emf_ref, cell_ref, side_ref,
    in_sem, rows_sem, strips_sem, back_sem, ghosts_back_sem, held_sem, strip_held_sem, row_sem, ghosts_sem,
    hand_sem, handed_sem,
):
    x, y_hi, z, y_lo, core = place()
    az, rad = lax.axis_index("az"), lax.axis_index("rad")
    parity = (x + y_hi + z) % 2
    group = (1 - y_lo) * 2 + parity
    index = core * 16 + az // 2
    piece, first_row = index // 8, index % 8
    held_refs = (held_0_ref, held_1_ref, held_2_ref, held_3_ref)
    among = index % 16
    for_inner = jnp.logical_and(jnp.logical_and(group == 0, core == 0), among % 4 < 2)
    for_outer = jnp.logical_and(
        jnp.logical_and(group == 3, core == 1), jnp.logical_or(among % 4 < 2, among == 2)
    )
    has_ghost = jnp.logical_or(for_inner, for_outer)
    ghost = jnp.where(among == 2, 16, among // 4 * 2 + among % 4 + jnp.where(for_outer, 8, 0))

    loads = [
        pltpu.make_async_copy(source, target, in_sem.at[n])
        for n, (source, target) in enumerate(
            ((state_hbm, state_ref), (shift_hbm, shift_ref), (frac_hbm, frac_ref))
        )
    ]
    for load in loads:
        load.start()

    barrier = pltpu.get_barrier_semaphore()

    def greet(target_az, target_rad):
        pl.semaphore_signal(
            barrier, inc=1, device_id={"az": target_az, "rad": target_rad}, device_id_type=MESH
        )

    for d in range(RING):
        greet(d, group)

    @pl.when(rad > 0)
    def _():
        greet(az, rad - 1)

    @pl.when(rad < 3)
    def _():
        greet(az, rad + 1)

    @pl.when(has_ghost)
    def _():
        for d in range(RING):
            greet(d, 3 - group)

    for load in loads:
        load.wait()

    def field_lines(field, row):
        eighth, rest = row if isinstance(row, tuple) else (row // 8, row % 8)
        return state_ref[pl.ds(field * 256 + eighth * 64 + rest, 8, stride=8), :]

    pl.semaphore_wait(barrier, RING + jnp.where(rad == 0, 10, jnp.where(rad == 3, 9, 2)))

    my_lines = pl.ds(pl.multiple_of(az * 8, 8), 8)

    def send_strips(ghosts):
        for n in ghosts:
            r, field = ghost_source(n)
            strips_ref[n] = field_lines(field, r)
            pltpu.make_async_remote_copy(
                src_ref=strips_ref.at[n],
                dst_ref=strip_held_ref.at[my_lines],
                send_sem=strips_sem,
                recv_sem=strip_held_sem,
                device_id=ghost_holder(n),
                device_id_type=MESH,
            ).start()

    pl.when(rad == 3)(lambda: send_strips(range(8)))
    pl.when(rad == 0)(lambda: send_strips(range(8, GHOSTS)))
    offset_parity = (core + parity) % 2

    def send_out(part):
        def some(j, carry):
            sends = []
            for m in range(GROUPED):
                k = j * GROUPED + m
                side, i = k // 16, k % 16
                dx, dz = i % 4, (i // 4 + i) % 4
                dy = (offset_parity + dx + dz) % 2
                target = ((x + dx) % 4) * 8 + ((y_hi + dy) % 2) * 4 + (z + dz) % 4
                to_piece, first = side * 2 + target // 16, target // 2 % 8
                row = row_of(part, first)
                for f in range(HELD):
                    rows_ref[to_piece, first, part, f] = field_lines(to_piece * HELD + f, row)
                sends.append(
                    pltpu.make_async_remote_copy(
                        src_ref=rows_ref.at[to_piece, first, part],
                        dst_ref=held_refs[part].at[:, my_lines],
                        send_sem=rows_sem,
                        recv_sem=held_sem.at[part],
                        device_id={"az": target, "rad": (1 - y_lo) * 2 + side},
                        device_id_type=MESH,
                    )
                )
            for send in sends:
                send.start()
            return carry

        lax.fori_loop(0, RING // GROUPED, some, 0)

    for part in range(PARTS):
        send_out(part)

    def same_size(ref, send_sem, recv_sem):
        return pltpu.make_async_remote_copy(
            src_ref=ref, dst_ref=ref, send_sem=send_sem, recv_sem=recv_sem,
            device_id={"az": az, "rad": (rad + 2) % 4}, device_id_type=MESH,
        )

    lane = lax.broadcasted_iota(jnp.int32, (8, TILE), 1)

    def taps_of(cells, weights):
        taps = []
        for n, weight in enumerate(weights):
            part = ((cells + n) % 4) * NZ
            halo = (lane + part) % TILE < TILE - NZ
            taps.append((1 - (cells % 4 + n) // 4, part, lane < TILE - part, halo, weight))
        return cells // 4, taps

    def blend(taps, tile_lines, halo_lines, fields):
        inner, outer = [None] * fields, None
        for start, part, here, halo, weight in taps:
            for f in range(fields):
                both = jnp.where(here, tile_lines(f, start + 2), tile_lines(f, start + 1))
                term = weight * pltpu.roll(both, part, 1)
                inner[f] = term if inner[f] is None else inner[f] + term
            after = jnp.where(here, halo_lines(start + 10), halo_lines(start + 9))
            before = jnp.where(here, halo_lines(start + 1), halo_lines(start))
            term = weight * pltpu.roll(jnp.where(halo, after, before), part, 1)
            outer = term if outer is None else outer + term
        return inner, outer

    odd = lax.broadcasted_iota(jnp.int32, (8, TILE), 0) % 2 == 1

    def ghost_taps():
        source_row = jnp.where(for_inner, ROWS * 4 - 1, ghost // 16)
        shift, fraction = shift_ref[source_row], frac_ref[source_row]
        edge_shift, edge_frac = edge_shift_ref[0], edge_frac_ref[0]
        more = jnp.where(for_inner, edge_shift, RING * COLUMNS // NZ - 1 - edge_shift)
        edge = jnp.where(for_inner, edge_frac, 1.0 - edge_frac)
        return taps_of(
            lax.rem(shift + more, RING * COLUMNS // NZ),
            (
                (1.0 - edge) * (1.0 - fraction),
                (1.0 - edge) * fraction + edge * (1.0 - fraction),
                edge * fraction,
            ),
        )

    def target(k):
        dx, dz, dy = k % 4, (k // 4 + k) % 4, (k // 16 + k) % 2
        return ((x + dx) % 4) * 8 + ((y_hi + dy) % 2) * 4 + (z + dz) % 4

    def first_tile(d, whole):
        return lax.rem(8 * d + 2 * TILES - 3 - whole, TILES)

    def send_back(part):
        held_ref = held_refs[part]
        same_size(held_ref.at[:, :TILES], rows_sem, held_sem.at[part]).wait_recv()
        for f in range(HELD):
            held_ref[f, TILES:] = held_ref[f, :PAD]
        eighth, rest = row_of(part, first_row)
        r = group * ROWS + eighth * 8 + rest
        shift, fraction = shift_ref[r], frac_ref[r]
        whole, taps = taps_of(shift, (1.0 - fraction, fraction))

        def fill(d):
            base = first_tile(d, whole)

            def halo_lines(n):
                pair = [
                    jnp.broadcast_to(held_ref[f, pl.ds(base + n, 1), :], (8, TILE))
                    for f in range(HELD)
                ]
                return jnp.where(odd, pair[1], pair[0])

            inner, outer = blend(
                taps, lambda f, n: held_ref[f, pl.ds(base + n, 8), :], halo_lines, HELD
            )
            for f in range(HELD):
                moved_ref[part, d, f * 8 : f * 8 + 8] = inner[f]
            moved_ref[part, d, HELD * 8 :] = outer

        def some(j, carry):
            ds = [target(j * GROUPED + m) for m in range(GROUPED)]
            for d in ds:
                fill(d)
            for d in ds:
                pltpu.make_async_remote_copy(
                    src_ref=moved_ref.at[part, d, :WINDOW],
                    dst_ref=cells_ref.at[eighth + 1, rest, piece, :WINDOW],
                    send_sem=back_sem,
                    recv_sem=row_sem.at[part],
                    device_id={"az": d, "rad": group},
                    device_id_type=MESH,
                ).start()
            return carry

        lax.fori_loop(0, RING // GROUPED, some, 0)

    def send_ghosts():
        same_size(strip_held_ref.at[:TILES], strips_sem, strip_held_sem).wait_recv()
        strip_held_ref[TILES:, :] = strip_held_ref[:PAD, :]
        whole, taps = ghost_taps()

        def fill(d):
            base = first_tile(d, whole)
            lines = lambda n: strip_held_ref[pl.ds(base + n, 8), :]
            inner, outer = blend(taps, lambda f, n: lines(n), lines, 1)
            moved_strip_ref[d, 0:8] = inner[0]
            moved_strip_ref[d, 8:16] = outer

        def some(j, carry):
            ds = [target(j * GROUPED + m) for m in range(GROUPED)]
            for d in ds:
                fill(d)
            for d in ds:
                pltpu.make_async_remote_copy(
                    src_ref=moved_strip_ref.at[d, :9],
                    dst_ref=ghosts_ref.at[pl.ds(pl.multiple_of(ghost * 16, 16), 9)],
                    send_sem=ghosts_back_sem,
                    recv_sem=ghosts_sem,
                    device_id={"az": d, "rad": group},
                    device_id_type=MESH,
                ).start()
            return carry

        lax.fori_loop(0, RING // GROUPED, some, 0)

    for part in range(PARTS):
        send_back(part)
        if part == 0:
            pl.when(has_ghost)(send_ghosts)

    def arrived(part):
        same_size(cells_ref.at[1, :, :, :WINDOW], back_sem, row_sem.at[part]).wait_recv()

    def hand(source, slot, n, neighbour):
        return pltpu.make_async_remote_copy(
            src_ref=source,
            dst_ref=slot,
            send_sem=hand_sem.at[n],
            recv_sem=handed_sem.at[n],
            device_id={"az": az, "rad": neighbour},
            device_id_type=MESH,
        )

    to_outer = [hand(cells_ref.at[4, 7, :, :WINDOW], cells_ref.at[0, 7, :, :WINDOW], 0, (rad + 1) % 4)]
    to_inner = [
        hand(cells_ref.at[1, 0, :, :WINDOW], cells_ref.at[5, 0, :, :WINDOW], 1, (rad + 3) % 4),
        hand(cells_ref.at[1, 1, BX_PIECE, :WINDOW], cells_ref.at[5, 1, BX_PIECE, :WINDOW], 2, (rad + 3) % 4),
    ]
    arrived(0)

    @pl.when(rad < 3)
    def _():
        for copy in to_outer:
            copy.start()

    @pl.when(rad > 0)
    def _():
        for copy in to_inner:
            copy.start()

    lines_ref = cells_ref.reshape(SLOTS[0] * SLOTS[1] * PIECES * LINES, TILE)

    def take_ghosts(ghosts):
        same_size(ghosts_ref.at[: len(ghosts) * 9], ghosts_back_sem, ghosts_sem).wait_recv()
        for n in ghosts:
            row, field = (-1, n) if n < 8 else (ROWS, n - 8) if n < 16 else (ROWS + 1, 4)
            first = ((row + 8) * PIECES + field // HELD) * LINES
            at, ninth = first + field % HELD * 8, first + HELD * 8 + field % HELD
            lines_ref[at : at + 8, :] = ghosts_ref[n * 16 : n * 16 + 8]
            lines_ref[ninth : ninth + 1, :] = ghosts_ref[n * 16 + 8 : n * 16 + 9]

    def received(copies):
        for copy in copies:
            copy.wait_recv()

    before_first, step = stepper(lines_ref, out_ref, flux_ref, part_ref, emf_ref, cell_ref, side_ref)

    def one(block, carry):
        @pl.when(block == 0)
        def _():
            arrived(1)
            pl.when(rad > 0)(lambda: received(to_outer))
            pl.when(rad == 0)(lambda: take_ghosts(range(8)))
            before_first()

        pl.when(block == 1)(lambda: arrived(2))

        @pl.when(block == 2)
        def _():
            arrived(3)
            pl.when(rad < 3)(lambda: received(to_inner))
            pl.when(rad == 3)(lambda: take_ghosts(range(8, GHOSTS)))

        step(block)
        return carry

    lax.fori_loop(0, ROWS // 8, one, 0)

    same_size(rows_ref, rows_sem, held_sem.at[0]).wait_send()
    same_size(moved_ref.at[:, :, :WINDOW], back_sem, held_sem.at[0]).wait_send()

    @pl.when(rad == 3)
    def _():
        same_size(strips_ref.at[:8], strips_sem, held_sem.at[0]).wait_send()

    @pl.when(rad == 0)
    def _():
        same_size(strips_ref.at[8:GHOSTS], strips_sem, held_sem.at[0]).wait_send()

    @pl.when(has_ghost)
    def _():
        same_size(moved_strip_ref.at[:, :9], ghosts_back_sem, held_sem.at[0]).wait_send()

    @pl.when(rad < 3)
    def _():
        for copy in to_outer:
            copy.wait_send()

    @pl.when(rad > 0)
    def _():
        for copy in to_inner:
            copy.wait_send()


def side(cell, normal, face):
    density, momenta, magnetic, tracer, inverse = cell
    field = list(magnetic)
    field[normal] = face
    square = field[0] * field[0] + field[1] * field[1] + field[2] * field[2]
    speed = momenta[normal] * inverse
    flux = [momenta[normal]]
    for n in range(3):
        term = momenta[n] * speed - face * field[n]
        if n == normal:
            term = term + (density + 0.5 * square)
        flux.append(term)
    flux.append(tracer * speed)
    reach = 1.0 + square * inverse
    return flux, jnp.abs(speed) + reach * lax.rsqrt(reach)


def face_flux(before, cell, normal, face):
    left, left_signal = side(before, normal, face)
    right, right_signal = side(cell, normal, face)
    bound = jnp.maximum(left_signal, right_signal)
    left_state = [before[0], *before[1], before[3]]
    right_state = [cell[0], *cell[1], cell[3]]
    return [
        0.5 * ((left[n] + right[n]) - bound * (right_state[n] - left_state[n])) for n in range(5)
    ]


def stepper(cells_ref, out_ref, flux_ref, part_ref, emf_ref, cell_ref, side_ref):
    lane = lax.broadcasted_iota(jnp.int32, (8, TILE), 1)
    level = lane % NZ
    up = jnp.where(level == NZ - 1, lane - (NZ - 1), lane + 1)
    down = jnp.where(level == 0, lane + (NZ - 1), lane - 1)

    def load(field, row, tile):
        line = field % HELD * 8 + tile if tile < 8 else HELD * 8 + field % HELD
        first = ((row + 8) * PIECES + field // HELD) * LINES + line
        return cells_ref[pl.ds(first, 8, stride=PIECES * LINES), :]

    def plus_z(v):
        return jnp.take_along_axis(v, up, axis=1, mode="promise_in_bounds")

    def minus_z(v):
        return jnp.take_along_axis(v, down, axis=1, mode="promise_in_bounds")

    def minus_y(before, v):
        return pltpu.roll(jnp.where(lane >= TILE - NZ, before, v), NZ, 1)

    def plus_y(v, after):
        return pltpu.roll(jnp.where(lane < NZ, after, v), TILE - NZ, 1)

    def lines_of(row):
        return pl.ds(pl.multiple_of(row + 16, 8), 8)

    def work_out(row):
        for tile in range(9):
            density = load(0, row + 1, tile)
            faces = [load(n, row + 1, tile) for n in (4, 5, 6)]
            c = [
                0.5 * (faces[0] + load(4, row + 2, tile)),
                0.5 * (faces[1] + plus_y(faces[1], load(5, row + 1, (tile + 1) % 9))),
                0.5 * (faces[2] + plus_z(faces[2])),
            ]
            inverse = 1.0 / density
            v = [load(n, row + 1, tile) * inverse for n in (1, 2, 3)]
            emf = [v[2] * c[1] - v[1] * c[2], v[0] * c[2] - v[2] * c[0], v[1] * c[0] - v[0] * c[1]]
            for n, value in enumerate([*c, inverse, *emf]):
                cell_ref[tile, n, lines_of(row), :] = value

    def known(n, row, tile):
        return cell_ref[tile, n, pl.ds(row + 15, 8), :]

    def cell_at(row, tile):
        return (
            load(0, row, tile),
            [load(n, row, tile) for n in (1, 2, 3)],
            [known(n, row, tile) for n in (0, 1, 2)],
            load(7, row, tile),
            known(3, row, tile),
        )

    def outer_flux(row, tile, cell):
        flux = face_flux(cell, cell_at(row + 1, tile), 0, load(4, row + 1, tile))
        for n in range(5):
            side_ref[tile, n, lines_of(row), :] = flux[n]
        return flux

    def before_first():
        work_out(-8)
        for tile in range(8):
            outer_flux(-8, tile, cell_at(-8, tile))

    def first(row, tile):
        before = (tile + 8) % 9
        cell = cell_at(row, tile)
        density, momenta, centred, tracer, inverse = cell
        faces = [load(n, row, tile) for n in (4, 5, 6)]

        def behind_of(field):
            return minus_y(load(field, row, before), load(field, row, tile))

        behind_density = behind_of(0)
        behind = (
            behind_density,
            [behind_of(n) for n in (1, 2, 3)],
            [minus_y(known(0, row, before), centred[0]), None, minus_y(known(2, row, before), centred[2])],
            behind_of(7),
            1.0 / behind_density,
        )
        flux_y = face_flux(behind, cell, 1, faces[1])
        for n in range(5):
            flux_ref[tile, n] = flux_y[n]

        emf_x, z_here = known(4, row, tile), known(6, row, tile)
        z_lower, z_upper = known(6, row - 1, tile), known(6, row + 1, tile)
        x_below = minus_z(emf_x)
        emf_ref[tile, 0] = z_here + z_lower
        emf_ref[tile, 1] = (plus_z(emf_x) - x_below) - (z_upper - z_lower)
        emf_ref[tile, 2] = emf_x + x_below
        if tile == 8:
            return
        y_here, y_lower, y_upper = known(5, row, tile), known(5, row - 1, tile), known(5, row + 1, tile)
        y_pair, y_across = y_here + y_lower, y_upper - y_lower
        part_ref[tile, 5] = faces[0] + 0.25 * TIME_STEP * (plus_z(y_pair) - minus_z(y_pair))
        part_ref[tile, 6] = faces[1]
        part_ref[tile, 7] = faces[2] - 0.25 * TIME_STEP * (y_across + minus_z(y_across))

        flux_high = outer_flux(row, tile, cell)
        flux_low = [side_ref[tile, n, pl.ds(row + 15, 8), :] for n in range(5)]
        below = (
            minus_z(density),
            [minus_z(m) for m in momenta],
            [minus_z(centred[0]), minus_z(centred[1]), None],
            minus_z(tracer),
            minus_z(inverse),
        )
        flux_z = face_flux(below, cell, 2, faces[2])
        state = [density, *momenta, tracer]
        for n in range(5):
            change = (flux_high[n] - flux_low[n]) + (plus_z(flux_z[n]) - flux_z[n])
            value = state[n] - TIME_STEP * change
            if n == 1:
                value = value + TIME_STEP * 2.0 * momenta[1]
            if n == 2:
                value = value - TIME_STEP * 0.5 * momenta[0]
            part_ref[tile, n] = value

    def last(row, tile):
        before, after = (tile + 8) % 9, tile + 1
        rows, columns = pl.ds(row, 8), pl.ds(tile * TILE, TILE)
        for n, field in enumerate((0, 1, 2, 3, 7)):
            flux = flux_ref[tile, n]
            out_ref[field, rows, columns] = part_ref[tile, n] - TIME_STEP * (
                plus_y(flux, flux_ref[after, n]) - flux
            )
        around = [(emf_ref[before, n], emf_ref[tile, n], emf_ref[after, n]) for n in range(3)]
        across_z = plus_y(around[0][1], around[0][2]) - minus_y(around[0][0], around[0][1])
        pair = around[1][1] + minus_y(around[1][0], around[1][1])
        across_x = plus_y(around[2][1], around[2][2]) - minus_y(around[2][0], around[2][1])
        out_ref[4, rows, columns] = part_ref[tile, 5] - 0.25 * TIME_STEP * across_z
        out_ref[5, rows, columns] = part_ref[tile, 6] - 0.25 * TIME_STEP * pair
        out_ref[6, rows, columns] = part_ref[tile, 7] + 0.25 * TIME_STEP * across_x

    def step(block):
        row = pl.multiple_of(block * 8, 8)
        work_out(row)
        for tile in range(9):
            first(row, tile)
        for tile in range(8):
            last(row, tile)

    return before_first, step


def per_device(state, row_shift, row_frac, edge_shift, edge_frac):
    tiles = state.reshape(FIELDS, ROWS // 8, 8, COLUMNS // TILE, TILE).transpose(0, 1, 3, 2, 4)
    tiles = tiles.reshape(FIELDS * ROWS * 8, TILE)
    dma, smem = pltpu.SemaphoreType.DMA, pltpu.SMEM

    def vmem(*shape):
        return pltpu.VMEM(shape, jnp.float32)

    return pl.pallas_call(
        kernel,
        out_shape=jax.ShapeDtypeStruct((FIELDS, ROWS, COLUMNS), jnp.float32),
        in_specs=[pl.BlockSpec(memory_space=pltpu.HBM)] * 3 + [pl.BlockSpec(memory_space=pltpu.SMEM)] * 2,
        out_specs=pl.BlockSpec(memory_space=pltpu.VMEM),
        scratch_shapes=[
            vmem(*tiles.shape),
            smem(row_shift.shape, jnp.int32), smem(row_frac.shape, jnp.float32),
            vmem(PIECES, 8, PARTS, HELD, 8, TILE),
            vmem(GHOSTS, 8, TILE),
            *[vmem(HELD, TILES + PAD, TILE)] * PARTS,
            vmem(TILES + PAD, TILE),
            vmem(PARTS, RING, LINES, TILE),
            vmem(RING, 16, TILE),
            vmem(*SLOTS, PIECES, LINES, TILE),
            vmem(GHOSTS * 16, TILE),
            vmem(9, 5, 8, TILE), vmem(9, 8, 8, TILE), vmem(9, 3, 8, TILE),
            vmem(9, 7, 48, TILE), vmem(8, 5, 48, TILE),
            dma((3,)), dma, dma, dma, dma, dma((PARTS,)), dma, dma((PARTS,)), dma, dma((3,)), dma((3,)),
        ],
        compiler_params=pltpu.CompilerParams(
            collective_id=0, has_side_effects=True, vmem_limit_bytes=VMEM_LIMIT
        ),
        name="step",
    )(
        *[pltpu.with_memory_space_constraint(a, pltpu.HBM) for a in (tiles, row_shift, row_frac)],
        edge_shift,
        edge_frac,
    )


def solution(mesh):
    return jax.shard_map(
        per_device,
        mesh=mesh,
        in_specs=(P(None, "rad", "az"), P(), P(), P(), P()),
        out_specs=P(None, "rad", "az"),
        check_vma=False,
    )
```

```python
import jax
import jax.numpy as jnp
from jax import lax
from jax.experimental import pallas as pl
from jax.experimental.pallas import tpu as pltpu
from jax.sharding import PartitionSpec as P

MESH = pl.DeviceIdType.MESH
NZ = 32
FIELDS = 8
HELD = 2
PIECES = 4
PARTS = 4
GROUPED = 4
ROWS = 32
COLUMNS = 1024
RING = 32
TILE = 128
TILES = RING * COLUMNS // TILE
PAD = 24
WINDOW = 18
SHORT = 17
LINES = 24
SLOTS = (6, 8)
B_PIECE = 2
GHOSTS = 17
VMEM_LIMIT = 28 * 2**20
TIME_STEP = 0.2


def share(lane, v):
    at = jnp.where(lane < TILE // 2, lane - NZ, lane + NZ)
    middle = jnp.logical_and(lane >= NZ, lane < TILE - NZ)
    return jnp.take_along_axis(v, jnp.where(middle, at, lane), axis=1, mode="promise_in_bounds")


def place():
    az, rad = lax.axis_index("az"), lax.axis_index("rad")
    return az // 8, (az // 4) % 2, az % 4, rad // 2, rad % 2


def row_of(part, first):
    last = first == 7
    if part == 0:
        return jnp.where(last, 3, 0), first
    return part - jnp.where(last, 1, 0), first


def ghost_holder(n):
    i = 2 if n == 16 else n % 8 // 2 * 4 + n % 2
    group = 0 if n < 8 else 3
    low = (group % 2 + i // 4 + (i // 2) % 2) % 2
    return {"az": 2 * i + low, "rad": 2 if n < 8 else 1}


def ghost_source(n):
    if n < 8:
        return ROWS - 1, n
    if n < 16:
        return 0, n - 8
    return 1, 4


def kernel(
    state_hbm, shift_hbm, frac_hbm, edge_shift_ref, edge_frac_ref,
    out_ref,
    state_ref, shift_ref, frac_ref,
    rows_ref, strips_ref, held_0_ref, held_1_ref, held_2_ref, held_3_ref, strip_held_ref,
    moved_ref, moved_strip_ref, cells_ref, ghosts_ref,
    flux_ref, part_ref, emf_ref, cell_ref, side_ref,
    in_sem, rows_sem, strips_sem, back_sem, ghosts_back_sem, held_sem, strip_held_sem, row_sem, ghosts_sem,
    hand_sem, handed_sem,
):
    x, y_hi, z, y_lo, core = place()
    az, rad = lax.axis_index("az"), lax.axis_index("rad")
    parity = (x + y_hi + z) % 2
    group = (1 - y_lo) * 2 + parity
    index = core * 16 + az // 2
    piece, first_row = index // 8, index % 8
    held_refs = (held_0_ref, held_1_ref, held_2_ref, held_3_ref)
    among = index % 16
    for_inner = jnp.logical_and(jnp.logical_and(group == 0, core == 0), among % 4 < 2)
    for_outer = jnp.logical_and(
        jnp.logical_and(group == 3, core == 1), jnp.logical_or(among % 4 < 2, among == 2)
    )
    has_ghost = jnp.logical_or(for_inner, for_outer)
    ghost = jnp.where(among == 2, 16, among // 4 * 2 + among % 4 + jnp.where(for_outer, 8, 0))

    loads = [
        pltpu.make_async_copy(source, target, in_sem.at[n])
        for n, (source, target) in enumerate(
            ((state_hbm, state_ref), (shift_hbm, shift_ref), (frac_hbm, frac_ref))
        )
    ]
    for load in loads:
        load.start()

    barrier = pltpu.get_barrier_semaphore()

    def greet(target_az, target_rad):
        pl.semaphore_signal(
            barrier, inc=1, device_id={"az": target_az, "rad": target_rad}, device_id_type=MESH
        )

    for d in range(RING):
        greet(d, group)

    @pl.when(rad > 0)
    def _():
        greet(az, rad - 1)

    @pl.when(rad < 3)
    def _():
        greet(az, rad + 1)

    @pl.when(has_ghost)
    def _():
        for d in range(RING):
            greet(d, 3 - group)

    for load in loads:
        load.wait()

    def field_lines(field, row):
        eighth, rest = row if isinstance(row, tuple) else (row // 8, row % 8)
        return state_ref[pl.ds(field * 256 + eighth * 64 + rest, 8, stride=8), :]

    pl.semaphore_wait(barrier, RING + jnp.where(rad == 0, 10, jnp.where(rad == 3, 9, 2)))

    my_lines = pl.ds(pl.multiple_of(az * 8, 8), 8)

    def send_strips(ghosts):
        for n in ghosts:
            r, field = ghost_source(n)
            strips_ref[n] = field_lines(field, r)
            pltpu.make_async_remote_copy(
                src_ref=strips_ref.at[n],
                dst_ref=strip_held_ref.at[my_lines],
                send_sem=strips_sem,
                recv_sem=strip_held_sem,
                device_id=ghost_holder(n),
                device_id_type=MESH,
            ).start()

    pl.when(rad == 3)(lambda: send_strips(range(8)))
    pl.when(rad == 0)(lambda: send_strips(range(8, GHOSTS)))
    offset_parity = (core + parity) % 2

    def send_out(part):
        def some(j, carry):
            sends = []
            for m in range(GROUPED):
                k = j * GROUPED + m
                side, i = k // 16, k % 16
                dx, dz = i % 4, (i // 4 + i) % 4
                dy = (offset_parity + dx + dz) % 2
                target = ((x + dx) % 4) * 8 + ((y_hi + dy) % 2) * 4 + (z + dz) % 4
                to_piece, first = side * 2 + target // 16, target // 2 % 8
                row = row_of(part, first)
                for f in range(HELD):
                    rows_ref[to_piece, first, part, f] = field_lines(to_piece * HELD + f, row)
                sends.append(
                    pltpu.make_async_remote_copy(
                        src_ref=rows_ref.at[to_piece, first, part],
                        dst_ref=held_refs[part].at[:, my_lines],
                        send_sem=rows_sem,
                        recv_sem=held_sem.at[part],
                        device_id={"az": target, "rad": (1 - y_lo) * 2 + side},
                        device_id_type=MESH,
                    )
                )
            for send in sends:
                send.start()
            return carry

        lax.fori_loop(0, RING // GROUPED, some, 0)

    for part in range(PARTS):
        send_out(part)

    def same_size(ref, send_sem, recv_sem):
        return pltpu.make_async_remote_copy(
            src_ref=ref, dst_ref=ref, send_sem=send_sem, recv_sem=recv_sem,
            device_id={"az": az, "rad": (rad + 2) % 4}, device_id_type=MESH,
        )

    lane = lax.broadcasted_iota(jnp.int32, (8, TILE), 1)

    def taps_of(cells, weights):
        taps = []
        for n, weight in enumerate(weights):
            part = ((cells + n) % 4) * NZ
            halo = (lane + part) % TILE < TILE - NZ
            taps.append((1 - (cells % 4 + n) // 4, part, lane < TILE - part, halo, weight))
        return cells // 4, taps

    def blend(taps, tile_lines, halo_lines, fields):
        inner, outer = [None] * fields, None
        for start, part, here, halo, weight in taps:
            for f in range(fields):
                both = jnp.where(here, tile_lines(f, start + 2), tile_lines(f, start + 1))
                term = weight * pltpu.roll(both, part, 1)
                inner[f] = term if inner[f] is None else inner[f] + term
            after = jnp.where(here, halo_lines(start + 10), halo_lines(start + 9))
            before = jnp.where(here, halo_lines(start + 1), halo_lines(start))
            term = weight * pltpu.roll(jnp.where(halo, after, before), part, 1)
            outer = term if outer is None else outer + term
        return inner, outer

    middle = jnp.logical_and(lane >= NZ, lane < TILE - NZ)
    odd = lax.broadcasted_iota(jnp.int32, (8, TILE), 0) % 2 == 1

    def ghost_taps():
        source_row = jnp.where(for_inner, ROWS * 4 - 1, ghost // 16)
        shift, fraction = shift_ref[source_row], frac_ref[source_row]
        edge_shift, edge_frac = edge_shift_ref[0], edge_frac_ref[0]
        more = jnp.where(for_inner, edge_shift, RING * COLUMNS // NZ - 1 - edge_shift)
        edge = jnp.where(for_inner, edge_frac, 1.0 - edge_frac)
        return taps_of(
            lax.rem(shift + more, RING * COLUMNS // NZ),
            (
                (1.0 - edge) * (1.0 - fraction),
                (1.0 - edge) * fraction + edge * (1.0 - fraction),
                edge * fraction,
            ),
        )

    def target(k):
        dx, dz, dy = k % 4, (k // 4 + k) % 4, (k // 16 + k) % 2
        return ((x + dx) % 4) * 8 + ((y_hi + dy) % 2) * 4 + (z + dz) % 4

    def first_tile(d, whole):
        return lax.rem(8 * d + 2 * TILES - 3 - whole, TILES)

    def send_back(part):
        held_ref = held_refs[part]
        same_size(held_ref.at[:, :TILES], rows_sem, held_sem.at[part]).wait_recv()
        for f in range(HELD):
            held_ref[f, TILES:] = held_ref[f, :PAD]
        eighth, rest = row_of(part, first_row)
        r = group * ROWS + eighth * 8 + rest
        shift, fraction = shift_ref[r], frac_ref[r]
        whole, taps = taps_of(shift, (1.0 - fraction, fraction))

        def fill(d):
            base = first_tile(d, whole)

            def halo_lines(n):
                pair = [
                    jnp.broadcast_to(held_ref[f, pl.ds(base + n, 1), :], (8, TILE))
                    for f in range(HELD)
                ]
                return jnp.where(odd, pair[1], pair[0])

            inner, outer = blend(
                taps, lambda f, n: held_ref[f, pl.ds(base + n, 8), :], halo_lines, HELD
            )
            for f in range(HELD):
                moved_ref[part, d, f * 8 : f * 8 + 8] = inner[f]
            second = share(lane, pltpu.roll(outer, 1, 0))
            shared = jnp.where(jnp.logical_and(middle, piece != B_PIECE), second, outer)
            moved_ref[part, d, HELD * 8 :] = shared

        def some(j, carry):
            ds = [target(j * GROUPED + m) for m in range(GROUPED)]
            for d in ds:
                fill(d)

            def send(size):
                for d in ds:
                    pltpu.make_async_remote_copy(
                        src_ref=moved_ref.at[part, d, :size],
                        dst_ref=cells_ref.at[eighth + 1, rest, piece, :size],
                        send_sem=back_sem,
                        recv_sem=row_sem.at[part],
                        device_id={"az": d, "rad": group},
                        device_id_type=MESH,
                    ).start()

            pl.when(piece == B_PIECE)(lambda: send(WINDOW))
            pl.when(piece != B_PIECE)(lambda: send(SHORT))
            return carry

        lax.fori_loop(0, RING // GROUPED, some, 0)

    def send_ghosts():
        same_size(strip_held_ref.at[:TILES], strips_sem, strip_held_sem).wait_recv()
        strip_held_ref[TILES:, :] = strip_held_ref[:PAD, :]
        whole, taps = ghost_taps()

        def fill(d):
            base = first_tile(d, whole)
            lines = lambda n: strip_held_ref[pl.ds(base + n, 8), :]
            inner, outer = blend(taps, lambda f, n: lines(n), lines, 1)
            moved_strip_ref[d, 0:8] = inner[0]
            moved_strip_ref[d, 8:16] = outer

        def some(j, carry):
            ds = [target(j * GROUPED + m) for m in range(GROUPED)]
            for d in ds:
                fill(d)
            for d in ds:
                pltpu.make_async_remote_copy(
                    src_ref=moved_strip_ref.at[d, :9],
                    dst_ref=ghosts_ref.at[pl.ds(pl.multiple_of(ghost * 16, 16), 9)],
                    send_sem=ghosts_back_sem,
                    recv_sem=ghosts_sem,
                    device_id={"az": d, "rad": group},
                    device_id_type=MESH,
                ).start()
            return carry

        lax.fori_loop(0, RING // GROUPED, some, 0)

    for part in range(PARTS):
        send_back(part)
        if part == 0:
            pl.when(has_ghost)(send_ghosts)

    lines_ref = cells_ref.reshape(SLOTS[0] * SLOTS[1] * PIECES * LINES, TILE)

    def arrived(part):
        lines = 8 * (3 * SHORT + WINDOW)
        same_size(lines_ref.at[:lines], back_sem, row_sem.at[part]).wait_recv()

    def hand(source, slot, n, neighbour):
        return pltpu.make_async_remote_copy(
            src_ref=source,
            dst_ref=slot,
            send_sem=hand_sem.at[n],
            recv_sem=handed_sem.at[n],
            device_id={"az": az, "rad": neighbour},
            device_id_type=MESH,
        )

    outer, inner = (rad + 1) % 4, (rad + 3) % 4
    last = (B_PIECE, slice(SHORT, WINDOW))
    to_outer = [
        hand(cells_ref.at[4, 7, :, :SHORT], cells_ref.at[0, 7, :, :SHORT], 0, outer),
        hand(cells_ref.at[4, 7, *last], cells_ref.at[0, 7, *last], 1, outer),
    ]
    to_inner = [
        hand(cells_ref.at[1, 0, :, :SHORT], cells_ref.at[5, 0, :, :SHORT], 2, inner),
        hand(cells_ref.at[1, 0, *last], cells_ref.at[5, 0, *last], 3, inner),
        hand(cells_ref.at[1, 1, B_PIECE, :SHORT], cells_ref.at[5, 1, B_PIECE, :SHORT], 4, inner),
    ]
    arrived(0)

    @pl.when(rad < 3)
    def _():
        for copy in to_outer:
            copy.start()

    @pl.when(rad > 0)
    def _():
        for copy in to_inner:
            copy.start()

    def take_ghosts(ghosts):
        same_size(ghosts_ref.at[: len(ghosts) * 9], ghosts_back_sem, ghosts_sem).wait_recv()
        for n in ghosts:
            row, field = (-1, n) if n < 8 else (ROWS, n - 8) if n < 16 else (ROWS + 1, 4)
            first = ((row + 8) * PIECES + field // HELD) * LINES
            at, ninth = first + field % HELD * 8, first + HELD * 8 + field % HELD
            lines_ref[at : at + 8, :] = ghosts_ref[n * 16 : n * 16 + 8]
            line = ghosts_ref[n * 16 + 8 : n * 16 + 9]
            if field // HELD == B_PIECE:
                lines_ref[ninth : ninth + 1, :] = line
            elif field % HELD == 0:
                second = jnp.broadcast_to(ghosts_ref[n * 16 + 24 : n * 16 + 25], (8, TILE))
                both = jnp.where(middle, share(lane, second), jnp.broadcast_to(line, (8, TILE)))
                lines_ref[ninth : ninth + 1, :] = both[:1]

    def received(copies):
        for copy in copies:
            copy.wait_recv()

    before_first, step = stepper(lines_ref, out_ref, flux_ref, part_ref, emf_ref, cell_ref, side_ref)

    def one(block, carry):
        @pl.when(block == 0)
        def _():
            arrived(1)
            pl.when(rad > 0)(lambda: received(to_outer))
            pl.when(rad == 0)(lambda: take_ghosts(range(8)))
            before_first()

        pl.when(block == 1)(lambda: arrived(2))

        @pl.when(block == 2)
        def _():
            arrived(3)
            pl.when(rad < 3)(lambda: received(to_inner))
            pl.when(rad == 3)(lambda: take_ghosts(range(8, GHOSTS)))

        step(block)
        return carry

    lax.fori_loop(0, ROWS // 8, one, 0)

    same_size(rows_ref, rows_sem, held_sem.at[0]).wait_send()
    for size, sent in ((WINDOW, piece == B_PIECE), (SHORT, piece != B_PIECE)):
        whole = same_size(moved_ref.at[:, :, :size], back_sem, held_sem.at[0])
        pl.when(sent)(whole.wait_send)

    @pl.when(rad == 3)
    def _():
        same_size(strips_ref.at[:8], strips_sem, held_sem.at[0]).wait_send()

    @pl.when(rad == 0)
    def _():
        same_size(strips_ref.at[8:GHOSTS], strips_sem, held_sem.at[0]).wait_send()

    @pl.when(has_ghost)
    def _():
        same_size(moved_strip_ref.at[:, :9], ghosts_back_sem, held_sem.at[0]).wait_send()

    @pl.when(rad < 3)
    def _():
        for copy in to_outer:
            copy.wait_send()

    @pl.when(rad > 0)
    def _():
        for copy in to_inner:
            copy.wait_send()


def side(cell, normal, face):
    density, momenta, magnetic, tracer, inverse = cell
    field = list(magnetic)
    field[normal] = face
    square = field[0] * field[0] + field[1] * field[1] + field[2] * field[2]
    speed = momenta[normal] * inverse
    flux = [momenta[normal]]
    for n in range(3):
        term = momenta[n] * speed - face * field[n]
        if n == normal:
            term = term + (density + 0.5 * square)
        flux.append(term)
    flux.append(tracer * speed)
    reach = 1.0 + square * inverse
    return flux, jnp.abs(speed) + reach * lax.rsqrt(reach)


def face_flux(before, cell, normal, face):
    left, left_signal = side(before, normal, face)
    right, right_signal = side(cell, normal, face)
    bound = jnp.maximum(left_signal, right_signal)
    left_state = [before[0], *before[1], before[3]]
    right_state = [cell[0], *cell[1], cell[3]]
    return [
        (left[n] + right[n]) - bound * (right_state[n] - left_state[n]) for n in range(5)
    ]


def stepper(cells_ref, out_ref, flux_ref, part_ref, emf_ref, cell_ref, side_ref):
    lane = lax.broadcasted_iota(jnp.int32, (8, TILE), 1)
    level = lane % NZ
    up = jnp.where(level == NZ - 1, lane - (NZ - 1), lane + 1)
    down = jnp.where(level == 0, lane + (NZ - 1), lane - 1)

    def load(field, row, tile):
        line = field % HELD * 8 + tile if tile < 8 else HELD * 8 + field % HELD
        first = ((row + 8) * PIECES + field // HELD) * LINES + line
        return cells_ref[pl.ds(first, 8, stride=PIECES * LINES), :]

    def plus_z(v):
        return jnp.take_along_axis(v, up, axis=1, mode="promise_in_bounds")

    def minus_z(v):
        return jnp.take_along_axis(v, down, axis=1, mode="promise_in_bounds")

    def minus_y(before, v):
        return pltpu.roll(jnp.where(lane >= TILE - NZ, before, v), NZ, 1)

    def plus_y(v, after):
        return pltpu.roll(jnp.where(lane < NZ, after, v), TILE - NZ, 1)

    def lines_of(row):
        return pl.ds(pl.multiple_of(row + 16, 8), 8)

    def part_lines(row):
        for piece in range(PIECES):
            if piece != B_PIECE:
                first = ((row + 8) * PIECES + piece) * LINES + HELD * 8
                both = cells_ref[pl.ds(first, 8, stride=PIECES * LINES), :]
                at = jnp.where(lane < NZ, lane + NZ, jnp.where(lane < TILE - NZ, lane, lane - NZ))
                second = jnp.take_along_axis(both, at, axis=1, mode="promise_in_bounds")
                cells_ref[pl.ds(first + 1, 8, stride=PIECES * LINES), :] = second

    def work_out(row):
        part_lines(row + 1)
        for tile in range(9):
            density = load(0, row + 1, tile)
            faces = [load(n, row + 1, tile) for n in (4, 5, 6)]
            c = [
                0.5 * (faces[0] + load(4, row + 2, tile)),
                0.5 * (faces[1] + plus_y(faces[1], load(5, row + 1, (tile + 1) % 9))),
                0.5 * (faces[2] + plus_z(faces[2])),
            ]
            inverse = 1.0 / density
            v = [load(n, row + 1, tile) * inverse for n in (1, 2, 3)]
            emf = [v[2] * c[1] - v[1] * c[2], v[0] * c[2] - v[2] * c[0], v[1] * c[0] - v[0] * c[1]]
            for n, value in enumerate([*c, inverse, *emf]):
                cell_ref[tile, n, lines_of(row), :] = value

    def known(n, row, tile):
        return cell_ref[tile, n, pl.ds(row + 15, 8), :]

    def cell_at(row, tile):
        return (
            load(0, row, tile),
            [load(n, row, tile) for n in (1, 2, 3)],
            [known(n, row, tile) for n in (0, 1, 2)],
            load(7, row, tile),
            known(3, row, tile),
        )

    def outer_flux(row, tile, cell):
        flux = face_flux(cell, cell_at(row + 1, tile), 0, load(4, row + 1, tile))
        for n in range(5):
            side_ref[tile, n, lines_of(row), :] = flux[n]
        return flux

    def before_first():
        work_out(-8)
        for tile in range(8):
            outer_flux(-8, tile, cell_at(-8, tile))

    def first(row, tile):
        before = (tile + 8) % 9
        cell = cell_at(row, tile)
        density, momenta, centred, tracer, inverse = cell
        faces = [load(n, row, tile) for n in (4, 5, 6)]

        def behind_of(field):
            return minus_y(load(field, row, before), load(field, row, tile))

        behind_density = behind_of(0)
        behind = (
            behind_density,
            [behind_of(n) for n in (1, 2, 3)],
            [minus_y(known(0, row, before), centred[0]), None, minus_y(known(2, row, before), centred[2])],
            behind_of(7),
            1.0 / behind_density,
        )
        flux_y = face_flux(behind, cell, 1, faces[1])
        for n in range(5):
            flux_ref[tile, n] = flux_y[n]

        emf_x, z_here = known(4, row, tile), known(6, row, tile)
        z_lower, z_upper = known(6, row - 1, tile), known(6, row + 1, tile)
        x_below = minus_z(emf_x)
        emf_ref[tile, 0] = z_here + z_lower
        emf_ref[tile, 1] = (plus_z(emf_x) - x_below) - (z_upper - z_lower)
        emf_ref[tile, 2] = emf_x + x_below
        if tile == 8:
            return
        y_here, y_lower, y_upper = known(5, row, tile), known(5, row - 1, tile), known(5, row + 1, tile)
        y_pair, y_across = y_here + y_lower, y_upper - y_lower
        part_ref[tile, 5] = faces[0] + 0.25 * TIME_STEP * (plus_z(y_pair) - minus_z(y_pair))
        part_ref[tile, 6] = faces[1]
        part_ref[tile, 7] = faces[2] - 0.25 * TIME_STEP * (y_across + minus_z(y_across))

        flux_high = outer_flux(row, tile, cell)
        flux_low = [side_ref[tile, n, pl.ds(row + 15, 8), :] for n in range(5)]
        below = (
            minus_z(density),
            [minus_z(m) for m in momenta],
            [minus_z(centred[0]), minus_z(centred[1]), None],
            minus_z(tracer),
            minus_z(inverse),
        )
        flux_z = face_flux(below, cell, 2, faces[2])
        state = [density, *momenta, tracer]
        for n in range(5):
            change = (flux_high[n] - flux_low[n]) + (plus_z(flux_z[n]) - flux_z[n])
            value = state[n] - 0.5 * TIME_STEP * change
            if n == 1:
                value = value + TIME_STEP * 2.0 * momenta[1]
            if n == 2:
                value = value - TIME_STEP * 0.5 * momenta[0]
            part_ref[tile, n] = value

    def last(row, tile):
        before, after = (tile + 8) % 9, tile + 1
        rows, columns = pl.ds(row, 8), pl.ds(tile * TILE, TILE)
        for n, field in enumerate((0, 1, 2, 3, 7)):
            flux = flux_ref[tile, n]
            out_ref[field, rows, columns] = part_ref[tile, n] - 0.5 * TIME_STEP * (
                plus_y(flux, flux_ref[after, n]) - flux
            )
        around = [(emf_ref[before, n], emf_ref[tile, n], emf_ref[after, n]) for n in range(3)]
        across_z = plus_y(around[0][1], around[0][2]) - minus_y(around[0][0], around[0][1])
        pair = around[1][1] + minus_y(around[1][0], around[1][1])
        across_x = plus_y(around[2][1], around[2][2]) - minus_y(around[2][0], around[2][1])
        out_ref[4, rows, columns] = part_ref[tile, 5] - 0.25 * TIME_STEP * across_z
        out_ref[5, rows, columns] = part_ref[tile, 6] - 0.25 * TIME_STEP * pair
        out_ref[6, rows, columns] = part_ref[tile, 7] + 0.25 * TIME_STEP * across_x

    def step(block):
        row = pl.multiple_of(block * 8, 8)
        work_out(row)
        for tile in range(9):
            first(row, tile)
        for tile in range(8):
            last(row, tile)

    return before_first, step


def per_device(state, row_shift, row_frac, edge_shift, edge_frac):
    tiles = state.reshape(FIELDS, ROWS // 8, 8, COLUMNS // TILE, TILE).transpose(0, 1, 3, 2, 4)
    tiles = tiles.reshape(FIELDS * ROWS * 8, TILE)
    dma, smem = pltpu.SemaphoreType.DMA, pltpu.SMEM

    def vmem(*shape):
        return pltpu.VMEM(shape, jnp.float32)

    return pl.pallas_call(
        kernel,
        out_shape=jax.ShapeDtypeStruct((FIELDS, ROWS, COLUMNS), jnp.float32),
        in_specs=[pl.BlockSpec(memory_space=pltpu.HBM)] * 3 + [pl.BlockSpec(memory_space=pltpu.SMEM)] * 2,
        out_specs=pl.BlockSpec(memory_space=pltpu.VMEM),
        scratch_shapes=[
            vmem(*tiles.shape),
            smem(row_shift.shape, jnp.int32), smem(row_frac.shape, jnp.float32),
            vmem(PIECES, 8, PARTS, HELD, 8, TILE),
            vmem(GHOSTS, 8, TILE),
            *[vmem(HELD, TILES + PAD, TILE)] * PARTS,
            vmem(TILES + PAD, TILE),
            vmem(PARTS, RING, LINES, TILE),
            vmem(RING, 16, TILE),
            vmem(*SLOTS, PIECES, LINES, TILE),
            vmem(GHOSTS * 16, TILE),
            vmem(9, 5, 8, TILE), vmem(9, 8, 8, TILE), vmem(9, 3, 8, TILE),
            vmem(9, 7, 48, TILE), vmem(8, 5, 48, TILE),
            dma((3,)), dma, dma, dma, dma, dma((PARTS,)), dma, dma((PARTS,)), dma, dma((5,)), dma((5,)),
        ],
        compiler_params=pltpu.CompilerParams(
            collective_id=0, has_side_effects=True, vmem_limit_bytes=VMEM_LIMIT
        ),
        name="step",
    )(
        *[pltpu.with_memory_space_constraint(a, pltpu.HBM) for a in (tiles, row_shift, row_frac)],
        edge_shift,
        edge_frac,
    )


def solution(mesh):
    return jax.shard_map(
        per_device,
        mesh=mesh,
        in_specs=(P(None, "rad", "az"), P(), P(), P(), P()),
        out_specs=P(None, "rad", "az"),
        check_vma=False,
    )
```

```python
import jax
import jax.numpy as jnp
from jax import lax
from jax.experimental import pallas as pl
from jax.experimental.pallas import tpu as pltpu
from jax.sharding import PartitionSpec as P

MESH = pl.DeviceIdType.MESH
NZ = 32
FIELDS = 8
HELD = 2
PIECES = 4
PARTS = 4
GROUPED = 4
ROWS = 32
COLUMNS = 1024
RING = 32
TILE = 128
TILES = RING * COLUMNS // TILE
PAD = 24
WINDOW = 18
SHORT = 17
LINES = 24
ROW_LINES = 104
SLOTS = (6, 8)
B_PIECE = 2
GHOSTS = 17
VMEM_LIMIT = 28 * 2**20
TIME_STEP = 0.2


def share(lane, v):
    at = jnp.where(lane < TILE // 2, lane - NZ, lane + NZ)
    middle = jnp.logical_and(lane >= NZ, lane < TILE - NZ)
    return jnp.take_along_axis(v, jnp.where(middle, at, lane), axis=1, mode="promise_in_bounds")


def place():
    az, rad = lax.axis_index("az"), lax.axis_index("rad")
    return az // 8, (az // 4) % 2, az % 4, rad // 2, rad % 2


def row_of(part, first):
    last = first == 7
    if part == 0:
        return jnp.where(last, 3, 0), first
    return part - jnp.where(last, 1, 0), first


def ghost_holder(n):
    i = 2 if n == 16 else n % 8 // 2 * 4 + n % 2
    group = 0 if n < 8 else 3
    low = (group % 2 + i // 4 + (i // 2) % 2) % 2
    return {"az": 2 * i + low, "rad": 2 if n < 8 else 1}


def ghost_source(n):
    if n < 8:
        return ROWS - 1, n
    if n < 16:
        return 0, n - 8
    return 1, 4


def kernel(
    state_hbm, shift_hbm, frac_hbm, edge_shift_ref, edge_frac_ref,
    out_ref,
    state_ref, shift_ref, frac_ref,
    rows_ref, strips_ref, held_0_ref, held_1_ref, held_2_ref, held_3_ref, strip_held_ref,
    moved_ref, moved_strip_ref, cells_ref, ghosts_ref,
    flux_ref, part_ref, emf_ref, cell_ref, side_ref,
    in_sem, rows_sem, strips_sem, back_sem, ghosts_back_sem, held_sem, strip_held_sem, row_sem, ghosts_sem,
    hand_sem, handed_sem,
):
    x, y_hi, z, y_lo, core = place()
    az, rad = lax.axis_index("az"), lax.axis_index("rad")
    parity = (x + y_hi + z) % 2
    group = (1 - y_lo) * 2 + parity
    index = core * 16 + az // 2
    piece, first_row = index // 8, index % 8
    held_refs = (held_0_ref, held_1_ref, held_2_ref, held_3_ref)
    among = index % 16
    for_inner = jnp.logical_and(jnp.logical_and(group == 0, core == 0), among % 4 < 2)
    for_outer = jnp.logical_and(
        jnp.logical_and(group == 3, core == 1), jnp.logical_or(among % 4 < 2, among == 2)
    )
    has_ghost = jnp.logical_or(for_inner, for_outer)
    ghost = jnp.where(among == 2, 16, among // 4 * 2 + among % 4 + jnp.where(for_outer, 8, 0))

    loads = [
        pltpu.make_async_copy(source, target, in_sem.at[n])
        for n, (source, target) in enumerate(
            ((state_hbm, state_ref), (shift_hbm, shift_ref), (frac_hbm, frac_ref))
        )
    ]
    for load in loads:
        load.start()

    barrier = pltpu.get_barrier_semaphore()

    def greet(target_az, target_rad):
        pl.semaphore_signal(
            barrier, inc=1, device_id={"az": target_az, "rad": target_rad}, device_id_type=MESH
        )

    for d in range(RING):
        greet(d, group)

    @pl.when(rad > 0)
    def _():
        greet(az, rad - 1)

    @pl.when(rad < 3)
    def _():
        greet(az, rad + 1)

    @pl.when(has_ghost)
    def _():
        for d in range(RING):
            greet(d, 3 - group)

    for load in loads:
        load.wait()

    def field_lines(field, row):
        eighth, rest = row if isinstance(row, tuple) else (row // 8, row % 8)
        return state_ref[pl.ds(field * 256 + eighth * 64 + rest, 8, stride=8), :]

    pl.semaphore_wait(barrier, RING + jnp.where(rad == 0, 10, jnp.where(rad == 3, 9, 2)))

    my_lines = pl.ds(pl.multiple_of(az * 8, 8), 8)

    def send_strips(ghosts):
        for n in ghosts:
            r, field = ghost_source(n)
            strips_ref[n] = field_lines(field, r)
            pltpu.make_async_remote_copy(
                src_ref=strips_ref.at[n],
                dst_ref=strip_held_ref.at[my_lines],
                send_sem=strips_sem,
                recv_sem=strip_held_sem,
                device_id=ghost_holder(n),
                device_id_type=MESH,
            ).start()

    pl.when(rad == 3)(lambda: send_strips(range(8)))
    pl.when(rad == 0)(lambda: send_strips(range(8, GHOSTS)))
    offset_parity = (core + parity) % 2

    def send_out(part):
        def some(j, carry):
            sends = []
            for m in range(GROUPED):
                k = j * GROUPED + m
                side, i = k // 16, k % 16
                dx, dz = i % 4, (i // 4 + i) % 4
                dy = (offset_parity + dx + dz) % 2
                target = ((x + dx) % 4) * 8 + ((y_hi + dy) % 2) * 4 + (z + dz) % 4
                to_piece, first = side * 2 + target // 16, target // 2 % 8
                row = row_of(part, first)
                for f in range(HELD):
                    rows_ref[to_piece, first, part, f] = field_lines(to_piece * HELD + f, row)
                sends.append(
                    pltpu.make_async_remote_copy(
                        src_ref=rows_ref.at[to_piece, first, part],
                        dst_ref=held_refs[part].at[:, my_lines],
                        send_sem=rows_sem,
                        recv_sem=held_sem.at[part],
                        device_id={"az": target, "rad": (1 - y_lo) * 2 + side},
                        device_id_type=MESH,
                    )
                )
            for send in sends:
                send.start()
            return carry

        lax.fori_loop(0, RING // GROUPED, some, 0)

    for part in range(PARTS):
        send_out(part)

    def same_size(ref, send_sem, recv_sem):
        return pltpu.make_async_remote_copy(
            src_ref=ref, dst_ref=ref, send_sem=send_sem, recv_sem=recv_sem,
            device_id={"az": az, "rad": (rad + 2) % 4}, device_id_type=MESH,
        )

    lane = lax.broadcasted_iota(jnp.int32, (8, TILE), 1)

    def taps_of(cells, weights):
        taps = []
        for n, weight in enumerate(weights):
            part = ((cells + n) % 4) * NZ
            halo = (lane + part) % TILE < TILE - NZ
            taps.append((1 - (cells % 4 + n) // 4, part, lane < TILE - part, halo, weight))
        return cells // 4, taps

    def blend(taps, tile_lines, halo_lines, fields):
        inner, outer = [None] * fields, None
        for start, part, here, halo, weight in taps:
            for f in range(fields):
                both = jnp.where(here, tile_lines(f, start + 2), tile_lines(f, start + 1))
                term = weight * pltpu.roll(both, part, 1)
                inner[f] = term if inner[f] is None else inner[f] + term
            after = jnp.where(here, halo_lines(start + 10), halo_lines(start + 9))
            before = jnp.where(here, halo_lines(start + 1), halo_lines(start))
            term = weight * pltpu.roll(jnp.where(halo, after, before), part, 1)
            outer = term if outer is None else outer + term
        return inner, outer

    middle = jnp.logical_and(lane >= NZ, lane < TILE - NZ)
    odd = lax.broadcasted_iota(jnp.int32, (8, TILE), 0) % 2 == 1

    def ghost_taps():
        source_row = jnp.where(for_inner, ROWS * 4 - 1, ghost // 16)
        shift, fraction = shift_ref[source_row], frac_ref[source_row]
        edge_shift, edge_frac = edge_shift_ref[0], edge_frac_ref[0]
        more = jnp.where(for_inner, edge_shift, RING * COLUMNS // NZ - 1 - edge_shift)
        edge = jnp.where(for_inner, edge_frac, 1.0 - edge_frac)
        return taps_of(
            lax.rem(shift + more, RING * COLUMNS // NZ),
            (
                (1.0 - edge) * (1.0 - fraction),
                (1.0 - edge) * fraction + edge * (1.0 - fraction),
                edge * fraction,
            ),
        )

    def target(k):
        dx, dz, dy = k % 4, (k // 4 + k) % 4, (k // 16 + k) % 2
        return ((x + dx) % 4) * 8 + ((y_hi + dy) % 2) * 4 + (z + dz) % 4

    def first_tile(d, whole):
        return lax.rem(8 * d + 2 * TILES - 3 - whole, TILES)

    def send_back(part):
        held_ref = held_refs[part]
        same_size(held_ref.at[:, :TILES], rows_sem, held_sem.at[part]).wait_recv()
        for f in range(HELD):
            held_ref[f, TILES:] = held_ref[f, :PAD]
        eighth, rest = row_of(part, first_row)
        r = group * ROWS + eighth * 8 + rest
        shift, fraction = shift_ref[r], frac_ref[r]
        whole, taps = taps_of(shift, (1.0 - fraction, fraction))

        def fill(d):
            base = first_tile(d, whole)

            def halo_lines(n):
                pair = [
                    jnp.broadcast_to(held_ref[f, pl.ds(base + n, 1), :], (8, TILE))
                    for f in range(HELD)
                ]
                return jnp.where(odd, pair[1], pair[0])

            inner, outer = blend(
                taps, lambda f, n: held_ref[f, pl.ds(base + n, 8), :], halo_lines, HELD
            )
            for f in range(HELD):
                moved_ref[part, d, f * 8 : f * 8 + 8] = inner[f]
            second = share(lane, pltpu.roll(outer, 1, 0))
            shared = jnp.where(jnp.logical_and(middle, piece != B_PIECE), second, outer)
            moved_ref[part, d, HELD * 8 :] = shared

        def some(j, carry):
            ds = [target(j * GROUPED + m) for m in range(GROUPED)]
            for d in ds:
                fill(d)

            def send(size):
                for d in ds:
                    pltpu.make_async_remote_copy(
                        src_ref=moved_ref.at[part, d, :size],
                        dst_ref=cells_ref.at[eighth + 1, rest, pl.ds(piece * LINES, size)],
                        send_sem=back_sem,
                        recv_sem=row_sem.at[part],
                        device_id={"az": d, "rad": group},
                        device_id_type=MESH,
                    ).start()

            pl.when(piece == B_PIECE)(lambda: send(WINDOW))
            pl.when(piece != B_PIECE)(lambda: send(SHORT))
            return carry

        lax.fori_loop(0, RING // GROUPED, some, 0)

    def send_ghosts():
        same_size(strip_held_ref.at[:TILES], strips_sem, strip_held_sem).wait_recv()
        strip_held_ref[TILES:, :] = strip_held_ref[:PAD, :]
        whole, taps = ghost_taps()

        def fill(d):
            base = first_tile(d, whole)
            lines = lambda n: strip_held_ref[pl.ds(base + n, 8), :]
            inner, outer = blend(taps, lambda f, n: lines(n), lines, 1)
            moved_strip_ref[d, 0:8] = inner[0]
            moved_strip_ref[d, 8:16] = outer

        def some(j, carry):
            ds = [target(j * GROUPED + m) for m in range(GROUPED)]
            for d in ds:
                fill(d)
            for d in ds:
                pltpu.make_async_remote_copy(
                    src_ref=moved_strip_ref.at[d, :9],
                    dst_ref=ghosts_ref.at[pl.ds(pl.multiple_of(ghost * 16, 16), 9)],
                    send_sem=ghosts_back_sem,
                    recv_sem=ghosts_sem,
                    device_id={"az": d, "rad": group},
                    device_id_type=MESH,
                ).start()
            return carry

        lax.fori_loop(0, RING // GROUPED, some, 0)

    for part in range(PARTS):
        send_back(part)
        if part == 0:
            pl.when(has_ghost)(send_ghosts)

    lines_ref = cells_ref.reshape(SLOTS[0] * SLOTS[1] * ROW_LINES, TILE)

    def arrived(part):
        lines = 8 * (3 * SHORT + WINDOW)
        same_size(lines_ref.at[:lines], back_sem, row_sem.at[part]).wait_recv()

    def hand(source, slot, n, neighbour):
        return pltpu.make_async_remote_copy(
            src_ref=source,
            dst_ref=slot,
            send_sem=hand_sem.at[n],
            recv_sem=handed_sem.at[n],
            device_id={"az": az, "rad": neighbour},
            device_id_type=MESH,
        )

    outer, inner = (rad + 1) % 4, (rad + 3) % 4
    windows = [
        pl.ds(n * LINES, WINDOW if n == B_PIECE else SHORT) for n in range(PIECES)
    ]
    to_outer = [
        hand(cells_ref.at[4, 7, window], cells_ref.at[0, 7, window], n, outer)
        for n, window in enumerate(windows)
    ]
    to_inner = [
        hand(cells_ref.at[1, 0, window], cells_ref.at[5, 0, window], PIECES + n, inner)
        for n, window in enumerate(windows)
    ]
    faces = pl.ds(B_PIECE * LINES, SHORT)
    to_inner.append(hand(cells_ref.at[1, 1, faces], cells_ref.at[5, 1, faces], 2 * PIECES, inner))
    arrived(0)

    @pl.when(rad < 3)
    def _():
        for copy in to_outer:
            copy.start()

    @pl.when(rad > 0)
    def _():
        for copy in to_inner:
            copy.start()

    def take_ghosts(ghosts):
        same_size(ghosts_ref.at[: len(ghosts) * 9], ghosts_back_sem, ghosts_sem).wait_recv()
        for n in ghosts:
            row, field = (-1, n) if n < 8 else (ROWS, n - 8) if n < 16 else (ROWS + 1, 4)
            first = (row + 8) * ROW_LINES + field // HELD * LINES
            at, ninth = first + field % HELD * 8, first + HELD * 8 + field % HELD
            lines_ref[at : at + 8, :] = ghosts_ref[n * 16 : n * 16 + 8]
            line = ghosts_ref[n * 16 + 8 : n * 16 + 9]
            if field // HELD == B_PIECE:
                lines_ref[ninth : ninth + 1, :] = line
            elif field % HELD == 0:
                second = jnp.broadcast_to(ghosts_ref[n * 16 + 24 : n * 16 + 25], (8, TILE))
                both = jnp.where(middle, share(lane, second), jnp.broadcast_to(line, (8, TILE)))
                lines_ref[ninth : ninth + 1, :] = both[:1]

    def received(copies):
        for copy in copies:
            copy.wait_recv()

    before_first, step = stepper(lines_ref, out_ref, flux_ref, part_ref, emf_ref, cell_ref, side_ref)

    def one(block, carry):
        @pl.when(block == 0)
        def _():
            arrived(1)
            pl.when(rad > 0)(lambda: received(to_outer))
            pl.when(rad == 0)(lambda: take_ghosts(range(8)))
            before_first()

        pl.when(block == 1)(lambda: arrived(2))

        @pl.when(block == 2)
        def _():
            arrived(3)
            pl.when(rad < 3)(lambda: received(to_inner))
            pl.when(rad == 3)(lambda: take_ghosts(range(8, GHOSTS)))

        step(block)
        return carry

    lax.fori_loop(0, ROWS // 8, one, 0)

    same_size(rows_ref, rows_sem, held_sem.at[0]).wait_send()
    for size, sent in ((WINDOW, piece == B_PIECE), (SHORT, piece != B_PIECE)):
        whole = same_size(moved_ref.at[:, :, :size], back_sem, held_sem.at[0])
        pl.when(sent)(whole.wait_send)

    @pl.when(rad == 3)
    def _():
        same_size(strips_ref.at[:8], strips_sem, held_sem.at[0]).wait_send()

    @pl.when(rad == 0)
    def _():
        same_size(strips_ref.at[8:GHOSTS], strips_sem, held_sem.at[0]).wait_send()

    @pl.when(has_ghost)
    def _():
        same_size(moved_strip_ref.at[:, :9], ghosts_back_sem, held_sem.at[0]).wait_send()

    @pl.when(rad < 3)
    def _():
        for copy in to_outer:
            copy.wait_send()

    @pl.when(rad > 0)
    def _():
        for copy in to_inner:
            copy.wait_send()


def side(cell, normal, face):
    density, momenta, magnetic, tracer, inverse = cell
    field = list(magnetic)
    field[normal] = face
    square = field[0] * field[0] + field[1] * field[1] + field[2] * field[2]
    speed = momenta[normal] * inverse
    flux = [momenta[normal]]
    for n in range(3):
        term = momenta[n] * speed - face * field[n]
        if n == normal:
            term = term + (density + 0.5 * square)
        flux.append(term)
    flux.append(tracer * speed)
    reach = 1.0 + square * inverse
    return flux, jnp.abs(speed) + reach * lax.rsqrt(reach)


def face_flux(before, cell, normal, face):
    left, left_signal = side(before, normal, face)
    right, right_signal = side(cell, normal, face)
    bound = jnp.maximum(left_signal, right_signal)
    left_state = [before[0], *before[1], before[3]]
    right_state = [cell[0], *cell[1], cell[3]]
    return [
        (left[n] + right[n]) - bound * (right_state[n] - left_state[n]) for n in range(5)
    ]


def stepper(cells_ref, out_ref, flux_ref, part_ref, emf_ref, cell_ref, side_ref):
    lane = lax.broadcasted_iota(jnp.int32, (8, TILE), 1)
    level = lane % NZ
    up = jnp.where(level == NZ - 1, lane - (NZ - 1), lane + 1)
    down = jnp.where(level == 0, lane + (NZ - 1), lane - 1)

    def load(field, row, tile):
        line = field % HELD * 8 + tile if tile < 8 else HELD * 8 + field % HELD
        first = (row + 8) * ROW_LINES + field // HELD * LINES + line
        return cells_ref[pl.ds(first, 8, stride=ROW_LINES), :]

    def plus_z(v):
        return jnp.take_along_axis(v, up, axis=1, mode="promise_in_bounds")

    def minus_z(v):
        return jnp.take_along_axis(v, down, axis=1, mode="promise_in_bounds")

    def minus_y(before, v):
        return pltpu.roll(jnp.where(lane >= TILE - NZ, before, v), NZ, 1)

    def plus_y(v, after):
        return pltpu.roll(jnp.where(lane < NZ, after, v), TILE - NZ, 1)

    def lines_of(row):
        return pl.ds(pl.multiple_of(row + 16, 8), 8)

    def part_lines(row):
        for piece in range(PIECES):
            if piece != B_PIECE:
                first = (row + 8) * ROW_LINES + piece * LINES + HELD * 8
                both = cells_ref[pl.ds(first, 8, stride=ROW_LINES), :]
                at = jnp.where(lane < NZ, lane + NZ, jnp.where(lane < TILE - NZ, lane, lane - NZ))
                second = jnp.take_along_axis(both, at, axis=1, mode="promise_in_bounds")
                cells_ref[pl.ds(first + 1, 8, stride=ROW_LINES), :] = second

    def work_out(row):
        part_lines(row + 1)
        for tile in range(9):
            density = load(0, row + 1, tile)
            faces = [load(n, row + 1, tile) for n in (4, 5, 6)]
            c = [
                0.5 * (faces[0] + load(4, row + 2, tile)),
                0.5 * (faces[1] + plus_y(faces[1], load(5, row + 1, (tile + 1) % 9))),
                0.5 * (faces[2] + plus_z(faces[2])),
            ]
            inverse = 1.0 / density
            v = [load(n, row + 1, tile) * inverse for n in (1, 2, 3)]
            emf = [v[2] * c[1] - v[1] * c[2], v[0] * c[2] - v[2] * c[0], v[1] * c[0] - v[0] * c[1]]
            for n, value in enumerate([*c, inverse, *emf]):
                cell_ref[tile, n, lines_of(row), :] = value

    def known(n, row, tile):
        return cell_ref[tile, n, pl.ds(row + 15, 8), :]

    def cell_at(row, tile):
        return (
            load(0, row, tile),
            [load(n, row, tile) for n in (1, 2, 3)],
            [known(n, row, tile) for n in (0, 1, 2)],
            load(7, row, tile),
            known(3, row, tile),
        )

    def outer_flux(row, tile, cell):
        flux = face_flux(cell, cell_at(row + 1, tile), 0, load(4, row + 1, tile))
        for n in range(5):
            side_ref[tile, n, lines_of(row), :] = flux[n]
        return flux

    def before_first():
        work_out(-8)
        for tile in range(8):
            outer_flux(-8, tile, cell_at(-8, tile))

    def first(row, tile):
        before = (tile + 8) % 9
        cell = cell_at(row, tile)
        density, momenta, centred, tracer, inverse = cell
        faces = [load(n, row, tile) for n in (4, 5, 6)]

        def behind_of(field):
            return minus_y(load(field, row, before), load(field, row, tile))

        behind_density = behind_of(0)
        behind = (
            behind_density,
            [behind_of(n) for n in (1, 2, 3)],
            [minus_y(known(0, row, before), centred[0]), None, minus_y(known(2, row, before), centred[2])],
            behind_of(7),
            1.0 / behind_density,
        )
        flux_y = face_flux(behind, cell, 1, faces[1])
        for n in range(5):
            flux_ref[tile, n] = flux_y[n]

        emf_x, z_here = known(4, row, tile), known(6, row, tile)
        z_lower, z_upper = known(6, row - 1, tile), known(6, row + 1, tile)
        x_below = minus_z(emf_x)
        emf_ref[tile, 0] = z_here + z_lower
        emf_ref[tile, 1] = (plus_z(emf_x) - x_below) - (z_upper - z_lower)
        emf_ref[tile, 2] = emf_x + x_below
        if tile == 8:
            return
        y_here, y_lower, y_upper = known(5, row, tile), known(5, row - 1, tile), known(5, row + 1, tile)
        y_pair, y_across = y_here + y_lower, y_upper - y_lower
        part_ref[tile, 5] = faces[0] + 0.25 * TIME_STEP * (plus_z(y_pair) - minus_z(y_pair))
        part_ref[tile, 6] = faces[1]
        part_ref[tile, 7] = faces[2] - 0.25 * TIME_STEP * (y_across + minus_z(y_across))

        flux_high = outer_flux(row, tile, cell)
        flux_low = [side_ref[tile, n, pl.ds(row + 15, 8), :] for n in range(5)]
        below = (
            minus_z(density),
            [minus_z(m) for m in momenta],
            [minus_z(centred[0]), minus_z(centred[1]), None],
            minus_z(tracer),
            minus_z(inverse),
        )
        flux_z = face_flux(below, cell, 2, faces[2])
        state = [density, *momenta, tracer]
        for n in range(5):
            change = (flux_high[n] - flux_low[n]) + (plus_z(flux_z[n]) - flux_z[n])
            value = state[n] - 0.5 * TIME_STEP * change
            if n == 1:
                value = value + TIME_STEP * 2.0 * momenta[1]
            if n == 2:
                value = value - TIME_STEP * 0.5 * momenta[0]
            part_ref[tile, n] = value

    def last(row, tile):
        before, after = (tile + 8) % 9, tile + 1
        rows, columns = pl.ds(row, 8), pl.ds(tile * TILE, TILE)
        for n, field in enumerate((0, 1, 2, 3, 7)):
            flux = flux_ref[tile, n]
            out_ref[field, rows, columns] = part_ref[tile, n] - 0.5 * TIME_STEP * (
                plus_y(flux, flux_ref[after, n]) - flux
            )
        around = [(emf_ref[before, n], emf_ref[tile, n], emf_ref[after, n]) for n in range(3)]
        across_z = plus_y(around[0][1], around[0][2]) - minus_y(around[0][0], around[0][1])
        pair = around[1][1] + minus_y(around[1][0], around[1][1])
        across_x = plus_y(around[2][1], around[2][2]) - minus_y(around[2][0], around[2][1])
        out_ref[4, rows, columns] = part_ref[tile, 5] - 0.25 * TIME_STEP * across_z
        out_ref[5, rows, columns] = part_ref[tile, 6] - 0.25 * TIME_STEP * pair
        out_ref[6, rows, columns] = part_ref[tile, 7] + 0.25 * TIME_STEP * across_x

    def step(block):
        row = pl.multiple_of(block * 8, 8)
        work_out(row)
        for tile in range(9):
            first(row, tile)
        for tile in range(8):
            last(row, tile)

    return before_first, step


def per_device(state, row_shift, row_frac, edge_shift, edge_frac):
    tiles = state.reshape(FIELDS, ROWS // 8, 8, COLUMNS // TILE, TILE).transpose(0, 1, 3, 2, 4)
    tiles = tiles.reshape(FIELDS * ROWS * 8, TILE)
    dma, smem = pltpu.SemaphoreType.DMA, pltpu.SMEM

    def vmem(*shape):
        return pltpu.VMEM(shape, jnp.float32)

    return pl.pallas_call(
        kernel,
        out_shape=jax.ShapeDtypeStruct((FIELDS, ROWS, COLUMNS), jnp.float32),
        in_specs=[pl.BlockSpec(memory_space=pltpu.HBM)] * 3 + [pl.BlockSpec(memory_space=pltpu.SMEM)] * 2,
        out_specs=pl.BlockSpec(memory_space=pltpu.VMEM),
        scratch_shapes=[
            vmem(*tiles.shape),
            smem(row_shift.shape, jnp.int32), smem(row_frac.shape, jnp.float32),
            vmem(PIECES, 8, PARTS, HELD, 8, TILE),
            vmem(GHOSTS, 8, TILE),
            *[vmem(HELD, TILES + PAD, TILE)] * PARTS,
            vmem(TILES + PAD, TILE),
            vmem(PARTS, RING, LINES, TILE),
            vmem(RING, 16, TILE),
            vmem(*SLOTS, ROW_LINES, TILE),
            vmem(GHOSTS * 16, TILE),
            vmem(9, 5, 8, TILE), vmem(9, 8, 8, TILE), vmem(9, 3, 8, TILE),
            vmem(9, 7, 48, TILE), vmem(8, 5, 48, TILE),
            dma((3,)), dma, dma, dma, dma, dma((PARTS,)), dma, dma((PARTS,)), dma, dma((9,)), dma((9,)),
        ],
        compiler_params=pltpu.CompilerParams(
            collective_id=0, has_side_effects=True, vmem_limit_bytes=VMEM_LIMIT
        ),
        name="step",
    )(
        *[pltpu.with_memory_space_constraint(a, pltpu.HBM) for a in (tiles, row_shift, row_frac)],
        edge_shift,
        edge_frac,
    )


def solution(mesh):
    return jax.shard_map(
        per_device,
        mesh=mesh,
        in_specs=(P(None, "rad", "az"), P(), P(), P(), P()),
        out_specs=P(None, "rad", "az"),
        check_vma=False,
    )
```

```python
import jax
import jax.numpy as jnp
from jax import lax
from jax.experimental import pallas as pl
from jax.experimental.pallas import tpu as pltpu
from jax.sharding import PartitionSpec as P

MESH = pl.DeviceIdType.MESH
NZ = 32
FIELDS = 8
HELD = 2
PIECES = 4
PARTS = 4
GROUPED = 4
ROWS = 32
COLUMNS = 1024
RING = 32
TILE = 128
TILES = RING * COLUMNS // TILE
PAD = 24
WINDOW = 18
SHORT = 17
LINES = 24
ROW_LINES = 104
SLOTS = (6, 8)
B_PIECE = 2
GHOSTS = 17
VMEM_LIMIT = 28 * 2**20
TIME_STEP = 0.2


def share(lane, v):
    at = jnp.where(lane < TILE // 2, lane - NZ, lane + NZ)
    middle = jnp.logical_and(lane >= NZ, lane < TILE - NZ)
    return jnp.take_along_axis(v, jnp.where(middle, at, lane), axis=1, mode="promise_in_bounds")


def place():
    az, rad = lax.axis_index("az"), lax.axis_index("rad")
    return az // 8, (az // 4) % 2, az % 4, rad // 2, rad % 2


def row_of(part, first):
    last = first == 7
    if part == 0:
        return jnp.where(last, 3, 0), first
    return part - jnp.where(last, 1, 0), first


def ghost_holder(n):
    i = 2 if n == 16 else n % 8 // 2 * 4 + n % 2
    group = 0 if n < 8 else 3
    low = (group % 2 + i // 4 + (i // 2) % 2) % 2
    return {"az": 2 * i + low, "rad": 2 if n < 8 else 1}


def ghost_source(n):
    if n < 8:
        return ROWS - 1, n
    if n < 16:
        return 0, n - 8
    return 1, 4


def kernel(
    state_hbm, shift_hbm, frac_hbm, edge_shift_ref, edge_frac_ref,
    out_ref,
    state_ref, shift_ref, frac_ref,
    rows_ref, strips_ref, held_0_ref, held_1_ref, held_2_ref, held_3_ref, strip_held_ref,
    moved_ref, moved_strip_ref, cells_ref, ghosts_ref,
    flux_ref, part_ref, emf_ref, cell_ref, side_ref,
    in_sem, rows_sem, strips_sem, back_sem, ghosts_back_sem, held_sem, strip_held_sem, row_sem, ghosts_sem,
    hand_sem, handed_sem,
):
    x, y_hi, z, y_lo, core = place()
    az, rad = lax.axis_index("az"), lax.axis_index("rad")
    parity = (x + y_hi + z) % 2
    group = (1 - y_lo) * 2 + parity
    index = core * 16 + az // 2
    piece, first_row = index // 8, index % 8
    held_refs = (held_0_ref, held_1_ref, held_2_ref, held_3_ref)
    among = index % 16
    for_inner = jnp.logical_and(jnp.logical_and(group == 0, core == 0), among % 4 < 2)
    for_outer = jnp.logical_and(
        jnp.logical_and(group == 3, core == 1), jnp.logical_or(among % 4 < 2, among == 2)
    )
    has_ghost = jnp.logical_or(for_inner, for_outer)
    ghost = jnp.where(among == 2, 16, among // 4 * 2 + among % 4 + jnp.where(for_outer, 8, 0))

    loads = [
        pltpu.make_async_copy(source, target, in_sem.at[n])
        for n, (source, target) in enumerate(
            ((state_hbm, state_ref), (shift_hbm, shift_ref), (frac_hbm, frac_ref))
        )
    ]
    for load in loads:
        load.start()

    barrier = pltpu.get_barrier_semaphore()

    def greet(target_az, target_rad):
        pl.semaphore_signal(
            barrier, inc=1, device_id={"az": target_az, "rad": target_rad}, device_id_type=MESH
        )

    for d in range(RING):
        greet(d, group)

    @pl.when(rad > 0)
    def _():
        greet(az, rad - 1)

    @pl.when(rad < 3)
    def _():
        greet(az, rad + 1)

    @pl.when(has_ghost)
    def _():
        for d in range(RING):
            greet(d, 3 - group)

    for load in loads:
        load.wait()

    def field_lines(field, row):
        eighth, rest = row if isinstance(row, tuple) else (row // 8, row % 8)
        return state_ref[pl.ds(field * 256 + eighth * 64 + rest, 8, stride=8), :]

    pl.semaphore_wait(barrier, RING + jnp.where(rad == 0, 10, jnp.where(rad == 3, 9, 2)))

    my_lines = pl.ds(pl.multiple_of(az * 8, 8), 8)

    def send_strips(ghosts):
        for n in ghosts:
            r, field = ghost_source(n)
            strips_ref[n] = field_lines(field, r)
            pltpu.make_async_remote_copy(
                src_ref=strips_ref.at[n],
                dst_ref=strip_held_ref.at[my_lines],
                send_sem=strips_sem,
                recv_sem=strip_held_sem,
                device_id=ghost_holder(n),
                device_id_type=MESH,
            ).start()

    pl.when(rad == 3)(lambda: send_strips(range(8)))
    pl.when(rad == 0)(lambda: send_strips(range(8, GHOSTS)))
    offset_parity = (core + parity) % 2

    def send_out(part):
        def some(j, carry):
            sends = []
            for m in range(GROUPED):
                k = j * GROUPED + m
                side, i = k // 16, k % 16
                dx, dz = i % 4, (i // 4 + i) % 4
                dy = (offset_parity + dx + dz) % 2
                target = ((x + dx) % 4) * 8 + ((y_hi + dy) % 2) * 4 + (z + dz) % 4
                to_piece, first = side * 2 + target // 16, target // 2 % 8
                row = row_of(part, first)
                for f in range(HELD):
                    rows_ref[to_piece, first, part, f] = field_lines(to_piece * HELD + f, row)
                sends.append(
                    pltpu.make_async_remote_copy(
                        src_ref=rows_ref.at[to_piece, first, part],
                        dst_ref=held_refs[part].at[:, my_lines],
                        send_sem=rows_sem,
                        recv_sem=held_sem.at[part],
                        device_id={"az": target, "rad": (1 - y_lo) * 2 + side},
                        device_id_type=MESH,
                    )
                )
            for send in sends:
                send.start()
            return carry

        lax.fori_loop(0, RING // GROUPED, some, 0)

    for part in range(PARTS):
        send_out(part)

    def same_size(ref, send_sem, recv_sem):
        return pltpu.make_async_remote_copy(
            src_ref=ref, dst_ref=ref, send_sem=send_sem, recv_sem=recv_sem,
            device_id={"az": az, "rad": (rad + 2) % 4}, device_id_type=MESH,
        )

    lane = lax.broadcasted_iota(jnp.int32, (8, TILE), 1)

    def taps_of(cells, weights):
        taps = []
        for n, weight in enumerate(weights):
            part = ((cells + n) % 4) * NZ
            halo = (lane + part) % TILE < TILE - NZ
            taps.append((1 - (cells % 4 + n) // 4, part, lane < TILE - part, halo, weight))
        return cells // 4, taps

    def blend(taps, tile_lines, halo_lines, fields):
        inner, outer = [None] * fields, None
        for start, part, here, halo, weight in taps:
            for f in range(fields):
                both = jnp.where(here, tile_lines(f, start + 2), tile_lines(f, start + 1))
                term = weight * pltpu.roll(both, part, 1)
                inner[f] = term if inner[f] is None else inner[f] + term
            after = jnp.where(here, halo_lines(start + 10), halo_lines(start + 9))
            before = jnp.where(here, halo_lines(start + 1), halo_lines(start))
            term = weight * pltpu.roll(jnp.where(halo, after, before), part, 1)
            outer = term if outer is None else outer + term
        return inner, outer

    middle = jnp.logical_and(lane >= NZ, lane < TILE - NZ)
    odd = lax.broadcasted_iota(jnp.int32, (8, TILE), 0) % 2 == 1

    def ghost_taps():
        source_row = jnp.where(for_inner, ROWS * 4 - 1, ghost // 16)
        shift, fraction = shift_ref[source_row], frac_ref[source_row]
        edge_shift, edge_frac = edge_shift_ref[0], edge_frac_ref[0]
        more = jnp.where(for_inner, edge_shift, RING * COLUMNS // NZ - 1 - edge_shift)
        edge = jnp.where(for_inner, edge_frac, 1.0 - edge_frac)
        return taps_of(
            lax.rem(shift + more, RING * COLUMNS // NZ),
            (
                (1.0 - edge) * (1.0 - fraction),
                (1.0 - edge) * fraction + edge * (1.0 - fraction),
                edge * fraction,
            ),
        )

    def target(k):
        dx, dz, dy = k % 4, (k // 4 + k) % 4, (k // 16 + k) % 2
        return ((x + dx) % 4) * 8 + ((y_hi + dy) % 2) * 4 + (z + dz) % 4

    def first_tile(d, whole):
        return lax.rem(8 * d + 2 * TILES - 3 - whole, TILES)

    def send_back(part):
        held_ref = held_refs[part]
        same_size(held_ref.at[:, :TILES], rows_sem, held_sem.at[part]).wait_recv()
        for f in range(HELD):
            held_ref[f, TILES:] = held_ref[f, :PAD]
        eighth, rest = row_of(part, first_row)
        r = group * ROWS + eighth * 8 + rest
        shift, fraction = shift_ref[r], frac_ref[r]
        whole, taps = taps_of(shift, (1.0 - fraction, fraction))

        def fill(d):
            base = first_tile(d, whole)

            def halo_lines(n):
                pair = [
                    jnp.broadcast_to(held_ref[f, pl.ds(base + n, 1), :], (8, TILE))
                    for f in range(HELD)
                ]
                return jnp.where(odd, pair[1], pair[0])

            inner, outer = blend(
                taps, lambda f, n: held_ref[f, pl.ds(base + n, 8), :], halo_lines, HELD
            )
            for f in range(HELD):
                moved_ref[part, d, f * 8 : f * 8 + 8] = inner[f]
            second = share(lane, pltpu.roll(outer, 1, 0))
            shared = jnp.where(jnp.logical_and(middle, piece != B_PIECE), second, outer)
            moved_ref[part, d, HELD * 8 :] = shared

        def some(j, carry):
            ds = [target(j * GROUPED + m) for m in range(GROUPED)]
            for d in ds:
                fill(d)

            def send(size):
                for d in ds:
                    pltpu.make_async_remote_copy(
                        src_ref=moved_ref.at[part, d, :size],
                        dst_ref=cells_ref.at[eighth + 1, rest, pl.ds(piece * LINES, size)],
                        send_sem=back_sem,
                        recv_sem=row_sem.at[part],
                        device_id={"az": d, "rad": group},
                        device_id_type=MESH,
                    ).start()

            pl.when(piece == B_PIECE)(lambda: send(WINDOW))
            pl.when(piece != B_PIECE)(lambda: send(SHORT))
            return carry

        lax.fori_loop(0, RING // GROUPED, some, 0)

    def send_ghosts():
        same_size(strip_held_ref.at[:TILES], strips_sem, strip_held_sem).wait_recv()
        strip_held_ref[TILES:, :] = strip_held_ref[:PAD, :]
        whole, taps = ghost_taps()

        def fill(d):
            base = first_tile(d, whole)
            lines = lambda n: strip_held_ref[pl.ds(base + n, 8), :]
            inner, outer = blend(taps, lambda f, n: lines(n), lines, 1)
            moved_strip_ref[d, 0:8] = inner[0]
            moved_strip_ref[d, 8:16] = outer

        def some(j, carry):
            ds = [target(j * GROUPED + m) for m in range(GROUPED)]
            for d in ds:
                fill(d)
            for d in ds:
                pltpu.make_async_remote_copy(
                    src_ref=moved_strip_ref.at[d, :9],
                    dst_ref=ghosts_ref.at[pl.ds(pl.multiple_of(ghost * 16, 16), 9)],
                    send_sem=ghosts_back_sem,
                    recv_sem=ghosts_sem,
                    device_id={"az": d, "rad": group},
                    device_id_type=MESH,
                ).start()
            return carry

        lax.fori_loop(0, RING // GROUPED, some, 0)

    for part in range(PARTS):
        send_back(part)
        if part == 0:
            pl.when(has_ghost)(send_ghosts)

    lines_ref = cells_ref.reshape(SLOTS[0] * SLOTS[1] * ROW_LINES, TILE)

    def arrived(part):
        lines = 8 * (3 * SHORT + WINDOW)
        same_size(lines_ref.at[:lines], back_sem, row_sem.at[part]).wait_recv()

    def hand(source, slot, n, neighbour):
        return pltpu.make_async_remote_copy(
            src_ref=source,
            dst_ref=slot,
            send_sem=hand_sem.at[n],
            recv_sem=handed_sem.at[n],
            device_id={"az": az, "rad": neighbour},
            device_id_type=MESH,
        )

    outer, inner = (rad + 1) % 4, (rad + 3) % 4
    windows = [
        pl.ds(n * LINES, WINDOW if n == B_PIECE else SHORT) for n in range(PIECES)
    ]
    to_outer = [
        hand(cells_ref.at[4, 7, window], cells_ref.at[0, 7, window], n, outer)
        for n, window in enumerate(windows)
    ]
    to_inner = [
        hand(cells_ref.at[1, 0, window], cells_ref.at[5, 0, window], PIECES + n, inner)
        for n, window in enumerate(windows)
    ]
    faces = pl.ds(B_PIECE * LINES, SHORT)
    to_inner.append(hand(cells_ref.at[1, 1, faces], cells_ref.at[5, 1, faces], 2 * PIECES, inner))
    arrived(0)

    @pl.when(rad < 3)
    def _():
        for copy in to_outer:
            copy.start()

    @pl.when(rad > 0)
    def _():
        for copy in to_inner:
            copy.start()

    def take_ghosts(ghosts):
        same_size(ghosts_ref.at[: len(ghosts) * 9], ghosts_back_sem, ghosts_sem).wait_recv()
        for n in ghosts:
            row, field = (-1, n) if n < 8 else (ROWS, n - 8) if n < 16 else (ROWS + 1, 4)
            first = (row + 8) * ROW_LINES + field // HELD * LINES
            at, ninth = first + field % HELD * 8, first + HELD * 8 + field % HELD
            lines_ref[at : at + 8, :] = ghosts_ref[n * 16 : n * 16 + 8]
            line = ghosts_ref[n * 16 + 8 : n * 16 + 9]
            if field // HELD == B_PIECE:
                lines_ref[ninth : ninth + 1, :] = line
            elif field % HELD == 0:
                second = jnp.broadcast_to(ghosts_ref[n * 16 + 24 : n * 16 + 25], (8, TILE))
                both = jnp.where(middle, share(lane, second), jnp.broadcast_to(line, (8, TILE)))
                lines_ref[ninth : ninth + 1, :] = both[:1]

    def received(copies):
        for copy in copies:
            copy.wait_recv()

    before_first, step = stepper(lines_ref, out_ref, flux_ref, part_ref, emf_ref, cell_ref, side_ref)

    def one(block, carry):
        @pl.when(block == 0)
        def _():
            arrived(1)
            pl.when(rad > 0)(lambda: received(to_outer))
            pl.when(rad == 0)(lambda: take_ghosts(range(8)))
            before_first()

        pl.when(block == 1)(lambda: arrived(2))

        @pl.when(block == 2)
        def _():
            arrived(3)
            pl.when(rad < 3)(lambda: received(to_inner))
            pl.when(rad == 3)(lambda: take_ghosts(range(8, GHOSTS)))

        step(block)
        return carry

    lax.fori_loop(0, ROWS // 8, one, 0)

    same_size(rows_ref, rows_sem, held_sem.at[0]).wait_send()
    for size, sent in ((WINDOW, piece == B_PIECE), (SHORT, piece != B_PIECE)):
        whole = same_size(moved_ref.at[:, :, :size], back_sem, held_sem.at[0])
        pl.when(sent)(whole.wait_send)

    @pl.when(rad == 3)
    def _():
        same_size(strips_ref.at[:8], strips_sem, held_sem.at[0]).wait_send()

    @pl.when(rad == 0)
    def _():
        same_size(strips_ref.at[8:GHOSTS], strips_sem, held_sem.at[0]).wait_send()

    @pl.when(has_ghost)
    def _():
        same_size(moved_strip_ref.at[:, :9], ghosts_back_sem, held_sem.at[0]).wait_send()

    @pl.when(rad < 3)
    def _():
        for copy in to_outer:
            copy.wait_send()

    @pl.when(rad > 0)
    def _():
        for copy in to_inner:
            copy.wait_send()


def side(cell, normal, face):
    density, momenta, magnetic, tracer, inverse = cell
    field = list(magnetic)
    field[normal] = face
    square = field[0] * field[0] + field[1] * field[1] + field[2] * field[2]
    speed = momenta[normal] * inverse
    flux = [momenta[normal]]
    for n in range(3):
        term = momenta[n] * speed - face * field[n]
        if n == normal:
            term = term + (density + 0.5 * square)
        flux.append(term)
    flux.append(tracer * speed)
    reach = 1.0 + square * inverse
    return flux, jnp.abs(speed) + reach * lax.rsqrt(reach)


def face_flux(before, cell, normal, face):
    left, left_signal = side(before, normal, face)
    right, right_signal = side(cell, normal, face)
    bound = jnp.maximum(left_signal, right_signal)
    left_state = [before[0], *before[1], before[3]]
    right_state = [cell[0], *cell[1], cell[3]]
    return [
        (left[n] + right[n]) - bound * (right_state[n] - left_state[n]) for n in range(5)
    ]


def stepper(cells_ref, out_ref, flux_ref, part_ref, emf_ref, cell_ref, side_ref):
    lane = lax.broadcasted_iota(jnp.int32, (8, TILE), 1)
    level = lane % NZ
    up = jnp.where(level == NZ - 1, lane - (NZ - 1), lane + 1)
    down = jnp.where(level == 0, lane + (NZ - 1), lane - 1)

    def load(field, row, tile):
        line = field % HELD * 8 + tile if tile < 8 else HELD * 8 + field % HELD
        first = (row + 8) * ROW_LINES + field // HELD * LINES + line
        return cells_ref[pl.ds(first, 8, stride=ROW_LINES), :]

    def plus_z(v):
        return jnp.take_along_axis(v, up, axis=1, mode="promise_in_bounds")

    def minus_z(v):
        return jnp.take_along_axis(v, down, axis=1, mode="promise_in_bounds")

    def minus_y(before, v):
        return pltpu.roll(jnp.where(lane >= TILE - NZ, before, v), NZ, 1)

    def plus_y(v, after):
        return pltpu.roll(jnp.where(lane < NZ, after, v), TILE - NZ, 1)

    def lines_of(row):
        return pl.ds(pl.multiple_of(row + 16, 8), 8)

    def part_lines(row):
        for piece in range(PIECES):
            if piece != B_PIECE:
                first = (row + 8) * ROW_LINES + piece * LINES + HELD * 8
                both = cells_ref[pl.ds(first, 8, stride=ROW_LINES), :]
                at = jnp.where(lane < NZ, lane + NZ, jnp.where(lane < TILE - NZ, lane, lane - NZ))
                second = jnp.take_along_axis(both, at, axis=1, mode="promise_in_bounds")
                cells_ref[pl.ds(first + 1, 8, stride=ROW_LINES), :] = second

    def work_out(row):
        part_lines(row + 1)
        for tile in range(9):
            density = load(0, row + 1, tile)
            faces = [load(n, row + 1, tile) for n in (4, 5, 6)]
            c = [
                0.5 * (faces[0] + load(4, row + 2, tile)),
                0.5 * (faces[1] + plus_y(faces[1], load(5, row + 1, (tile + 1) % 9))),
                0.5 * (faces[2] + plus_z(faces[2])),
            ]
            inverse = 1.0 / density
            v = [load(n, row + 1, tile) * inverse for n in (1, 2, 3)]
            emf = [v[2] * c[1] - v[1] * c[2], v[0] * c[2] - v[2] * c[0], v[1] * c[0] - v[0] * c[1]]
            for n, value in enumerate([*c, inverse, *emf]):
                cell_ref[tile, n, lines_of(row), :] = value

    def known(n, row, tile):
        return cell_ref[tile, n, pl.ds(row + 15, 8), :]

    def cell_at(row, tile):
        return (
            load(0, row, tile),
            [load(n, row, tile) for n in (1, 2, 3)],
            [known(n, row, tile) for n in (0, 1, 2)],
            load(7, row, tile),
            known(3, row, tile),
        )

    def outer_flux(row, tile, cell):
        flux = face_flux(cell, cell_at(row + 1, tile), 0, load(4, row + 1, tile))
        for n in range(5):
            side_ref[tile, n, lines_of(row), :] = flux[n]
        return flux

    def before_first():
        work_out(-8)
        for tile in range(8):
            outer_flux(-8, tile, cell_at(-8, tile))

    def first(row, tile):
        before = (tile + 8) % 9
        cell = cell_at(row, tile)
        density, momenta, centred, tracer, inverse = cell
        faces = [load(n, row, tile) for n in (4, 5, 6)]

        def behind_of(field):
            return minus_y(load(field, row, before), load(field, row, tile))

        behind_density = behind_of(0)
        behind = (
            behind_density,
            [behind_of(n) for n in (1, 2, 3)],
            [minus_y(known(0, row, before), centred[0]), None, minus_y(known(2, row, before), centred[2])],
            behind_of(7),
            1.0 / behind_density,
        )
        flux_y = face_flux(behind, cell, 1, faces[1])
        for n in range(5):
            flux_ref[tile, n] = flux_y[n]

        emf_x, z_here = known(4, row, tile), known(6, row, tile)
        z_lower, z_upper = known(6, row - 1, tile), known(6, row + 1, tile)
        x_below = minus_z(emf_x)
        emf_ref[tile, 0] = z_here + z_lower
        emf_ref[tile, 1] = (plus_z(emf_x) - x_below) - (z_upper - z_lower)
        emf_ref[tile, 2] = emf_x + x_below
        if tile == 8:
            return
        y_here, y_lower, y_upper = known(5, row, tile), known(5, row - 1, tile), known(5, row + 1, tile)
        y_pair, y_across = y_here + y_lower, y_upper - y_lower
        part_ref[tile, 5] = faces[0] + 0.25 * TIME_STEP * (plus_z(y_pair) - minus_z(y_pair))
        part_ref[tile, 6] = faces[1]
        part_ref[tile, 7] = faces[2] - 0.25 * TIME_STEP * (y_across + minus_z(y_across))

        flux_high = outer_flux(row, tile, cell)
        flux_low = [side_ref[tile, n, pl.ds(row + 15, 8), :] for n in range(5)]
        below = (
            minus_z(density),
            [minus_z(m) for m in momenta],
            [minus_z(centred[0]), minus_z(centred[1]), None],
            minus_z(tracer),
            minus_z(inverse),
        )
        flux_z = face_flux(below, cell, 2, faces[2])
        state = [density, *momenta, tracer]
        for n in range(5):
            change = (flux_high[n] - flux_low[n]) + (plus_z(flux_z[n]) - flux_z[n])
            value = state[n] - 0.5 * TIME_STEP * change
            if n == 1:
                value = value + TIME_STEP * 2.0 * momenta[1]
            if n == 2:
                value = value - TIME_STEP * 0.5 * momenta[0]
            part_ref[tile, n] = value

    def last(row, tile):
        before, after = (tile + 8) % 9, tile + 1
        rows, columns = pl.ds(row, 8), pl.ds(tile * TILE, TILE)
        for n, field in enumerate((0, 1, 2, 3, 7)):
            flux = flux_ref[tile, n]
            out_ref[field, rows, columns] = part_ref[tile, n] - 0.5 * TIME_STEP * (
                plus_y(flux, flux_ref[after, n]) - flux
            )
        around = [(emf_ref[before, n], emf_ref[tile, n], emf_ref[after, n]) for n in range(3)]
        across_z = plus_y(around[0][1], around[0][2]) - minus_y(around[0][0], around[0][1])
        pair = around[1][1] + minus_y(around[1][0], around[1][1])
        across_x = plus_y(around[2][1], around[2][2]) - minus_y(around[2][0], around[2][1])
        out_ref[4, rows, columns] = part_ref[tile, 5] - 0.25 * TIME_STEP * across_z
        out_ref[5, rows, columns] = part_ref[tile, 6] - 0.25 * TIME_STEP * pair
        out_ref[6, rows, columns] = part_ref[tile, 7] + 0.25 * TIME_STEP * across_x

    def step(block):
        row = pl.multiple_of(block * 8, 8)
        work_out(row)
        first(row, 8)
        first(row, 0)
        for tile in range(1, 8):
            first(row, tile)
            last(row, tile - 1)
        last(row, 7)

    return before_first, step


def per_device(state, row_shift, row_frac, edge_shift, edge_frac):
    tiles = state.reshape(FIELDS, ROWS // 8, 8, COLUMNS // TILE, TILE).transpose(0, 1, 3, 2, 4)
    tiles = tiles.reshape(FIELDS * ROWS * 8, TILE)
    dma, smem = pltpu.SemaphoreType.DMA, pltpu.SMEM

    def vmem(*shape):
        return pltpu.VMEM(shape, jnp.float32)

    return pl.pallas_call(
        kernel,
        out_shape=jax.ShapeDtypeStruct((FIELDS, ROWS, COLUMNS), jnp.float32),
        in_specs=[pl.BlockSpec(memory_space=pltpu.HBM)] * 3 + [pl.BlockSpec(memory_space=pltpu.SMEM)] * 2,
        out_specs=pl.BlockSpec(memory_space=pltpu.VMEM),
        scratch_shapes=[
            vmem(*tiles.shape),
            smem(row_shift.shape, jnp.int32), smem(row_frac.shape, jnp.float32),
            vmem(PIECES, 8, PARTS, HELD, 8, TILE),
            vmem(GHOSTS, 8, TILE),
            *[vmem(HELD, TILES + PAD, TILE)] * PARTS,
            vmem(TILES + PAD, TILE),
            vmem(PARTS, RING, LINES, TILE),
            vmem(RING, 16, TILE),
            vmem(*SLOTS, ROW_LINES, TILE),
            vmem(GHOSTS * 16, TILE),
            vmem(9, 5, 8, TILE), vmem(9, 8, 8, TILE), vmem(9, 3, 8, TILE),
            vmem(9, 7, 48, TILE), vmem(8, 5, 48, TILE),
            dma((3,)), dma, dma, dma, dma, dma((PARTS,)), dma, dma((PARTS,)), dma, dma((9,)), dma((9,)),
        ],
        compiler_params=pltpu.CompilerParams(
            collective_id=0, has_side_effects=True, vmem_limit_bytes=VMEM_LIMIT
        ),
        name="step",
    )(
        *[pltpu.with_memory_space_constraint(a, pltpu.HBM) for a in (tiles, row_shift, row_frac)],
        edge_shift,
        edge_frac,
    )


def solution(mesh):
    return jax.shard_map(
        per_device,
        mesh=mesh,
        in_specs=(P(None, "rad", "az"), P(), P(), P(), P()),
        out_specs=P(None, "rad", "az"),
        check_vma=False,
    )
```

```python
import jax
import jax.numpy as jnp
from jax import lax
from jax.experimental import pallas as pl
from jax.experimental.pallas import tpu as pltpu
from jax.sharding import PartitionSpec as P

MESH = pl.DeviceIdType.MESH
NZ = 32
FIELDS = 8
HELD = 2
PIECES = 4
PARTS = 4
GROUPED = 4
ROWS = 32
COLUMNS = 1024
RING = 32
TILE = 128
TILES = RING * COLUMNS // TILE
PAD = 24
WINDOW = 18
SHORT = 17
LINES = 24
ROW_LINES = 100
SLOTS = (6, 8)
B_PIECE = 2
GHOSTS = 17
VMEM_LIMIT = 28 * 2**20
TIME_STEP = 0.2


def share(lane, v):
    at = jnp.where(lane < TILE // 2, lane - NZ, lane + NZ)
    middle = jnp.logical_and(lane >= NZ, lane < TILE - NZ)
    return jnp.take_along_axis(v, jnp.where(middle, at, lane), axis=1, mode="promise_in_bounds")


def place():
    az, rad = lax.axis_index("az"), lax.axis_index("rad")
    return az // 8, (az // 4) % 2, az % 4, rad // 2, rad % 2


def row_of(part, first):
    last = first == 7
    if part == 0:
        return jnp.where(last, 3, 0), first
    return part - jnp.where(last, 1, 0), first


def ghost_holder(n):
    i = 2 if n == 16 else n % 8 // 2 * 4 + n % 2
    group = 0 if n < 8 else 3
    low = (group % 2 + i // 4 + (i // 2) % 2) % 2
    return {"az": 2 * i + low, "rad": 2 if n < 8 else 1}


def ghost_source(n):
    if n < 8:
        return ROWS - 1, n
    if n < 16:
        return 0, n - 8
    return 1, 4


def kernel(
    state_hbm, shift_hbm, frac_hbm, edge_shift_ref, edge_frac_ref,
    out_ref,
    state_ref, shift_ref, frac_ref,
    rows_ref, strips_ref, held_0_ref, held_1_ref, held_2_ref, held_3_ref, strip_held_ref,
    moved_ref, moved_strip_ref, cells_ref, ghosts_ref,
    flux_ref, part_ref, emf_ref, cell_ref, side_ref,
    in_sem, rows_sem, strips_sem, back_sem, ghosts_back_sem, held_sem, strip_held_sem, row_sem, ghosts_sem,
    hand_sem, handed_sem,
):
    x, y_hi, z, y_lo, core = place()
    az, rad = lax.axis_index("az"), lax.axis_index("rad")
    parity = (x + y_hi + z) % 2
    group = (1 - y_lo) * 2 + parity
    index = core * 16 + az // 2
    piece, first_row = index // 8, index % 8
    held_refs = (held_0_ref, held_1_ref, held_2_ref, held_3_ref)
    among = index % 16
    for_inner = jnp.logical_and(jnp.logical_and(group == 0, core == 0), among % 4 < 2)
    for_outer = jnp.logical_and(
        jnp.logical_and(group == 3, core == 1), jnp.logical_or(among % 4 < 2, among == 2)
    )
    has_ghost = jnp.logical_or(for_inner, for_outer)
    ghost = jnp.where(among == 2, 16, among // 4 * 2 + among % 4 + jnp.where(for_outer, 8, 0))

    loads = [
        pltpu.make_async_copy(source, target, in_sem.at[n])
        for n, (source, target) in enumerate(
            ((state_hbm, state_ref), (shift_hbm, shift_ref), (frac_hbm, frac_ref))
        )
    ]
    for load in loads:
        load.start()

    barrier = pltpu.get_barrier_semaphore()

    def greet(target_az, target_rad):
        pl.semaphore_signal(
            barrier, inc=1, device_id={"az": target_az, "rad": target_rad}, device_id_type=MESH
        )

    for d in range(RING):
        greet(d, group)

    @pl.when(rad > 0)
    def _():
        greet(az, rad - 1)

    @pl.when(rad < 3)
    def _():
        greet(az, rad + 1)

    @pl.when(has_ghost)
    def _():
        for d in range(RING):
            greet(d, 3 - group)

    for load in loads:
        load.wait()

    def field_lines(field, row):
        eighth, rest = row if isinstance(row, tuple) else (row // 8, row % 8)
        return state_ref[pl.ds(field * 256 + eighth * 64 + rest, 8, stride=8), :]

    pl.semaphore_wait(barrier, RING + jnp.where(rad == 0, 10, jnp.where(rad == 3, 9, 2)))

    my_lines = pl.ds(pl.multiple_of(az * 8, 8), 8)

    def send_strips(ghosts):
        for n in ghosts:
            r, field = ghost_source(n)
            strips_ref[n] = field_lines(field, r)
            pltpu.make_async_remote_copy(
                src_ref=strips_ref.at[n],
                dst_ref=strip_held_ref.at[my_lines],
                send_sem=strips_sem,
                recv_sem=strip_held_sem,
                device_id=ghost_holder(n),
                device_id_type=MESH,
            ).start()

    pl.when(rad == 3)(lambda: send_strips(range(8)))
    pl.when(rad == 0)(lambda: send_strips(range(8, GHOSTS)))
    offset_parity = (core + parity) % 2

    def send_out(part):
        def some(j, carry):
            sends = []
            for m in range(GROUPED):
                k = j * GROUPED + m
                side, i = k // 16, k % 16
                dx, dz = i % 4, (i // 4 + i) % 4
                dy = (offset_parity + dx + dz) % 2
                target = ((x + dx) % 4) * 8 + ((y_hi + dy) % 2) * 4 + (z + dz) % 4
                to_piece, first = side * 2 + target // 16, target // 2 % 8
                row = row_of(part, first)
                for f in range(HELD):
                    rows_ref[to_piece, first, part, f] = field_lines(to_piece * HELD + f, row)
                sends.append(
                    pltpu.make_async_remote_copy(
                        src_ref=rows_ref.at[to_piece, first, part],
                        dst_ref=held_refs[part].at[:, my_lines],
                        send_sem=rows_sem,
                        recv_sem=held_sem.at[part],
                        device_id={"az": target, "rad": (1 - y_lo) * 2 + side},
                        device_id_type=MESH,
                    )
                )
            for send in sends:
                send.start()
            return carry

        lax.fori_loop(0, RING // GROUPED, some, 0)

    for part in range(PARTS):
        send_out(part)

    def same_size(ref, send_sem, recv_sem):
        return pltpu.make_async_remote_copy(
            src_ref=ref, dst_ref=ref, send_sem=send_sem, recv_sem=recv_sem,
            device_id={"az": az, "rad": (rad + 2) % 4}, device_id_type=MESH,
        )

    lane = lax.broadcasted_iota(jnp.int32, (8, TILE), 1)

    def taps_of(cells, weights):
        taps = []
        for n, weight in enumerate(weights):
            part = ((cells + n) % 4) * NZ
            halo = (lane + part) % TILE < TILE - NZ
            taps.append((1 - (cells % 4 + n) // 4, part, lane < TILE - part, halo, weight))
        return cells // 4, taps

    def blend(taps, tile_lines, halo_lines, fields):
        inner, outer = [None] * fields, None
        for start, part, here, halo, weight in taps:
            for f in range(fields):
                both = jnp.where(here, tile_lines(f, start + 2), tile_lines(f, start + 1))
                term = weight * pltpu.roll(both, part, 1)
                inner[f] = term if inner[f] is None else inner[f] + term
            after = jnp.where(here, halo_lines(start + 10), halo_lines(start + 9))
            before = jnp.where(here, halo_lines(start + 1), halo_lines(start))
            term = weight * pltpu.roll(jnp.where(halo, after, before), part, 1)
            outer = term if outer is None else outer + term
        return inner, outer

    middle = jnp.logical_and(lane >= NZ, lane < TILE - NZ)
    lines_ref = cells_ref

    def lines_at(slot, n, size):
        return pl.ds(slot * ROW_LINES + n * LINES, size)

    odd = lax.broadcasted_iota(jnp.int32, (8, TILE), 0) % 2 == 1

    def ghost_taps():
        source_row = jnp.where(for_inner, ROWS * 4 - 1, ghost // 16)
        shift, fraction = shift_ref[source_row], frac_ref[source_row]
        edge_shift, edge_frac = edge_shift_ref[0], edge_frac_ref[0]
        more = jnp.where(for_inner, edge_shift, RING * COLUMNS // NZ - 1 - edge_shift)
        edge = jnp.where(for_inner, edge_frac, 1.0 - edge_frac)
        return taps_of(
            lax.rem(shift + more, RING * COLUMNS // NZ),
            (
                (1.0 - edge) * (1.0 - fraction),
                (1.0 - edge) * fraction + edge * (1.0 - fraction),
                edge * fraction,
            ),
        )

    def target(k):
        dx, dz, dy = k % 4, (k // 4 + k) % 4, (k // 16 + k) % 2
        return ((x + dx) % 4) * 8 + ((y_hi + dy) % 2) * 4 + (z + dz) % 4

    def first_tile(d, whole):
        return lax.rem(8 * d + 2 * TILES - 3 - whole, TILES)

    def send_back(part):
        held_ref = held_refs[part]
        same_size(held_ref.at[:, :TILES], rows_sem, held_sem.at[part]).wait_recv()
        for f in range(HELD):
            held_ref[f, TILES:] = held_ref[f, :PAD]
        eighth, rest = row_of(part, first_row)
        r = group * ROWS + eighth * 8 + rest
        shift, fraction = shift_ref[r], frac_ref[r]
        whole, taps = taps_of(shift, (1.0 - fraction, fraction))

        def fill(d):
            base = first_tile(d, whole)

            def halo_lines(n):
                pair = [
                    jnp.broadcast_to(held_ref[f, pl.ds(base + n, 1), :], (8, TILE))
                    for f in range(HELD)
                ]
                return jnp.where(odd, pair[1], pair[0])

            inner, outer = blend(
                taps, lambda f, n: held_ref[f, pl.ds(base + n, 8), :], halo_lines, HELD
            )
            for f in range(HELD):
                moved_ref[part, d, f * 8 : f * 8 + 8] = inner[f]
            second = share(lane, pltpu.roll(outer, 1, 0))
            shared = jnp.where(jnp.logical_and(middle, piece != B_PIECE), second, outer)
            moved_ref[part, d, HELD * 8 :] = shared

        def some(j, carry):
            ds = [target(j * GROUPED + m) for m in range(GROUPED)]
            for d in ds:
                fill(d)

            def send(size):
                for d in ds:
                    pltpu.make_async_remote_copy(
                        src_ref=moved_ref.at[part, d, :size],
                        dst_ref=lines_ref.at[lines_at((eighth + 1) * 8 + rest, piece, size)],
                        send_sem=back_sem,
                        recv_sem=row_sem.at[part],
                        device_id={"az": d, "rad": group},
                        device_id_type=MESH,
                    ).start()

            pl.when(piece == B_PIECE)(lambda: send(WINDOW))
            pl.when(piece != B_PIECE)(lambda: send(SHORT))
            return carry

        lax.fori_loop(0, RING // GROUPED, some, 0)

    def send_ghosts():
        same_size(strip_held_ref.at[:TILES], strips_sem, strip_held_sem).wait_recv()
        strip_held_ref[TILES:, :] = strip_held_ref[:PAD, :]
        whole, taps = ghost_taps()

        def fill(d):
            base = first_tile(d, whole)
            lines = lambda n: strip_held_ref[pl.ds(base + n, 8), :]
            inner, outer = blend(taps, lambda f, n: lines(n), lines, 1)
            moved_strip_ref[d, 0:8] = inner[0]
            moved_strip_ref[d, 8:16] = outer

        def some(j, carry):
            ds = [target(j * GROUPED + m) for m in range(GROUPED)]
            for d in ds:
                fill(d)
            for d in ds:
                pltpu.make_async_remote_copy(
                    src_ref=moved_strip_ref.at[d, :9],
                    dst_ref=ghosts_ref.at[pl.ds(pl.multiple_of(ghost * 16, 16), 9)],
                    send_sem=ghosts_back_sem,
                    recv_sem=ghosts_sem,
                    device_id={"az": d, "rad": group},
                    device_id_type=MESH,
                ).start()
            return carry

        lax.fori_loop(0, RING // GROUPED, some, 0)

    for part in range(PARTS):
        send_back(part)
        if part == 0:
            pl.when(has_ghost)(send_ghosts)

    def arrived(part):
        lines = 8 * (3 * SHORT + WINDOW)
        same_size(lines_ref.at[:lines], back_sem, row_sem.at[part]).wait_recv()

    def hand(source, slot, n, neighbour):
        return pltpu.make_async_remote_copy(
            src_ref=source,
            dst_ref=slot,
            send_sem=hand_sem.at[n],
            recv_sem=handed_sem.at[n],
            device_id={"az": az, "rad": neighbour},
            device_id_type=MESH,
        )

    outer, inner = (rad + 1) % 4, (rad + 3) % 4
    sizes = [WINDOW if n == B_PIECE else SHORT for n in range(PIECES)]

    def hand_row(source, slot, pieces, first, neighbour):
        return [
            hand(
                lines_ref.at[lines_at(source, n, sizes[n])],
                lines_ref.at[lines_at(slot, n, sizes[n])],
                first + n,
                neighbour,
            )
            for n in pieces
        ]

    to_outer = hand_row(39, 7, range(PIECES), 0, outer)
    to_inner = hand_row(8, 40, range(PIECES), PIECES, inner)
    to_inner += hand_row(9, 41, (B_PIECE,), 2 * PIECES - B_PIECE, inner)
    arrived(0)

    @pl.when(rad < 3)
    def _():
        for copy in to_outer:
            copy.start()

    @pl.when(rad > 0)
    def _():
        for copy in to_inner:
            copy.start()

    def take_ghosts(ghosts):
        same_size(ghosts_ref.at[: len(ghosts) * 9], ghosts_back_sem, ghosts_sem).wait_recv()
        for n in ghosts:
            row, field = (-1, n) if n < 8 else (ROWS, n - 8) if n < 16 else (ROWS + 1, 4)
            first = (row + 8) * ROW_LINES + field // HELD * LINES
            at, ninth = first + field % HELD * 8, first + HELD * 8 + field % HELD
            lines_ref[at : at + 8, :] = ghosts_ref[n * 16 : n * 16 + 8]
            line = ghosts_ref[n * 16 + 8 : n * 16 + 9]
            if field // HELD == B_PIECE:
                lines_ref[ninth : ninth + 1, :] = line
            elif field % HELD == 0:
                second = jnp.broadcast_to(ghosts_ref[n * 16 + 24 : n * 16 + 25], (8, TILE))
                both = jnp.where(middle, share(lane, second), jnp.broadcast_to(line, (8, TILE)))
                lines_ref[ninth : ninth + 1, :] = both[:1]

    def received(copies):
        for copy in copies:
            copy.wait_recv()

    before_first, step = stepper(lines_ref, out_ref, flux_ref, part_ref, emf_ref, cell_ref, side_ref)

    def one(block, carry):
        @pl.when(block == 0)
        def _():
            arrived(1)
            pl.when(rad > 0)(lambda: received(to_outer))
            pl.when(rad == 0)(lambda: take_ghosts(range(8)))
            before_first()

        pl.when(block == 1)(lambda: arrived(2))

        @pl.when(block == 2)
        def _():
            arrived(3)
            pl.when(rad < 3)(lambda: received(to_inner))
            pl.when(rad == 3)(lambda: take_ghosts(range(8, GHOSTS)))

        step(block)
        return carry

    lax.fori_loop(0, ROWS // 8, one, 0)

    same_size(rows_ref, rows_sem, held_sem.at[0]).wait_send()
    for size, sent in ((WINDOW, piece == B_PIECE), (SHORT, piece != B_PIECE)):
        whole = same_size(moved_ref.at[:, :, :size], back_sem, held_sem.at[0])
        pl.when(sent)(whole.wait_send)

    @pl.when(rad == 3)
    def _():
        same_size(strips_ref.at[:8], strips_sem, held_sem.at[0]).wait_send()

    @pl.when(rad == 0)
    def _():
        same_size(strips_ref.at[8:GHOSTS], strips_sem, held_sem.at[0]).wait_send()

    @pl.when(has_ghost)
    def _():
        same_size(moved_strip_ref.at[:, :9], ghosts_back_sem, held_sem.at[0]).wait_send()

    @pl.when(rad < 3)
    def _():
        for copy in to_outer:
            copy.wait_send()

    @pl.when(rad > 0)
    def _():
        for copy in to_inner:
            copy.wait_send()


def side(cell, normal, face):
    density, momenta, magnetic, tracer, inverse = cell
    field = list(magnetic)
    field[normal] = face
    square = field[0] * field[0] + field[1] * field[1] + field[2] * field[2]
    speed = momenta[normal] * inverse
    flux = [momenta[normal]]
    for n in range(3):
        term = momenta[n] * speed - face * field[n]
        if n == normal:
            term = term + (density + 0.5 * square)
        flux.append(term)
    flux.append(tracer * speed)
    reach = 1.0 + square * inverse
    return flux, jnp.abs(speed) + reach * lax.rsqrt(reach)


def face_flux(before, cell, normal, face):
    left, left_signal = side(before, normal, face)
    right, right_signal = side(cell, normal, face)
    bound = jnp.maximum(left_signal, right_signal)
    left_state = [before[0], *before[1], before[3]]
    right_state = [cell[0], *cell[1], cell[3]]
    return [
        (left[n] + right[n]) - bound * (right_state[n] - left_state[n]) for n in range(5)
    ]


def stepper(cells_ref, out_ref, flux_ref, part_ref, emf_ref, cell_ref, side_ref):
    lane = lax.broadcasted_iota(jnp.int32, (8, TILE), 1)
    level = lane % NZ
    up = jnp.where(level == NZ - 1, lane - (NZ - 1), lane + 1)
    down = jnp.where(level == 0, lane + (NZ - 1), lane - 1)

    def load(field, row, tile):
        line = field % HELD * 8 + tile if tile < 8 else HELD * 8 + field % HELD
        first = (row + 8) * ROW_LINES + field // HELD * LINES + line
        return cells_ref[pl.ds(first, 8, stride=ROW_LINES), :]

    def plus_z(v):
        return jnp.take_along_axis(v, up, axis=1, mode="promise_in_bounds")

    def minus_z(v):
        return jnp.take_along_axis(v, down, axis=1, mode="promise_in_bounds")

    def minus_y(before, v):
        return pltpu.roll(jnp.where(lane >= TILE - NZ, before, v), NZ, 1)

    def plus_y(v, after):
        return pltpu.roll(jnp.where(lane < NZ, after, v), TILE - NZ, 1)

    def lines_of(row):
        return pl.ds(pl.multiple_of(row + 16, 8), 8)

    def part_lines(row):
        for piece in range(PIECES):
            if piece != B_PIECE:
                first = (row + 8) * ROW_LINES + piece * LINES + HELD * 8
                both = cells_ref[pl.ds(first, 8, stride=ROW_LINES), :]
                at = jnp.where(lane < NZ, lane + NZ, jnp.where(lane < TILE - NZ, lane, lane - NZ))
                second = jnp.take_along_axis(both, at, axis=1, mode="promise_in_bounds")
                cells_ref[pl.ds(first + 1, 8, stride=ROW_LINES), :] = second

    def work_out(row):
        part_lines(row + 1)
        for tile in range(9):
            density = load(0, row + 1, tile)
            faces = [load(n, row + 1, tile) for n in (4, 5, 6)]
            c = [
                0.5 * (faces[0] + load(4, row + 2, tile)),
                0.5 * (faces[1] + plus_y(faces[1], load(5, row + 1, (tile + 1) % 9))),
                0.5 * (faces[2] + plus_z(faces[2])),
            ]
            inverse = 1.0 / density
            v = [load(n, row + 1, tile) * inverse for n in (1, 2, 3)]
            emf = [v[2] * c[1] - v[1] * c[2], v[0] * c[2] - v[2] * c[0], v[1] * c[0] - v[0] * c[1]]
            for n, value in enumerate([*c, inverse, *emf]):
                cell_ref[tile, n, lines_of(row), :] = value

    def known(n, row, tile):
        return cell_ref[tile, n, pl.ds(row + 15, 8), :]

    def cell_at(row, tile):
        return (
            load(0, row, tile),
            [load(n, row, tile) for n in (1, 2, 3)],
            [known(n, row, tile) for n in (0, 1, 2)],
            load(7, row, tile),
            known(3, row, tile),
        )

    def outer_flux(row, tile, cell):
        flux = face_flux(cell, cell_at(row + 1, tile), 0, load(4, row + 1, tile))
        for n in range(5):
            side_ref[tile, n, lines_of(row), :] = flux[n]
        return flux

    def before_first():
        work_out(-8)
        for tile in range(8):
            outer_flux(-8, tile, cell_at(-8, tile))

    def first(row, tile):
        before = (tile + 8) % 9
        cell = cell_at(row, tile)
        density, momenta, centred, tracer, inverse = cell
        faces = [load(n, row, tile) for n in (4, 5, 6)]

        def behind_of(field):
            return minus_y(load(field, row, before), load(field, row, tile))

        behind_density = behind_of(0)
        behind = (
            behind_density,
            [behind_of(n) for n in (1, 2, 3)],
            [minus_y(known(0, row, before), centred[0]), None, minus_y(known(2, row, before), centred[2])],
            behind_of(7),
            1.0 / behind_density,
        )
        flux_y = face_flux(behind, cell, 1, faces[1])
        for n in range(5):
            flux_ref[tile, n] = flux_y[n]

        emf_x, z_here = known(4, row, tile), known(6, row, tile)
        z_lower, z_upper = known(6, row - 1, tile), known(6, row + 1, tile)
        x_below = minus_z(emf_x)
        emf_ref[tile, 0] = z_here + z_lower
        emf_ref[tile, 1] = (plus_z(emf_x) - x_below) - (z_upper - z_lower)
        emf_ref[tile, 2] = emf_x + x_below
        if tile == 8:
            return
        y_here, y_lower, y_upper = known(5, row, tile), known(5, row - 1, tile), known(5, row + 1, tile)
        y_pair, y_across = y_here + y_lower, y_upper - y_lower
        part_ref[tile, 5] = faces[0] + 0.25 * TIME_STEP * (plus_z(y_pair) - minus_z(y_pair))
        part_ref[tile, 6] = faces[1]
        part_ref[tile, 7] = faces[2] - 0.25 * TIME_STEP * (y_across + minus_z(y_across))

        flux_high = outer_flux(row, tile, cell)
        flux_low = [side_ref[tile, n, pl.ds(row + 15, 8), :] for n in range(5)]
        below = (
            minus_z(density),
            [minus_z(m) for m in momenta],
            [minus_z(centred[0]), minus_z(centred[1]), None],
            minus_z(tracer),
            minus_z(inverse),
        )
        flux_z = face_flux(below, cell, 2, faces[2])
        state = [density, *momenta, tracer]
        for n in range(5):
            change = (flux_high[n] - flux_low[n]) + (plus_z(flux_z[n]) - flux_z[n])
            value = state[n] - 0.5 * TIME_STEP * change
            if n == 1:
                value = value + TIME_STEP * 2.0 * momenta[1]
            if n == 2:
                value = value - TIME_STEP * 0.5 * momenta[0]
            part_ref[tile, n] = value

    def last(row, tile):
        before, after = (tile + 8) % 9, tile + 1
        rows, columns = pl.ds(row, 8), pl.ds(tile * TILE, TILE)
        for n, field in enumerate((0, 1, 2, 3, 7)):
            flux = flux_ref[tile, n]
            out_ref[field, rows, columns] = part_ref[tile, n] - 0.5 * TIME_STEP * (
                plus_y(flux, flux_ref[after, n]) - flux
            )
        around = [(emf_ref[before, n], emf_ref[tile, n], emf_ref[after, n]) for n in range(3)]
        across_z = plus_y(around[0][1], around[0][2]) - minus_y(around[0][0], around[0][1])
        pair = around[1][1] + minus_y(around[1][0], around[1][1])
        across_x = plus_y(around[2][1], around[2][2]) - minus_y(around[2][0], around[2][1])
        out_ref[4, rows, columns] = part_ref[tile, 5] - 0.25 * TIME_STEP * across_z
        out_ref[5, rows, columns] = part_ref[tile, 6] - 0.25 * TIME_STEP * pair
        out_ref[6, rows, columns] = part_ref[tile, 7] + 0.25 * TIME_STEP * across_x

    def step(block):
        row = pl.multiple_of(block * 8, 8)
        work_out(row)
        first(row, 8)
        first(row, 0)
        for tile in range(1, 8):
            first(row, tile)
            last(row, tile - 1)
        last(row, 7)

    return before_first, step


def per_device(state, row_shift, row_frac, edge_shift, edge_frac):
    tiles = state.reshape(FIELDS, ROWS // 8, 8, COLUMNS // TILE, TILE).transpose(0, 1, 3, 2, 4)
    tiles = tiles.reshape(FIELDS * ROWS * 8, TILE)
    dma, smem = pltpu.SemaphoreType.DMA, pltpu.SMEM

    def vmem(*shape):
        return pltpu.VMEM(shape, jnp.float32)

    return pl.pallas_call(
        kernel,
        out_shape=jax.ShapeDtypeStruct((FIELDS, ROWS, COLUMNS), jnp.float32),
        in_specs=[pl.BlockSpec(memory_space=pltpu.HBM)] * 3 + [pl.BlockSpec(memory_space=pltpu.SMEM)] * 2,
        out_specs=pl.BlockSpec(memory_space=pltpu.VMEM),
        scratch_shapes=[
            vmem(*tiles.shape),
            smem(row_shift.shape, jnp.int32), smem(row_frac.shape, jnp.float32),
            vmem(PIECES, 8, PARTS, HELD, 8, TILE),
            vmem(GHOSTS, 8, TILE),
            *[vmem(HELD, TILES + PAD, TILE)] * PARTS,
            vmem(TILES + PAD, TILE),
            vmem(PARTS, RING, LINES, TILE),
            vmem(RING, 16, TILE),
            vmem(SLOTS[0] * SLOTS[1] * ROW_LINES, TILE),
            vmem(GHOSTS * 16, TILE),
            vmem(9, 5, 8, TILE), vmem(9, 8, 8, TILE), vmem(9, 3, 8, TILE),
            vmem(9, 7, 48, TILE), vmem(8, 5, 48, TILE),
            dma((3,)), dma, dma, dma, dma, dma((PARTS,)), dma, dma((PARTS,)), dma, dma((9,)), dma((9,)),
        ],
        compiler_params=pltpu.CompilerParams(
            collective_id=0, has_side_effects=True, vmem_limit_bytes=VMEM_LIMIT
        ),
        name="step",
    )(
        *[pltpu.with_memory_space_constraint(a, pltpu.HBM) for a in (tiles, row_shift, row_frac)],
        edge_shift,
        edge_frac,
    )


def solution(mesh):
    return jax.shard_map(
        per_device,
        mesh=mesh,
        in_specs=(P(None, "rad", "az"), P(), P(), P(), P()),
        out_specs=P(None, "rad", "az"),
        check_vma=False,
    )
```

```python
import jax
import jax.numpy as jnp
from jax import lax
from jax.experimental import pallas as pl
from jax.experimental.pallas import tpu as pltpu
from jax.sharding import PartitionSpec as P

MESH = pl.DeviceIdType.MESH
NZ = 32
FIELDS = 8
HELD = 2
PIECES = 4
PARTS = 4
GROUPED = 4
ROWS = 32
COLUMNS = 1024
RING = 32
TILE = 128
TILES = RING * COLUMNS // TILE
PAD = 24
WINDOW = 18
SHORT = 17
LINES = 24
ROW_LINES = 100
SLOTS = (6, 8)
B_PIECE = 2
GHOSTS = 17
VMEM_LIMIT = 28 * 2**20
TIME_STEP = 0.2


def share(lane, v):
    at = jnp.where(lane < TILE // 2, lane - NZ, lane + NZ)
    middle = jnp.logical_and(lane >= NZ, lane < TILE - NZ)
    return jnp.take_along_axis(v, jnp.where(middle, at, lane), axis=1, mode="promise_in_bounds")


def place():
    az, rad = lax.axis_index("az"), lax.axis_index("rad")
    return az // 8, (az // 4) % 2, az % 4, rad // 2, rad % 2


def row_of(part, first):
    last = first == 7
    if part == 0:
        return jnp.where(last, 3, 0), first
    return part - jnp.where(last, 1, 0), first


def ghost_holder(n):
    i = 2 if n == 16 else n % 8 // 2 * 4 + n % 2
    group = 0 if n < 8 else 3
    low = (group % 2 + i // 4 + (i // 2) % 2) % 2
    return {"az": 2 * i + low, "rad": 2 if n < 8 else 1}


def ghost_source(n):
    if n < 8:
        return ROWS - 1, n
    if n < 16:
        return 0, n - 8
    return 1, 4


def kernel(
    state_hbm, shift_hbm, frac_hbm, edge_shift_ref, edge_frac_ref,
    out_ref,
    state_ref, shift_ref, frac_ref,
    rows_ref, strips_ref, held_0_ref, held_1_ref, held_2_ref, held_3_ref, strip_held_ref,
    moved_ref, moved_strip_ref, cells_ref, ghosts_ref,
    flux_ref, part_ref, emf_ref, cell_ref, side_ref,
    in_sem, rows_sem, strips_sem, back_sem, ghosts_back_sem, held_sem, strip_held_sem, row_sem, ghosts_sem,
    hand_sem, handed_sem,
):
    x, y_hi, z, y_lo, core = place()
    az, rad = lax.axis_index("az"), lax.axis_index("rad")
    parity = (x + y_hi + z) % 2
    group = (1 - y_lo) * 2 + parity
    index = core * 16 + az // 2
    piece, first_row = index // 8, index % 8
    held_refs = (held_0_ref, held_1_ref, held_2_ref, held_3_ref)
    among = index % 16
    for_inner = jnp.logical_and(jnp.logical_and(group == 0, core == 0), among % 4 < 2)
    for_outer = jnp.logical_and(
        jnp.logical_and(group == 3, core == 1), jnp.logical_or(among % 4 < 2, among == 2)
    )
    has_ghost = jnp.logical_or(for_inner, for_outer)
    ghost = jnp.where(among == 2, 16, among // 4 * 2 + among % 4 + jnp.where(for_outer, 8, 0))

    loads = [
        pltpu.make_async_copy(source, target, in_sem.at[n])
        for n, (source, target) in enumerate(
            ((state_hbm, state_ref), (shift_hbm, shift_ref), (frac_hbm, frac_ref))
        )
    ]
    for load in loads:
        load.start()

    barrier = pltpu.get_barrier_semaphore()

    def greet(target_az, target_rad):
        pl.semaphore_signal(
            barrier, inc=1, device_id={"az": target_az, "rad": target_rad}, device_id_type=MESH
        )

    for d in range(RING):
        greet(d, group)

    @pl.when(rad > 0)
    def _():
        greet(az, rad - 1)

    @pl.when(rad < 3)
    def _():
        greet(az, rad + 1)

    @pl.when(has_ghost)
    def _():
        for d in range(RING):
            greet(d, 3 - group)

    for load in loads:
        load.wait()

    def field_lines(field, row):
        eighth, rest = row if isinstance(row, tuple) else (row // 8, row % 8)
        return state_ref[pl.ds(field * 256 + eighth * 64 + rest, 8, stride=8), :]

    pl.semaphore_wait(barrier, RING + jnp.where(rad == 0, 10, jnp.where(rad == 3, 9, 2)))

    my_lines = pl.ds(pl.multiple_of(az * 8, 8), 8)

    def send_strips(ghosts):
        for n in ghosts:
            r, field = ghost_source(n)
            strips_ref[n] = field_lines(field, r)
            pltpu.make_async_remote_copy(
                src_ref=strips_ref.at[n],
                dst_ref=strip_held_ref.at[my_lines],
                send_sem=strips_sem,
                recv_sem=strip_held_sem,
                device_id=ghost_holder(n),
                device_id_type=MESH,
            ).start()

    pl.when(rad == 3)(lambda: send_strips(range(8)))
    pl.when(rad == 0)(lambda: send_strips(range(8, GHOSTS)))
    offset_parity = (core + parity) % 2

    def send_out(part):
        def some(j, carry):
            sends = []
            for m in range(GROUPED):
                k = j * GROUPED + m
                side, i = k // 16, k % 16
                dx, dz = i % 4, (i // 4 + i) % 4
                dy = (offset_parity + dx + dz) % 2
                target = ((x + dx) % 4) * 8 + ((y_hi + dy) % 2) * 4 + (z + dz) % 4
                to_piece, first = side * 2 + target // 16, target // 2 % 8
                row = row_of(part, first)
                for f in range(HELD):
                    rows_ref[to_piece, first, part, f] = field_lines(to_piece * HELD + f, row)
                sends.append(
                    pltpu.make_async_remote_copy(
                        src_ref=rows_ref.at[to_piece, first, part],
                        dst_ref=held_refs[part].at[:, my_lines],
                        send_sem=rows_sem,
                        recv_sem=held_sem.at[part],
                        device_id={"az": target, "rad": (1 - y_lo) * 2 + side},
                        device_id_type=MESH,
                    )
                )
            for send in sends:
                send.start()
            return carry

        lax.fori_loop(0, RING // GROUPED, some, 0)

    for part in range(PARTS):
        send_out(part)

    def same_size(ref, send_sem, recv_sem):
        return pltpu.make_async_remote_copy(
            src_ref=ref, dst_ref=ref, send_sem=send_sem, recv_sem=recv_sem,
            device_id={"az": az, "rad": (rad + 2) % 4}, device_id_type=MESH,
        )

    lane = lax.broadcasted_iota(jnp.int32, (8, TILE), 1)

    def taps_of(cells, weights):
        taps = []
        for n, weight in enumerate(weights):
            part = ((cells + n) % 4) * NZ
            halo = (lane + part) % TILE < TILE - NZ
            taps.append((1 - (cells % 4 + n) // 4, part, lane < TILE - part, halo, weight))
        return cells // 4, taps

    def blend(taps, tile_lines, halo_lines, fields):
        inner, outer = [None] * fields, None
        for start, part, here, halo, weight in taps:
            for f in range(fields):
                both = jnp.where(here, tile_lines(f, start + 2), tile_lines(f, start + 1))
                term = weight * pltpu.roll(both, part, 1)
                inner[f] = term if inner[f] is None else inner[f] + term
            after = jnp.where(here, halo_lines(start + 10), halo_lines(start + 9))
            before = jnp.where(here, halo_lines(start + 1), halo_lines(start))
            term = weight * pltpu.roll(jnp.where(halo, after, before), part, 1)
            outer = term if outer is None else outer + term
        return inner, outer

    middle = jnp.logical_and(lane >= NZ, lane < TILE - NZ)
    lines_ref = cells_ref

    def lines_at(slot, n, size):
        return pl.ds(slot * ROW_LINES + n * LINES, size)

    odd = lax.broadcasted_iota(jnp.int32, (8, TILE), 0) % 2 == 1

    def ghost_taps():
        source_row = jnp.where(for_inner, ROWS * 4 - 1, ghost // 16)
        shift, fraction = shift_ref[source_row], frac_ref[source_row]
        edge_shift, edge_frac = edge_shift_ref[0], edge_frac_ref[0]
        more = jnp.where(for_inner, edge_shift, RING * COLUMNS // NZ - 1 - edge_shift)
        edge = jnp.where(for_inner, edge_frac, 1.0 - edge_frac)
        return taps_of(
            lax.rem(shift + more, RING * COLUMNS // NZ),
            (
                (1.0 - edge) * (1.0 - fraction),
                (1.0 - edge) * fraction + edge * (1.0 - fraction),
                edge * fraction,
            ),
        )

    def target(k):
        dx, dz, dy = k % 4, (k // 4 + k) % 4, (k // 16 + k) % 2
        return ((x + dx) % 4) * 8 + ((y_hi + dy) % 2) * 4 + (z + dz) % 4

    def first_tile(d, whole):
        return lax.rem(8 * d + 2 * TILES - 3 - whole, TILES)

    def send_back(part):
        held_ref = held_refs[part]
        same_size(held_ref.at[:, :TILES], rows_sem, held_sem.at[part]).wait_recv()
        for f in range(HELD):
            held_ref[f, TILES:] = held_ref[f, :PAD]
        eighth, rest = row_of(part, first_row)
        r = group * ROWS + eighth * 8 + rest
        shift, fraction = shift_ref[r], frac_ref[r]
        whole, taps = taps_of(shift, (1.0 - fraction, fraction))

        def fill(d):
            base = first_tile(d, whole)

            def halo_lines(n):
                pair = [
                    jnp.broadcast_to(held_ref[f, pl.ds(base + n, 1), :], (8, TILE))
                    for f in range(HELD)
                ]
                return jnp.where(odd, pair[1], pair[0])

            inner, outer = blend(
                taps, lambda f, n: held_ref[f, pl.ds(base + n, 8), :], halo_lines, HELD
            )
            for f in range(HELD):
                moved_ref[part, d, f * 8 : f * 8 + 8] = inner[f]
            second = share(lane, pltpu.roll(outer, 1, 0))
            shared = jnp.where(jnp.logical_and(middle, piece != B_PIECE), second, outer)
            moved_ref[part, d, HELD * 8 :] = shared

        def some(j, carry):
            ds = [target(j * GROUPED + m) for m in range(GROUPED)]
            for d in ds:
                fill(d)

            def send(size):
                for d in ds:
                    pltpu.make_async_remote_copy(
                        src_ref=moved_ref.at[part, d, :size],
                        dst_ref=lines_ref.at[lines_at((eighth + 1) * 8 + rest, piece, size)],
                        send_sem=back_sem,
                        recv_sem=row_sem.at[part],
                        device_id={"az": d, "rad": group},
                        device_id_type=MESH,
                    ).start()

            pl.when(piece == B_PIECE)(lambda: send(WINDOW))
            pl.when(piece != B_PIECE)(lambda: send(SHORT))
            return carry

        lax.fori_loop(0, RING // GROUPED, some, 0)

    def send_ghosts():
        same_size(strip_held_ref.at[:TILES], strips_sem, strip_held_sem).wait_recv()
        strip_held_ref[TILES:, :] = strip_held_ref[:PAD, :]
        whole, taps = ghost_taps()

        def fill(d):
            base = first_tile(d, whole)
            lines = lambda n: strip_held_ref[pl.ds(base + n, 8), :]
            inner, outer = blend(taps, lambda f, n: lines(n), lines, 1)
            moved_strip_ref[d, 0:8] = inner[0]
            moved_strip_ref[d, 8:16] = outer

        def some(j, carry):
            ds = [target(j * GROUPED + m) for m in range(GROUPED)]
            for d in ds:
                fill(d)
            for d in ds:
                pltpu.make_async_remote_copy(
                    src_ref=moved_strip_ref.at[d, :9],
                    dst_ref=ghosts_ref.at[pl.ds(pl.multiple_of(ghost * 16, 16), 9)],
                    send_sem=ghosts_back_sem,
                    recv_sem=ghosts_sem,
                    device_id={"az": d, "rad": group},
                    device_id_type=MESH,
                ).start()
            return carry

        lax.fori_loop(0, RING // GROUPED, some, 0)

    for part in range(PARTS):
        send_back(part)
        if part == 0:
            pl.when(has_ghost)(send_ghosts)

    def arrived(part):
        lines = 8 * (3 * SHORT + WINDOW)
        same_size(lines_ref.at[:lines], back_sem, row_sem.at[part]).wait_recv()

    def hand(source, slot, n, neighbour):
        return pltpu.make_async_remote_copy(
            src_ref=source,
            dst_ref=slot,
            send_sem=hand_sem.at[n],
            recv_sem=handed_sem.at[n],
            device_id={"az": az, "rad": neighbour},
            device_id_type=MESH,
        )

    outer, inner = (rad + 1) % 4, (rad + 3) % 4
    sizes = [WINDOW if n == B_PIECE else SHORT for n in range(PIECES)]

    def hand_row(source, slot, pieces, first, neighbour):
        return [
            hand(
                lines_ref.at[lines_at(source, n, sizes[n])],
                lines_ref.at[lines_at(slot, n, sizes[n])],
                first + n,
                neighbour,
            )
            for n in pieces
        ]

    to_outer = hand_row(39, 7, range(PIECES), 0, outer)
    to_inner = hand_row(8, 40, range(PIECES), PIECES, inner)
    to_inner += hand_row(9, 41, (B_PIECE,), 2 * PIECES - B_PIECE, inner)
    arrived(0)

    @pl.when(rad < 3)
    def _():
        for copy in to_outer:
            copy.start()

    @pl.when(rad > 0)
    def _():
        for copy in to_inner:
            copy.start()

    def take_ghosts(ghosts):
        same_size(ghosts_ref.at[: len(ghosts) * 9], ghosts_back_sem, ghosts_sem).wait_recv()
        for n in ghosts:
            row, field = (-1, n) if n < 8 else (ROWS, n - 8) if n < 16 else (ROWS + 1, 4)
            first = (row + 8) * ROW_LINES + field // HELD * LINES
            at, ninth = first + field % HELD * 8, first + HELD * 8 + field % HELD
            lines_ref[at : at + 8, :] = ghosts_ref[n * 16 : n * 16 + 8]
            line = ghosts_ref[n * 16 + 8 : n * 16 + 9]
            if field // HELD == B_PIECE:
                lines_ref[ninth : ninth + 1, :] = line
            elif field % HELD == 0:
                second = jnp.broadcast_to(ghosts_ref[n * 16 + 24 : n * 16 + 25], (8, TILE))
                both = jnp.where(middle, share(lane, second), jnp.broadcast_to(line, (8, TILE)))
                lines_ref[ninth : ninth + 1, :] = both[:1]

    def received(copies):
        for copy in copies:
            copy.wait_recv()

    before_first, step = stepper(lines_ref, out_ref, flux_ref, part_ref, emf_ref, cell_ref, side_ref)

    def one(block, carry):
        @pl.when(block == 0)
        def _():
            arrived(1)
            pl.when(rad > 0)(lambda: received(to_outer))
            pl.when(rad == 0)(lambda: take_ghosts(range(8)))
            before_first()

        pl.when(block == 1)(lambda: arrived(2))

        @pl.when(block == 2)
        def _():
            arrived(3)
            pl.when(rad < 3)(lambda: received(to_inner))
            pl.when(rad == 3)(lambda: take_ghosts(range(8, GHOSTS)))

        step(block)
        return carry

    lax.fori_loop(0, ROWS // 8, one, 0)

    same_size(rows_ref, rows_sem, held_sem.at[0]).wait_send()
    for size, sent in ((WINDOW, piece == B_PIECE), (SHORT, piece != B_PIECE)):
        whole = same_size(moved_ref.at[:, :, :size], back_sem, held_sem.at[0])
        pl.when(sent)(whole.wait_send)

    @pl.when(rad == 3)
    def _():
        same_size(strips_ref.at[:8], strips_sem, held_sem.at[0]).wait_send()

    @pl.when(rad == 0)
    def _():
        same_size(strips_ref.at[8:GHOSTS], strips_sem, held_sem.at[0]).wait_send()

    @pl.when(has_ghost)
    def _():
        same_size(moved_strip_ref.at[:, :9], ghosts_back_sem, held_sem.at[0]).wait_send()

    @pl.when(rad < 3)
    def _():
        for copy in to_outer:
            copy.wait_send()

    @pl.when(rad > 0)
    def _():
        for copy in to_inner:
            copy.wait_send()


def side(cell, normal, face):
    density, momenta, magnetic, tracer, inverse = cell
    field = list(magnetic)
    field[normal] = face
    square = field[0] * field[0] + field[1] * field[1] + field[2] * field[2]
    speed = momenta[normal] * inverse
    flux = [momenta[normal]]
    for n in range(3):
        term = momenta[n] * speed - face * field[n]
        if n == normal:
            term = term + (density + 0.5 * square)
        flux.append(term)
    flux.append(tracer * speed)
    reach = 1.0 + square * inverse
    return flux, jnp.abs(speed) + reach * lax.rsqrt(reach)


def face_flux(before, cell, normal, face):
    left, left_signal = side(before, normal, face)
    right, right_signal = side(cell, normal, face)
    bound = jnp.maximum(left_signal, right_signal)
    left_state = [before[0], *before[1], before[3]]
    right_state = [cell[0], *cell[1], cell[3]]
    return [
        (left[n] + right[n]) - bound * (right_state[n] - left_state[n]) for n in range(5)
    ]


def stepper(cells_ref, out_ref, flux_ref, part_ref, emf_ref, cell_ref, side_ref):
    lane = lax.broadcasted_iota(jnp.int32, (8, TILE), 1)
    level = lane % NZ
    up = jnp.where(level == NZ - 1, lane - (NZ - 1), lane + 1)
    down = jnp.where(level == 0, lane + (NZ - 1), lane - 1)

    def load(field, row, tile):
        line = field % HELD * 8 + tile if tile < 8 else HELD * 8 + field % HELD
        first = (row + 8) * ROW_LINES + field // HELD * LINES + line
        return cells_ref[pl.ds(first, 8, stride=ROW_LINES), :]

    def plus_z(v):
        return jnp.take_along_axis(v, up, axis=1, mode="promise_in_bounds")

    def minus_z(v):
        return jnp.take_along_axis(v, down, axis=1, mode="promise_in_bounds")

    def minus_y(before, v):
        return pltpu.roll(jnp.where(lane >= TILE - NZ, before, v), NZ, 1)

    def plus_y(v, after):
        return pltpu.roll(jnp.where(lane < NZ, after, v), TILE - NZ, 1)

    def lines_of(row):
        return pl.ds(pl.multiple_of(row + 16, 8), 8)

    def part_lines(row):
        for piece in range(PIECES):
            if piece != B_PIECE:
                first = (row + 8) * ROW_LINES + piece * LINES + HELD * 8
                both = cells_ref[pl.ds(first, 8, stride=ROW_LINES), :]
                at = jnp.where(lane < NZ, lane + NZ, jnp.where(lane < TILE - NZ, lane, lane - NZ))
                second = jnp.take_along_axis(both, at, axis=1, mode="promise_in_bounds")
                cells_ref[pl.ds(first + 1, 8, stride=ROW_LINES), :] = second

    def work_out(row):
        part_lines(row + 1)
        for tile in range(9):
            density = load(0, row + 1, tile)
            faces = [load(n, row + 1, tile) for n in (4, 5, 6)]
            c = [
                0.5 * (faces[0] + load(4, row + 2, tile)),
                0.5 * (faces[1] + plus_y(faces[1], load(5, row + 1, (tile + 1) % 9))),
                0.5 * (faces[2] + plus_z(faces[2])),
            ]
            inverse = 1.0 / density
            v = [load(n, row + 1, tile) * inverse for n in (1, 2, 3)]
            emf = [v[2] * c[1] - v[1] * c[2], v[0] * c[2] - v[2] * c[0], v[1] * c[0] - v[0] * c[1]]
            for n, value in enumerate([*c, inverse, *emf]):
                cell_ref[tile, n, lines_of(row), :] = value

    def known(n, row, tile):
        return cell_ref[tile, n, pl.ds(row + 15, 8), :]

    def cell_at(row, tile):
        return (
            load(0, row, tile),
            [load(n, row, tile) for n in (1, 2, 3)],
            [known(n, row, tile) for n in (0, 1, 2)],
            load(7, row, tile),
            known(3, row, tile),
        )

    def outer_flux(row, tile, cell):
        flux = face_flux(cell, cell_at(row + 1, tile), 0, load(4, row + 1, tile))
        for n in range(5):
            side_ref[tile, n, lines_of(row), :] = flux[n]
        return flux

    def before_first():
        work_out(-8)
        for tile in range(8):
            outer_flux(-8, tile, cell_at(-8, tile))

    def first(row, tile):
        before = (tile + 8) % 9
        cell = cell_at(row, tile)
        density, momenta, centred, tracer, inverse = cell
        faces = [load(n, row, tile) for n in (4, 5, 6)]

        def behind_of(field):
            return minus_y(load(field, row, before), load(field, row, tile))

        behind_density = behind_of(0)
        behind = (
            behind_density,
            [behind_of(n) for n in (1, 2, 3)],
            [minus_y(known(0, row, before), centred[0]), None, minus_y(known(2, row, before), centred[2])],
            behind_of(7),
            1.0 / behind_density,
        )
        flux_y = face_flux(behind, cell, 1, faces[1])
        for n in range(5):
            flux_ref[tile, n] = flux_y[n]

        emf_x, z_here = known(4, row, tile), known(6, row, tile)
        z_lower, z_upper = known(6, row - 1, tile), known(6, row + 1, tile)
        x_below = minus_z(emf_x)
        emf_ref[tile, 0] = z_here + z_lower
        emf_ref[tile, 1] = (plus_z(emf_x) - x_below) - (z_upper - z_lower)
        emf_ref[tile, 2] = emf_x + x_below
        if tile == 8:
            return
        y_here, y_lower, y_upper = known(5, row, tile), known(5, row - 1, tile), known(5, row + 1, tile)
        y_pair, y_across = y_here + y_lower, y_upper - y_lower
        part_ref[tile, 5] = faces[0] + 0.25 * TIME_STEP * (plus_z(y_pair) - minus_z(y_pair))
        part_ref[tile, 6] = faces[1]
        part_ref[tile, 7] = faces[2] - 0.25 * TIME_STEP * (y_across + minus_z(y_across))

        flux_high = outer_flux(row, tile, cell)
        flux_low = [side_ref[tile, n, pl.ds(row + 15, 8), :] for n in range(5)]
        below_density = minus_z(density)
        below = (
            below_density,
            [minus_z(m) for m in momenta],
            [minus_z(centred[0]), minus_z(centred[1]), None],
            minus_z(tracer),
            1.0 / below_density,
        )
        flux_z = face_flux(below, cell, 2, faces[2])
        state = [density, *momenta, tracer]
        for n in range(5):
            change = (flux_high[n] - flux_low[n]) + (plus_z(flux_z[n]) - flux_z[n])
            value = state[n] - 0.5 * TIME_STEP * change
            if n == 1:
                value = value + TIME_STEP * 2.0 * momenta[1]
            if n == 2:
                value = value - TIME_STEP * 0.5 * momenta[0]
            part_ref[tile, n] = value

    def last(row, tile):
        before, after = (tile + 8) % 9, tile + 1
        rows, columns = pl.ds(row, 8), pl.ds(tile * TILE, TILE)
        for n, field in enumerate((0, 1, 2, 3, 7)):
            flux = flux_ref[tile, n]
            out_ref[field, rows, columns] = part_ref[tile, n] - 0.5 * TIME_STEP * (
                plus_y(flux, flux_ref[after, n]) - flux
            )
        around = [(emf_ref[before, n], emf_ref[tile, n], emf_ref[after, n]) for n in range(3)]
        across_z = plus_y(around[0][1], around[0][2]) - minus_y(around[0][0], around[0][1])
        pair = around[1][1] + minus_y(around[1][0], around[1][1])
        across_x = plus_y(around[2][1], around[2][2]) - minus_y(around[2][0], around[2][1])
        out_ref[4, rows, columns] = part_ref[tile, 5] - 0.25 * TIME_STEP * across_z
        out_ref[5, rows, columns] = part_ref[tile, 6] - 0.25 * TIME_STEP * pair
        out_ref[6, rows, columns] = part_ref[tile, 7] + 0.25 * TIME_STEP * across_x

    def step(block):
        row = pl.multiple_of(block * 8, 8)
        work_out(row)
        first(row, 8)
        first(row, 0)
        for tile in range(1, 8):
            first(row, tile)
            last(row, tile - 1)
        last(row, 7)

    return before_first, step


def per_device(state, row_shift, row_frac, edge_shift, edge_frac):
    tiles = state.reshape(FIELDS, ROWS // 8, 8, COLUMNS // TILE, TILE).transpose(0, 1, 3, 2, 4)
    tiles = tiles.reshape(FIELDS * ROWS * 8, TILE)
    dma, smem = pltpu.SemaphoreType.DMA, pltpu.SMEM

    def vmem(*shape):
        return pltpu.VMEM(shape, jnp.float32)

    return pl.pallas_call(
        kernel,
        out_shape=jax.ShapeDtypeStruct((FIELDS, ROWS, COLUMNS), jnp.float32),
        in_specs=[pl.BlockSpec(memory_space=pltpu.HBM)] * 3 + [pl.BlockSpec(memory_space=pltpu.SMEM)] * 2,
        out_specs=pl.BlockSpec(memory_space=pltpu.VMEM),
        scratch_shapes=[
            vmem(*tiles.shape),
            smem(row_shift.shape, jnp.int32), smem(row_frac.shape, jnp.float32),
            vmem(PIECES, 8, PARTS, HELD, 8, TILE),
            vmem(GHOSTS, 8, TILE),
            *[vmem(HELD, TILES + PAD, TILE)] * PARTS,
            vmem(TILES + PAD, TILE),
            vmem(PARTS, RING, LINES, TILE),
            vmem(RING, 16, TILE),
            vmem(SLOTS[0] * SLOTS[1] * ROW_LINES, TILE),
            vmem(GHOSTS * 16, TILE),
            vmem(9, 5, 8, TILE), vmem(9, 8, 8, TILE), vmem(9, 3, 8, TILE),
            vmem(9, 7, 48, TILE), vmem(8, 5, 48, TILE),
            dma((3,)), dma, dma, dma, dma, dma((PARTS,)), dma, dma((PARTS,)), dma, dma((9,)), dma((9,)),
        ],
        compiler_params=pltpu.CompilerParams(
            collective_id=0, has_side_effects=True, vmem_limit_bytes=VMEM_LIMIT
        ),
        name="step",
    )(
        *[pltpu.with_memory_space_constraint(a, pltpu.HBM) for a in (tiles, row_shift, row_frac)],
        edge_shift,
        edge_frac,
    )


def solution(mesh):
    return jax.shard_map(
        per_device,
        mesh=mesh,
        in_specs=(P(None, "rad", "az"), P(), P(), P(), P()),
        out_specs=P(None, "rad", "az"),
        check_vma=False,
    )
```

```python
import jax
import jax.numpy as jnp
from jax import lax
from jax.experimental import pallas as pl
from jax.experimental.pallas import tpu as pltpu
from jax.sharding import PartitionSpec as P

MESH = pl.DeviceIdType.MESH
NZ = 32
FIELDS = 8
HELD = 2
PIECES = 4
PARTS = 4
GROUPED = 4
ROWS = 32
COLUMNS = 1024
RING = 32
TILE = 128
TILES = RING * COLUMNS // TILE
PAD = 24
WINDOW = 18
SHORT = 17
LINES = 24
ROW_LINES = 100
SLOTS = (6, 8)
B_PIECE = 2
GHOSTS = 17
VMEM_LIMIT = 28 * 2**20
TIME_STEP = 0.2


def share(lane, v):
    at = jnp.where(lane < TILE // 2, lane - NZ, lane + NZ)
    middle = jnp.logical_and(lane >= NZ, lane < TILE - NZ)
    return jnp.take_along_axis(v, jnp.where(middle, at, lane), axis=1, mode="promise_in_bounds")


def place():
    az, rad = lax.axis_index("az"), lax.axis_index("rad")
    return az // 8, (az // 4) % 2, az % 4, rad // 2, rad % 2


def row_of(part, first):
    last = first == 7
    if part == 0:
        return jnp.where(last, 3, 0), first
    return part - jnp.where(last, 1, 0), first


def ghost_holder(n):
    i = 2 if n == 16 else n % 8 // 2 * 4 + n % 2
    group = 0 if n < 8 else 3
    low = (group % 2 + i // 4 + (i // 2) % 2) % 2
    return {"az": 2 * i + low, "rad": 2 if n < 8 else 1}


def ghost_source(n):
    if n < 8:
        return ROWS - 1, n
    if n < 16:
        return 0, n - 8
    return 1, 4


def kernel(
    state_hbm, shift_hbm, frac_hbm, edge_shift_ref, edge_frac_ref,
    out_ref,
    state_ref, shift_ref, frac_ref,
    rows_ref, strips_ref, held_0_ref, held_1_ref, held_2_ref, held_3_ref, strip_held_ref,
    moved_ref, moved_strip_ref, cells_ref, ghosts_ref,
    flux_ref, part_ref, emf_ref, cell_ref, side_ref,
    in_sem, rows_sem, strips_sem, back_sem, ghosts_back_sem, held_sem, strip_held_sem, row_sem, ghosts_sem,
    hand_sem, handed_sem,
):
    x, y_hi, z, y_lo, core = place()
    az, rad = lax.axis_index("az"), lax.axis_index("rad")
    parity = (x + y_hi + z) % 2
    group = (1 - y_lo) * 2 + parity
    index = core * 16 + az // 2
    piece, first_row = index // 8, index % 8
    held_refs = (held_0_ref, held_1_ref, held_2_ref, held_3_ref)
    among = index % 16
    for_inner = jnp.logical_and(jnp.logical_and(group == 0, core == 0), among % 4 < 2)
    for_outer = jnp.logical_and(
        jnp.logical_and(group == 3, core == 1), jnp.logical_or(among % 4 < 2, among == 2)
    )
    has_ghost = jnp.logical_or(for_inner, for_outer)
    ghost = jnp.where(among == 2, 16, among // 4 * 2 + among % 4 + jnp.where(for_outer, 8, 0))

    loads = [
        pltpu.make_async_copy(source, target, in_sem.at[n])
        for n, (source, target) in enumerate(
            ((state_hbm, state_ref), (shift_hbm, shift_ref), (frac_hbm, frac_ref))
        )
    ]
    for load in loads:
        load.start()

    barrier = pltpu.get_barrier_semaphore()

    def greet(target_az, target_rad):
        pl.semaphore_signal(
            barrier, inc=1, device_id={"az": target_az, "rad": target_rad}, device_id_type=MESH
        )

    for d in range(RING):
        greet(d, group)

    @pl.when(rad > 0)
    def _():
        greet(az, rad - 1)

    @pl.when(rad < 3)
    def _():
        greet(az, rad + 1)

    @pl.when(has_ghost)
    def _():
        for d in range(RING):
            greet(d, 3 - group)

    for load in loads:
        load.wait()

    def field_lines(field, row):
        eighth, rest = row if isinstance(row, tuple) else (row // 8, row % 8)
        return state_ref[pl.ds(field * 256 + eighth * 64 + rest, 8, stride=8), :]

    pl.semaphore_wait(barrier, RING + jnp.where(rad == 0, 10, jnp.where(rad == 3, 9, 2)))

    my_lines = pl.ds(pl.multiple_of(az * 8, 8), 8)

    def send_strips(ghosts):
        for n in ghosts:
            r, field = ghost_source(n)
            strips_ref[n] = field_lines(field, r)
            pltpu.make_async_remote_copy(
                src_ref=strips_ref.at[n],
                dst_ref=strip_held_ref.at[my_lines],
                send_sem=strips_sem,
                recv_sem=strip_held_sem,
                device_id=ghost_holder(n),
                device_id_type=MESH,
            ).start()

    pl.when(rad == 3)(lambda: send_strips(range(8)))
    pl.when(rad == 0)(lambda: send_strips(range(8, GHOSTS)))
    offset_parity = (core + parity) % 2

    def send_out(part):
        def some(j, carry):
            sends = []
            for m in range(GROUPED):
                k = j * GROUPED + m
                side, i = k // 16, k % 16
                dx, dz = i % 4, (i // 4 + i) % 4
                dy = (offset_parity + dx + dz) % 2
                target = ((x + dx) % 4) * 8 + ((y_hi + dy) % 2) * 4 + (z + dz) % 4
                to_piece, first = side * 2 + target // 16, target // 2 % 8
                row = row_of(part, first)
                for f in range(HELD):
                    rows_ref[to_piece, first, part, f] = field_lines(to_piece * HELD + f, row)
                sends.append(
                    pltpu.make_async_remote_copy(
                        src_ref=rows_ref.at[to_piece, first, part],
                        dst_ref=held_refs[part].at[:, my_lines],
                        send_sem=rows_sem,
                        recv_sem=held_sem.at[part],
                        device_id={"az": target, "rad": (1 - y_lo) * 2 + side},
                        device_id_type=MESH,
                    )
                )
            for send in sends:
                send.start()
            return carry

        lax.fori_loop(0, RING // GROUPED, some, 0)

    for part in range(PARTS):
        send_out(part)

    def same_size(ref, send_sem, recv_sem):
        return pltpu.make_async_remote_copy(
            src_ref=ref, dst_ref=ref, send_sem=send_sem, recv_sem=recv_sem,
            device_id={"az": az, "rad": (rad + 2) % 4}, device_id_type=MESH,
        )

    lane = lax.broadcasted_iota(jnp.int32, (8, TILE), 1)

    def taps_of(cells, weights):
        taps = []
        for n, weight in enumerate(weights):
            part = ((cells + n) % 4) * NZ
            halo = (lane + part) % TILE < TILE - NZ
            taps.append((1 - (cells % 4 + n) // 4, part, lane < TILE - part, halo, weight))
        return cells // 4, taps

    def blend(taps, tile_lines, halo_lines, fields):
        inner, outer = [None] * fields, None
        for start, part, here, halo, weight in taps:
            for f in range(fields):
                both = jnp.where(here, tile_lines(f, start + 2), tile_lines(f, start + 1))
                term = weight * pltpu.roll(both, part, 1)
                inner[f] = term if inner[f] is None else inner[f] + term
            after = jnp.where(here, halo_lines(start + 10), halo_lines(start + 9))
            before = jnp.where(here, halo_lines(start + 1), halo_lines(start))
            term = weight * pltpu.roll(jnp.where(halo, after, before), part, 1)
            outer = term if outer is None else outer + term
        return inner, outer

    middle = jnp.logical_and(lane >= NZ, lane < TILE - NZ)
    lines_ref = cells_ref

    def lines_at(slot, n, size):
        return pl.ds(slot * ROW_LINES + n * LINES, size)

    odd = lax.broadcasted_iota(jnp.int32, (8, TILE), 0) % 2 == 1

    def ghost_taps():
        source_row = jnp.where(for_inner, ROWS * 4 - 1, ghost // 16)
        shift, fraction = shift_ref[source_row], frac_ref[source_row]
        edge_shift, edge_frac = edge_shift_ref[0], edge_frac_ref[0]
        more = jnp.where(for_inner, edge_shift, RING * COLUMNS // NZ - 1 - edge_shift)
        edge = jnp.where(for_inner, edge_frac, 1.0 - edge_frac)
        return taps_of(
            lax.rem(shift + more, RING * COLUMNS // NZ),
            (
                (1.0 - edge) * (1.0 - fraction),
                (1.0 - edge) * fraction + edge * (1.0 - fraction),
                edge * fraction,
            ),
        )

    def target(k):
        dx, dz, dy = k % 4, (k // 4 + k) % 4, (k // 16 + k) % 2
        return ((x + dx) % 4) * 8 + ((y_hi + dy) % 2) * 4 + (z + dz) % 4

    def first_tile(d, whole):
        return lax.rem(8 * d + 2 * TILES - 3 - whole, TILES)

    def send_back(part):
        held_ref = held_refs[part]
        same_size(held_ref.at[:, :TILES], rows_sem, held_sem.at[part]).wait_recv()
        for f in range(HELD):
            held_ref[f, TILES:] = held_ref[f, :PAD]
        eighth, rest = row_of(part, first_row)
        r = group * ROWS + eighth * 8 + rest
        shift, fraction = shift_ref[r], frac_ref[r]
        whole, taps = taps_of(shift, (1.0 - fraction, fraction))

        def fill(d):
            base = first_tile(d, whole)

            def halo_lines(n):
                pair = [
                    jnp.broadcast_to(held_ref[f, pl.ds(base + n, 1), :], (8, TILE))
                    for f in range(HELD)
                ]
                return jnp.where(odd, pair[1], pair[0])

            inner, outer = blend(
                taps, lambda f, n: held_ref[f, pl.ds(base + n, 8), :], halo_lines, HELD
            )
            for f in range(HELD):
                moved_ref[part, d, f * 8 : f * 8 + 8] = inner[f]
            second = share(lane, pltpu.roll(outer, 1, 0))
            shared = jnp.where(jnp.logical_and(middle, piece != B_PIECE), second, outer)
            moved_ref[part, d, HELD * 8 :] = shared

        def some(j, carry):
            ds = [target(j * GROUPED + m) for m in range(GROUPED)]
            for d in ds:
                fill(d)

            def send(size):
                for d in ds:
                    pltpu.make_async_remote_copy(
                        src_ref=moved_ref.at[part, d, :size],
                        dst_ref=lines_ref.at[lines_at((eighth + 1) * 8 + rest, piece, size)],
                        send_sem=back_sem,
                        recv_sem=row_sem.at[part],
                        device_id={"az": d, "rad": group},
                        device_id_type=MESH,
                    ).start()

            pl.when(piece == B_PIECE)(lambda: send(WINDOW))
            pl.when(piece != B_PIECE)(lambda: send(SHORT))
            return carry

        lax.fori_loop(0, RING // GROUPED, some, 0)

    def send_ghosts():
        same_size(strip_held_ref.at[:TILES], strips_sem, strip_held_sem).wait_recv()
        strip_held_ref[TILES:, :] = strip_held_ref[:PAD, :]
        whole, taps = ghost_taps()

        def fill(d):
            base = first_tile(d, whole)
            lines = lambda n: strip_held_ref[pl.ds(base + n, 8), :]
            inner, outer = blend(taps, lambda f, n: lines(n), lines, 1)
            moved_strip_ref[d, 0:8] = inner[0]
            moved_strip_ref[d, 8:16] = outer

        def some(j, carry):
            ds = [target(j * GROUPED + m) for m in range(GROUPED)]
            for d in ds:
                fill(d)
            for d in ds:
                pltpu.make_async_remote_copy(
                    src_ref=moved_strip_ref.at[d, :9],
                    dst_ref=ghosts_ref.at[pl.ds(pl.multiple_of(ghost * 16, 16), 9)],
                    send_sem=ghosts_back_sem,
                    recv_sem=ghosts_sem,
                    device_id={"az": d, "rad": group},
                    device_id_type=MESH,
                ).start()
            return carry

        lax.fori_loop(0, RING // GROUPED, some, 0)

    for part in range(PARTS):
        send_back(part)
        if part == 0:
            pl.when(has_ghost)(send_ghosts)

    def arrived(part):
        lines = 8 * (3 * SHORT + WINDOW)
        same_size(lines_ref.at[:lines], back_sem, row_sem.at[part]).wait_recv()

    def hand(source, slot, n, neighbour):
        return pltpu.make_async_remote_copy(
            src_ref=source,
            dst_ref=slot,
            send_sem=hand_sem.at[n],
            recv_sem=handed_sem.at[n],
            device_id={"az": az, "rad": neighbour},
            device_id_type=MESH,
        )

    outer, inner = (rad + 1) % 4, (rad + 3) % 4
    sizes = [WINDOW if n == B_PIECE else SHORT for n in range(PIECES)]

    def hand_row(source, slot, pieces, first, neighbour):
        return [
            hand(
                lines_ref.at[lines_at(source, n, sizes[n])],
                lines_ref.at[lines_at(slot, n, sizes[n])],
                first + n,
                neighbour,
            )
            for n in pieces
        ]

    to_outer = hand_row(39, 7, range(PIECES), 0, outer)
    to_inner = hand_row(8, 40, range(PIECES), PIECES, inner)
    to_inner += hand_row(9, 41, (B_PIECE,), 2 * PIECES - B_PIECE, inner)
    arrived(0)

    @pl.when(rad < 3)
    def _():
        for copy in to_outer:
            copy.start()

    @pl.when(rad > 0)
    def _():
        for copy in to_inner:
            copy.start()

    def take_ghosts(ghosts):
        same_size(ghosts_ref.at[: len(ghosts) * 9], ghosts_back_sem, ghosts_sem).wait_recv()
        for n in ghosts:
            row, field = (-1, n) if n < 8 else (ROWS, n - 8) if n < 16 else (ROWS + 1, 4)
            first = (row + 8) * ROW_LINES + field // HELD * LINES
            at, ninth = first + field % HELD * 8, first + HELD * 8 + field % HELD
            lines_ref[at : at + 8, :] = ghosts_ref[n * 16 : n * 16 + 8]
            line = ghosts_ref[n * 16 + 8 : n * 16 + 9]
            if field // HELD == B_PIECE:
                lines_ref[ninth : ninth + 1, :] = line
            elif field % HELD == 0:
                second = jnp.broadcast_to(ghosts_ref[n * 16 + 24 : n * 16 + 25], (8, TILE))
                both = jnp.where(middle, share(lane, second), jnp.broadcast_to(line, (8, TILE)))
                lines_ref[ninth : ninth + 1, :] = both[:1]

    def received(copies):
        for copy in copies:
            copy.wait_recv()

    before_first, step = stepper(lines_ref, out_ref, flux_ref, part_ref, emf_ref, cell_ref, side_ref)

    def one(block, carry):
        @pl.when(block == 0)
        def _():
            pl.when(rad > 0)(lambda: received(to_outer))
            pl.when(rad == 0)(lambda: take_ghosts(range(8)))
            before_first()
            arrived(1)

        pl.when(block == 1)(lambda: arrived(2))

        @pl.when(block == 2)
        def _():
            arrived(3)
            pl.when(rad < 3)(lambda: received(to_inner))
            pl.when(rad == 3)(lambda: take_ghosts(range(8, GHOSTS)))

        step(block)
        return carry

    lax.fori_loop(0, ROWS // 8, one, 0)

    same_size(rows_ref, rows_sem, held_sem.at[0]).wait_send()
    for size, sent in ((WINDOW, piece == B_PIECE), (SHORT, piece != B_PIECE)):
        whole = same_size(moved_ref.at[:, :, :size], back_sem, held_sem.at[0])
        pl.when(sent)(whole.wait_send)

    @pl.when(rad == 3)
    def _():
        same_size(strips_ref.at[:8], strips_sem, held_sem.at[0]).wait_send()

    @pl.when(rad == 0)
    def _():
        same_size(strips_ref.at[8:GHOSTS], strips_sem, held_sem.at[0]).wait_send()

    @pl.when(has_ghost)
    def _():
        same_size(moved_strip_ref.at[:, :9], ghosts_back_sem, held_sem.at[0]).wait_send()

    @pl.when(rad < 3)
    def _():
        for copy in to_outer:
            copy.wait_send()

    @pl.when(rad > 0)
    def _():
        for copy in to_inner:
            copy.wait_send()


def side(cell, normal, face):
    density, momenta, magnetic, tracer, inverse = cell
    field = list(magnetic)
    field[normal] = face
    square = field[0] * field[0] + field[1] * field[1] + field[2] * field[2]
    speed = momenta[normal] * inverse
    flux = [momenta[normal]]
    for n in range(3):
        term = momenta[n] * speed - face * field[n]
        if n == normal:
            term = term + (density + 0.5 * square)
        flux.append(term)
    flux.append(tracer * speed)
    reach = 1.0 + square * inverse
    return flux, jnp.abs(speed) + reach * lax.rsqrt(reach)


def face_flux(before, cell, normal, face):
    left, left_signal = side(before, normal, face)
    right, right_signal = side(cell, normal, face)
    bound = jnp.maximum(left_signal, right_signal)
    left_state = [before[0], *before[1], before[3]]
    right_state = [cell[0], *cell[1], cell[3]]
    return [
        (left[n] + right[n]) - bound * (right_state[n] - left_state[n]) for n in range(5)
    ]


def stepper(cells_ref, out_ref, flux_ref, part_ref, emf_ref, cell_ref, side_ref):
    lane = lax.broadcasted_iota(jnp.int32, (8, TILE), 1)
    level = lane % NZ
    up = jnp.where(level == NZ - 1, lane - (NZ - 1), lane + 1)
    down = jnp.where(level == 0, lane + (NZ - 1), lane - 1)

    def load(field, row, tile):
        line = field % HELD * 8 + tile if tile < 8 else HELD * 8 + field % HELD
        first = (row + 8) * ROW_LINES + field // HELD * LINES + line
        return cells_ref[pl.ds(first, 8, stride=ROW_LINES), :]

    def plus_z(v):
        return jnp.take_along_axis(v, up, axis=1, mode="promise_in_bounds")

    def minus_z(v):
        return jnp.take_along_axis(v, down, axis=1, mode="promise_in_bounds")

    def minus_y(before, v):
        return pltpu.roll(jnp.where(lane >= TILE - NZ, before, v), NZ, 1)

    def plus_y(v, after):
        return pltpu.roll(jnp.where(lane < NZ, after, v), TILE - NZ, 1)

    def lines_of(row):
        return pl.ds(pl.multiple_of(row + 16, 8), 8)

    def part_lines(row):
        for piece in range(PIECES):
            if piece != B_PIECE:
                first = (row + 8) * ROW_LINES + piece * LINES + HELD * 8
                both = cells_ref[pl.ds(first, 8, stride=ROW_LINES), :]
                at = jnp.where(lane < NZ, lane + NZ, jnp.where(lane < TILE - NZ, lane, lane - NZ))
                second = jnp.take_along_axis(both, at, axis=1, mode="promise_in_bounds")
                cells_ref[pl.ds(first + 1, 8, stride=ROW_LINES), :] = second

    def work_out(row):
        part_lines(row + 1)
        for tile in range(9):
            density = load(0, row + 1, tile)
            faces = [load(n, row + 1, tile) for n in (4, 5, 6)]
            c = [
                0.5 * (faces[0] + load(4, row + 2, tile)),
                0.5 * (faces[1] + plus_y(faces[1], load(5, row + 1, (tile + 1) % 9))),
                0.5 * (faces[2] + plus_z(faces[2])),
            ]
            inverse = 1.0 / density
            v = [load(n, row + 1, tile) * inverse for n in (1, 2, 3)]
            emf = [v[2] * c[1] - v[1] * c[2], v[0] * c[2] - v[2] * c[0], v[1] * c[0] - v[0] * c[1]]
            for n, value in enumerate([*c, inverse, *emf]):
                cell_ref[tile, n, lines_of(row), :] = value

    def known(n, row, tile):
        return cell_ref[tile, n, pl.ds(row + 15, 8), :]

    def cell_at(row, tile):
        return (
            load(0, row, tile),
            [load(n, row, tile) for n in (1, 2, 3)],
            [known(n, row, tile) for n in (0, 1, 2)],
            load(7, row, tile),
            known(3, row, tile),
        )

    def outer_flux(row, tile, cell):
        flux = face_flux(cell, cell_at(row + 1, tile), 0, load(4, row + 1, tile))
        for n in range(5):
            side_ref[tile, n, lines_of(row), :] = flux[n]
        return flux

    def before_first():
        work_out(-8)
        for tile in range(8):
            outer_flux(-8, tile, cell_at(-8, tile))

    def first(row, tile):
        before = (tile + 8) % 9
        cell = cell_at(row, tile)
        density, momenta, centred, tracer, inverse = cell
        faces = [load(n, row, tile) for n in (4, 5, 6)]

        def behind_of(field):
            return minus_y(load(field, row, before), load(field, row, tile))

        behind_density = behind_of(0)
        behind = (
            behind_density,
            [behind_of(n) for n in (1, 2, 3)],
            [minus_y(known(0, row, before), centred[0]), None, minus_y(known(2, row, before), centred[2])],
            behind_of(7),
            1.0 / behind_density,
        )
        flux_y = face_flux(behind, cell, 1, faces[1])
        for n in range(5):
            flux_ref[tile, n] = flux_y[n]

        emf_x, z_here = known(4, row, tile), known(6, row, tile)
        z_lower, z_upper = known(6, row - 1, tile), known(6, row + 1, tile)
        x_below = minus_z(emf_x)
        emf_ref[tile, 0] = z_here + z_lower
        emf_ref[tile, 1] = (plus_z(emf_x) - x_below) - (z_upper - z_lower)
        emf_ref[tile, 2] = emf_x + x_below
        if tile == 8:
            return
        y_here, y_lower, y_upper = known(5, row, tile), known(5, row - 1, tile), known(5, row + 1, tile)
        y_pair, y_across = y_here + y_lower, y_upper - y_lower
        part_ref[tile, 5] = faces[0] + 0.25 * TIME_STEP * (plus_z(y_pair) - minus_z(y_pair))
        part_ref[tile, 6] = faces[1]
        part_ref[tile, 7] = faces[2] - 0.25 * TIME_STEP * (y_across + minus_z(y_across))

        flux_high = outer_flux(row, tile, cell)
        flux_low = [side_ref[tile, n, pl.ds(row + 15, 8), :] for n in range(5)]
        below = (
            minus_z(density),
            [minus_z(m) for m in momenta],
            [minus_z(centred[0]), minus_z(centred[1]), None],
            minus_z(tracer),
            minus_z(inverse),
        )
        flux_z = face_flux(below, cell, 2, faces[2])
        state = [density, *momenta, tracer]
        for n in range(5):
            change = (flux_high[n] - flux_low[n]) + (plus_z(flux_z[n]) - flux_z[n])
            value = state[n] - 0.5 * TIME_STEP * change
            if n == 1:
                value = value + TIME_STEP * 2.0 * momenta[1]
            if n == 2:
                value = value - TIME_STEP * 0.5 * momenta[0]
            part_ref[tile, n] = value

    def last(row, tile):
        before, after = (tile + 8) % 9, tile + 1
        rows, columns = pl.ds(row, 8), pl.ds(tile * TILE, TILE)
        for n, field in enumerate((0, 1, 2, 3, 7)):
            flux = flux_ref[tile, n]
            out_ref[field, rows, columns] = part_ref[tile, n] - 0.5 * TIME_STEP * (
                plus_y(flux, flux_ref[after, n]) - flux
            )
        around = [(emf_ref[before, n], emf_ref[tile, n], emf_ref[after, n]) for n in range(3)]
        across_z = plus_y(around[0][1], around[0][2]) - minus_y(around[0][0], around[0][1])
        pair = around[1][1] + minus_y(around[1][0], around[1][1])
        across_x = plus_y(around[2][1], around[2][2]) - minus_y(around[2][0], around[2][1])
        out_ref[4, rows, columns] = part_ref[tile, 5] - 0.25 * TIME_STEP * across_z
        out_ref[5, rows, columns] = part_ref[tile, 6] - 0.25 * TIME_STEP * pair
        out_ref[6, rows, columns] = part_ref[tile, 7] + 0.25 * TIME_STEP * across_x

    def step(block):
        row = pl.multiple_of(block * 8, 8)
        work_out(row)
        first(row, 8)
        first(row, 0)
        for tile in range(1, 8):
            first(row, tile)
            last(row, tile - 1)
        last(row, 7)

    return before_first, step


def per_device(state, row_shift, row_frac, edge_shift, edge_frac):
    tiles = state.reshape(FIELDS, ROWS // 8, 8, COLUMNS // TILE, TILE).transpose(0, 1, 3, 2, 4)
    tiles = tiles.reshape(FIELDS * ROWS * 8, TILE)
    dma, smem = pltpu.SemaphoreType.DMA, pltpu.SMEM

    def vmem(*shape):
        return pltpu.VMEM(shape, jnp.float32)

    return pl.pallas_call(
        kernel,
        out_shape=jax.ShapeDtypeStruct((FIELDS, ROWS, COLUMNS), jnp.float32),
        in_specs=[pl.BlockSpec(memory_space=pltpu.HBM)] * 3 + [pl.BlockSpec(memory_space=pltpu.SMEM)] * 2,
        out_specs=pl.BlockSpec(memory_space=pltpu.VMEM),
        scratch_shapes=[
            vmem(*tiles.shape),
            smem(row_shift.shape, jnp.int32), smem(row_frac.shape, jnp.float32),
            vmem(PIECES, 8, PARTS, HELD, 8, TILE),
            vmem(GHOSTS, 8, TILE),
            *[vmem(HELD, TILES + PAD, TILE)] * PARTS,
            vmem(TILES + PAD, TILE),
            vmem(PARTS, RING, LINES, TILE),
            vmem(RING, 16, TILE),
            vmem(SLOTS[0] * SLOTS[1] * ROW_LINES, TILE),
            vmem(GHOSTS * 16, TILE),
            vmem(9, 5, 8, TILE), vmem(9, 8, 8, TILE), vmem(9, 3, 8, TILE),
            vmem(9, 7, 48, TILE), vmem(8, 5, 48, TILE),
            dma((3,)), dma, dma, dma, dma, dma((PARTS,)), dma, dma((PARTS,)), dma, dma((9,)), dma((9,)),
        ],
        compiler_params=pltpu.CompilerParams(
            collective_id=0, has_side_effects=True, vmem_limit_bytes=VMEM_LIMIT
        ),
        name="step",
    )(
        *[pltpu.with_memory_space_constraint(a, pltpu.HBM) for a in (tiles, row_shift, row_frac)],
        edge_shift,
        edge_frac,
    )


def solution(mesh):
    return jax.shard_map(
        per_device,
        mesh=mesh,
        in_specs=(P(None, "rad", "az"), P(), P(), P(), P()),
        out_specs=P(None, "rad", "az"),
        check_vma=False,
    )
```
